32 devices in a mesh: ctx: 8 (over y, x, core), head: 4 (over z).
Axes of the slice: x: 2, y: 2, z: 4, core: 2. Of those that a mesh axis runs over, the one named last changes fastest.
Arguments:
- queries: bfloat16 [4096, 2048], P(('ctx', 'head')), may hold values from -16 to 16
- keys: bfloat16 [4096, 512], P(('ctx', 'head')), may hold values from -4 to 4
- values: bfloat16 [4096, 512], P(('ctx', 'head')), may hold values from -6 to 6
- d_out: bfloat16 [4096, 2048], P(('ctx', 'head')), may hold values from -6 to 6
- lengths: int32 [32], replicated, may hold values from 1 to 2048, 4096 in all
Outputs:
- attn_out: bfloat16 [4096, 2048], P(('ctx', 'head'))
- grad_queries: bfloat16 [4096, 2048], P(('ctx', 'head'))
- grad_keys: bfloat16 [4096, 512], P(('ctx', 'head'))
- grad_values: bfloat16 [4096, 512], P(('ctx', 'head'))
The draws below stay inside these ranges and needn't reach their ends.
Inputs may be any that keep to these rules, and one draw needn't show every extreme that they name: The 32 lengths sum to 4096; the longest is exactly 2048.
All inputs are finite; a program needn't handle non-finite values.
Results may differ from the reference program's by a relative error of at most 0.035.
Values may be sent and summed in bfloat16 or wider, within the bound.
No kernel may reach another device: no remote copies, remote signals or barrier semaphores. Data moves between devices by JAX's collectives and lax.ppermute only.
A program may use at most 128 MiB of HBM per device.

```python
import math
import jax
import jax.numpy as jnp
import numpy as np
from jax import lax

QH = 16
KVH = 4
HD = 128
DOCS = 32
SEQ = 4096
DOC_MOST = 2048


def key_field(key):
    return jnp.clip(jax.random.normal(jax.random.fold_in(key, 11), (SEQ, KVH * HD), jnp.float32), -4.0, 4.0)


def draw_keys(key, part):
    return key_field(key).astype(jnp.bfloat16)


def draw_queries(key, part):
    drawn = jnp.clip(jax.random.normal(jax.random.fold_in(key, 21), (SEQ, QH * HD), jnp.float32), -4.0, 4.0)
    return drawn.astype(jnp.bfloat16)


def shard_levels(rng, dims, pieces, least, top_value):
    def one(dim, parts):
        steps = jax.random.uniform(jax.random.fold_in(jax.random.fold_in(rng, 6), dim), (parts,), jnp.float32, least / len(pieces), top_value / len(pieces))
        return jnp.repeat(jnp.exp(steps), dims[dim] // parts).reshape((-1,) + (1,) * (len(dims) - dim - 1))

    factor_of = one(*pieces[0])
    for cut in pieces[1:]:
        factor_of = factor_of * one(*cut)
    return factor_of


def profile(amount, total, most, skew):
    weights = [(1 << 20) // math.isqrt(standing ** skew) + 1 for standing in range(2, amount + 1)]
    rest, counts = total - most - (amount - 1), [1] * (amount - 1)
    while rest > 0:
        candidates = [i for i in range(amount - 1) if counts[i] < most]
        whole, remaining = sum([weights[i] for i in candidates]), rest
        for i in candidates:
            addition = min(most - counts[i], max(1, remaining * weights[i] // whole), rest)
            counts[i] = counts[i] + addition
            rest = rest - addition
    return np.array([most] + counts)


def ragged_sizes(key, count, total, bound, skew):
    if count == 2:
        one = jax.random.randint(key, (), max(1, total - bound), min(bound, total - 1) + 1)
        return jnp.stack([one, total - one])
    sizes = jnp.asarray(profile(count, total, bound, skew), jnp.int32)
    pairs = (count - 1) // 2
    source_of, taker = sizes[1:1 + 2 * pairs:2], sizes[2:2 + 2 * pairs:2]
    margin = jnp.minimum(source_of - 1, bound - taker)
    passed = jax.random.randint(jax.random.fold_in(key, 1), (pairs,), 0, 1 << 20) % (margin + 1)
    sizes = sizes.at[1:1 + 2 * pairs:2].set(source_of - passed).at[2:2 + 2 * pairs:2].set(taker + passed)
    return sizes[jax.random.permutation(jax.random.fold_in(key, 2), count)]


def noise(stream_key, shape, width, most, pieces=(), kind=jnp.bfloat16):
    entries = width * jax.random.normal(stream_key, shape, jnp.float32)
    if pieces:
        entries = entries * shard_levels(stream_key, shape, pieces, -0.22, 0.18)
    return jnp.clip(entries, -most, most).astype(kind)


def setup_inputs(seed: int = 0) -> dict:
    arg_keys = jax.random.split(jax.random.key(seed), 6)
    return {
        "queries": draw_queries(jax.random.fold_in(arg_keys[5], 71), 0),
        "keys": draw_keys(jax.random.fold_in(arg_keys[5], 71), 0),
        "values": noise(arg_keys[2], (SEQ, KVH * HD), 1.0, 6.0, ((0, 32),)),
        "d_out": noise(arg_keys[3], (SEQ, QH * HD), 1.0, 6.0, ((0, 32),)),
        "lengths": ragged_sizes(arg_keys[4], DOCS, SEQ, DOC_MOST, 2).astype(jnp.int32),
    }


NEG_FILL = -1e30


def reference(queries, keys, values, d_out, lengths):
    total = queries.shape[0]
    group_size = QH // KVH
    scaling = HD ** -0.5
    block_rows = min(128, total)
    window = min(DOC_MOST + block_rows, total)
    doc_ends = jnp.cumsum(lengths)
    positions = jnp.arange(total, dtype=jnp.int32)
    starts = jnp.sum(jnp.where(doc_ends[None, :] <= positions[:, None], lengths[None, :], 0), axis=1).astype(jnp.int32)
    query_heads = queries.reshape(total, KVH, group_size, HD)
    key_heads = keys.reshape(total, KVH, HD)
    value_heads = values.reshape(total, KVH, HD)
    grad_heads = d_out.reshape(total, KVH, group_size, HD)

    def one_block(carried, block_index):
        key_acc, value_acc = carried
        first = block_index * block_rows
        window_first = jnp.clip(first + block_rows - window, 0, total - window).astype(jnp.int32)
        query_block = lax.dynamic_slice_in_dim(query_heads, first, block_rows, 0).astype(jnp.float32)
        grad_block = lax.dynamic_slice_in_dim(grad_heads, first, block_rows, 0).astype(jnp.float32)
        key_window = lax.dynamic_slice_in_dim(key_heads, window_first, window, 0).astype(jnp.float32)
        value_window = lax.dynamic_slice_in_dim(value_heads, window_first, window, 0).astype(jnp.float32)
        query_pos = first + jnp.arange(block_rows, dtype=jnp.int32)
        key_pos = window_first + jnp.arange(window, dtype=jnp.int32)
        start_rows = lax.dynamic_slice_in_dim(starts, first, block_rows, 0)
        mask = (key_pos[None, :] <= query_pos[:, None]) & (key_pos[None, :] >= start_rows[:, None])
        mask = mask[:, None, None, :]
        scores = jnp.einsum("qkgd,ckd->qkgc", query_block, key_window) * scaling
        masked = jnp.where(mask, scores, NEG_FILL)
        row_max = jnp.max(masked, axis=-1)
        row_total = jnp.sum(jnp.where(mask, jnp.exp(masked - row_max[..., None]), 0.0), axis=-1)
        lse_rows = row_max + jnp.log(row_total)
        prob_raw = jnp.where(mask, jnp.exp(scores - lse_rows[..., None]), 0.0)
        weights = lax.optimization_barrier(prob_raw.astype(jnp.bfloat16)).astype(jnp.float32)
        attn_block = jnp.einsum("qkgc,ckd->qkgd", weights, value_window).astype(jnp.bfloat16)
        delta_rows = jnp.sum(grad_block * attn_block.astype(jnp.float32), axis=-1)
        prob_grad = jnp.einsum("qkgd,ckd->qkgc", grad_block, value_window)
        score_grad = (prob_raw * (prob_grad - delta_rows[..., None]) * scaling).astype(jnp.bfloat16)
        score_grad = lax.optimization_barrier(score_grad).astype(jnp.float32)
        query_grad = jnp.einsum("qkgc,ckd->qkgd", score_grad, key_window).astype(jnp.bfloat16)
        key_part = jnp.einsum("qkgc,qkgd->ckd", score_grad, query_block)
        value_part = jnp.einsum("qkgc,qkgd->ckd", weights, grad_block)
        key_acc = lax.dynamic_update_slice_in_dim(key_acc, lax.dynamic_slice_in_dim(key_acc, window_first, window, 0) + key_part, window_first, 0)
        value_acc = lax.dynamic_update_slice_in_dim(value_acc, lax.dynamic_slice_in_dim(value_acc, window_first, window, 0) + value_part, window_first, 0)
        return (key_acc, value_acc), (attn_block, query_grad)

    empty = jnp.zeros((total, KVH, HD), jnp.float32)
    (key_acc, value_acc), (attn_blocks, query_grads) = lax.scan(one_block, (empty, empty), jnp.arange(total // block_rows, dtype=jnp.int32))
    attn_out = attn_blocks.reshape(total, QH * HD)
    grad_queries = query_grads.reshape(total, QH * HD)
    grad_keys = key_acc.reshape(total, KVH * HD).astype(jnp.bfloat16)
    grad_values = value_acc.reshape(total, KVH * HD).astype(jnp.bfloat16)
    return (attn_out, grad_queries, grad_keys, grad_values)
```

```python
import functools
import math

import jax
import jax.numpy as jnp
from jax import lax
from jax.experimental import pallas as pl
from jax.experimental.pallas import tpu as pltpu
from jax.sharding import PartitionSpec as P

QH = 16
KVH = 4
HD = 128
REACH = 4


NEG_FILL = -1e30


def shifted(value, axis, steps):
    count = lax.axis_size(axis)
    first, last = (max(0, -steps), min(count, count - steps))
    return lax.ppermute(value, axis, [(source, source + steps) for source in range(first, last)])


def doc_starts(lengths, first, count):
    doc_ends = jnp.cumsum(lengths)
    positions = first + jnp.arange(count, dtype=jnp.int32)
    passed = doc_ends[None, :] <= positions[:, None]
    return jnp.sum(jnp.where(passed, lengths[None, :], 0), axis=1)


def visible_pairs(query_first, key_first, start_rows, block_rows):
    query_pos = query_first + jnp.arange(block_rows, dtype=jnp.int32)
    key_pos = key_first + jnp.arange(block_rows, dtype=jnp.int32)
    mask = (key_pos[None, :] <= query_pos[:, None]) & (key_pos[None, :] >= start_rows[:, None])
    return mask[:, None, None, :]


def block_live(query_first, key_first, tile_starts, tile_first, block_rows):
    lowest = jnp.maximum(query_first, key_first)
    picked = jnp.clip(lowest - tile_first, 0, tile_starts.shape[0] - 1)
    first_start = lax.dynamic_index_in_dim(tile_starts, picked, 0, keepdims=False)
    return (lowest <= query_first + block_rows - 1) & (first_start <= key_first + block_rows - 1)


def shards(queries, keys, values, d_out, lengths):
    heads_dev = lax.axis_size("head")
    tok_dev = queries.shape[0]
    copies = max(1, heads_dev // KVH)
    kv_local = max(1, KVH // heads_dev)
    q_local = QH // heads_dev
    group_size = q_local // kv_local
    scaling = HD ** (-0.5)

    def spread(array_in):
        if copies > 1:
            return jnp.repeat(array_in.reshape(tok_dev, KVH, HD), copies, axis=1).reshape(
                tok_dev, KVH * copies * HD
            )
        return array_in

    q_tile, k_tile, v_tile = (
        lax.all_to_all(queries, "head", split_axis=1, concat_axis=0, tiled=True),
        lax.all_to_all(spread(keys), "head", split_axis=1, concat_axis=0, tiled=True),
        lax.all_to_all(spread(values), "head", split_axis=1, concat_axis=0, tiled=True),
    )
    tile_rows = q_tile.shape[0]
    block_rows = min(1024, tile_rows)
    block_count = tile_rows // block_rows
    ctx_index = lax.axis_index("ctx")
    tile_first = ctx_index * tile_rows
    tile_starts = doc_starts(lengths, tile_first, tile_rows)
    query_blocks = [
        q_tile[number * block_rows : (number + 1) * block_rows].reshape(
            block_rows, kv_local, group_size, HD
        )
        for number in range(block_count)
    ]
    start_blocks = [
        tile_starts[number * block_rows : (number + 1) * block_rows]
        for number in range(block_count)
    ]
    query_firsts = [tile_first + number * block_rows for number in range(block_count)]
    key_pair = jnp.stack([k_tile, v_tile])
    key_tiles = [key_pair]
    moving = key_pair
    for offset in range(1, REACH + 1):
        moving = shifted(moving, "ctx", 1)
        key_tiles.append(moving)

    def split_keys(tile_pair):
        key_list = [
            tile_pair[0, number * block_rows : (number + 1) * block_rows].reshape(
                block_rows, kv_local, HD
            )
            for number in range(block_count)
        ]
        value_list = [
            tile_pair[1, number * block_rows : (number + 1) * block_rows].reshape(
                block_rows, kv_local, HD
            )
            for number in range(block_count)
        ]
        return (key_list, value_list)

    states = [
        (
            jnp.full((block_rows, kv_local, group_size), NEG_FILL, jnp.float32),
            jnp.zeros((block_rows, kv_local, group_size), jnp.float32),
            jnp.zeros((block_rows, kv_local, group_size, HD), jnp.float32),
        )
        for number in range(block_count)
    ]
    for offset in range(REACH + 1):
        key_list, value_list = split_keys(key_tiles[offset])
        key_start = (ctx_index - offset) * tile_rows
        for query_number in range(block_count):
            query_block = query_blocks[query_number]
            query_first = query_firsts[query_number]
            start_rows = start_blocks[query_number]
            for key_number in range(block_count):
                key_block = key_list[key_number]
                value_block = value_list[key_number]
                key_first = key_start + key_number * block_rows

                def forward_block(
                    current,
                    query_block=query_block,
                    query_first=query_first,
                    start_rows=start_rows,
                    key_block=key_block,
                    value_block=value_block,
                    key_first=key_first,
                ):
                    max_old, sum_old, acc_old = current
                    mask = visible_pairs(query_first, key_first, start_rows, block_rows)
                    scores = (
                        jnp.einsum(
                            "qkgd,ckd->qkgc",
                            query_block,
                            key_block,
                            preferred_element_type=jnp.float32,
                        )
                        * scaling
                    )
                    scores = jnp.where(mask, scores, NEG_FILL)
                    max_new = jnp.maximum(max_old, jnp.max(scores, axis=-1))
                    prob_raw = jnp.where(mask, jnp.exp(scores - max_new[..., None]), 0.0)
                    rescale = jnp.exp(max_old - max_new)
                    sum_new = sum_old * rescale + jnp.sum(prob_raw, axis=-1)
                    acc_new = acc_old * rescale[..., None] + jnp.einsum(
                        "qkgc,ckd->qkgd",
                        prob_raw.astype(jnp.bfloat16),
                        value_block,
                        preferred_element_type=jnp.float32,
                    )
                    return (max_new, sum_new, acc_new)

                live = block_live(query_first, key_first, tile_starts, tile_first, block_rows)
                states[query_number] = lax.cond(
                    live, forward_block, lambda unchanged: unchanged, states[query_number]
                )
    out_blocks = [(state[2] / state[1][..., None]).astype(jnp.bfloat16) for state in states]
    lse_blocks = [state[0] + jnp.log(state[1]) for state in states]
    grad_tile = lax.all_to_all(d_out, "head", split_axis=1, concat_axis=0, tiled=True)
    grad_blocks = [
        grad_tile[number * block_rows : (number + 1) * block_rows].reshape(
            block_rows, kv_local, group_size, HD
        )
        for number in range(block_count)
    ]
    delta_blocks = [
        jnp.sum(
            grad_blocks[number].astype(jnp.float32) * out_blocks[number].astype(jnp.float32),
            axis=-1,
        )
        for number in range(block_count)
    ]
    query_totals = [
        jnp.zeros((block_rows, kv_local, group_size, HD), jnp.float32)
        for number in range(block_count)
    ]
    partial_grads = []
    for offset in range(REACH + 1):
        key_list, value_list = split_keys(key_tiles[offset])
        key_start = (ctx_index - offset) * tile_rows
        key_sums = [
            jnp.zeros((block_rows, kv_local, HD), jnp.float32) for number in range(block_count)
        ]
        value_sums = [
            jnp.zeros((block_rows, kv_local, HD), jnp.float32) for number in range(block_count)
        ]
        for query_number in range(block_count):
            query_block = query_blocks[query_number]
            grad_block = grad_blocks[query_number]
            query_first = query_firsts[query_number]
            start_rows = start_blocks[query_number]
            lse_rows = lse_blocks[query_number]
            delta_rows = delta_blocks[query_number]
            for key_number in range(block_count):
                key_block = key_list[key_number]
                value_block = value_list[key_number]
                key_first = key_start + key_number * block_rows

                def backward_block(
                    current,
                    query_block=query_block,
                    grad_block=grad_block,
                    query_first=query_first,
                    start_rows=start_rows,
                    lse_rows=lse_rows,
                    delta_rows=delta_rows,
                    key_block=key_block,
                    value_block=value_block,
                    key_first=key_first,
                ):
                    query_grad, key_grad, value_grad = current
                    mask = visible_pairs(query_first, key_first, start_rows, block_rows)
                    scores = (
                        jnp.einsum(
                            "qkgd,ckd->qkgc",
                            query_block,
                            key_block,
                            preferred_element_type=jnp.float32,
                        )
                        * scaling
                    )
                    prob_raw = jnp.where(mask, jnp.exp(scores - lse_rows[..., None]), 0.0)
                    weights = prob_raw.astype(jnp.bfloat16)
                    value_grad = value_grad + jnp.einsum(
                        "qkgc,qkgd->ckd", weights, grad_block, preferred_element_type=jnp.float32
                    )
                    prob_grad = jnp.einsum(
                        "qkgd,ckd->qkgc",
                        grad_block,
                        value_block,
                        preferred_element_type=jnp.float32,
                    )
                    score_grad = (prob_raw * (prob_grad - delta_rows[..., None]) * scaling).astype(
                        jnp.bfloat16
                    )
                    query_grad = query_grad + jnp.einsum(
                        "qkgc,ckd->qkgd", score_grad, key_block, preferred_element_type=jnp.float32
                    )
                    key_grad = key_grad + jnp.einsum(
                        "qkgc,qkgd->ckd",
                        score_grad,
                        query_block,
                        preferred_element_type=jnp.float32,
                    )
                    return (query_grad, key_grad, value_grad)

                live = block_live(query_first, key_first, tile_starts, tile_first, block_rows)
                current = (query_totals[query_number], key_sums[key_number], value_sums[key_number])
                query_totals[query_number], key_sums[key_number], value_sums[key_number] = lax.cond(
                    live, backward_block, lambda unchanged: unchanged, current
                )
        key_whole = jnp.concatenate(key_sums, axis=0).reshape(tile_rows, kv_local * HD)
        value_whole = jnp.concatenate(value_sums, axis=0).reshape(tile_rows, kv_local * HD)
        partial_grads.append(jnp.stack([key_whole, value_whole]))
    grad_total = partial_grads[REACH]
    for offset in range(REACH - 1, -1, -1):
        grad_total = (
            shifted(grad_total.astype(jnp.bfloat16), "ctx", -1).astype(grad_total.dtype)
            + partial_grads[offset]
        )
    out_tile = jnp.concatenate(out_blocks, axis=0).reshape(tile_rows, q_local * HD)
    query_tile = (
        jnp.concatenate(query_totals, axis=0).reshape(tile_rows, q_local * HD).astype(jnp.bfloat16)
    )
    attn_out, grad_queries = (
        lax.all_to_all(out_tile, "head", split_axis=0, concat_axis=1, tiled=True),
        lax.all_to_all(query_tile, "head", split_axis=0, concat_axis=1, tiled=True),
    )
    token_grads = lax.all_to_all(
        grad_total.astype(jnp.bfloat16), "head", split_axis=1, concat_axis=2, tiled=True
    ).astype(grad_total.dtype)
    if copies > 1:
        token_grads = jnp.sum(token_grads.reshape(2, tok_dev, KVH, copies, HD), axis=3).reshape(
            2, tok_dev, KVH * HD
        )
    token_grads = token_grads.astype(jnp.bfloat16)
    return (attn_out, grad_queries, token_grads[0], token_grads[1])


KEY_ROWS = 256
CONTRACT_LAST = (((1,), (1,)), ((), ()))
CONTRACT_FIRST = (((0,), (0,)), ((), ()))
VMEM = pl.BlockSpec(memory_space=pltpu.VMEM)
SMEM = pl.BlockSpec(memory_space=pltpu.SMEM)


def flipped(value, axis, bits):
    count = lax.axis_size(axis)
    return lax.ppermute(value, axis, [(source, source ^ bits) for source in range(count)])


def pack_heads_kernel(cores, wide, left_ref, right_ref, *out_refs):
    part = lax.axis_index("ctx") // cores
    for flip, out_ref in enumerate(out_refs):
        columns = pl.ds(pl.multiple_of((part ^ flip) * wide, HD), wide)
        out_ref[:, :wide] = left_ref[:, columns]
        out_ref[:, wide:] = right_ref[:, columns]


def unpack_heads_kernel(cores, wide, *refs):
    in_refs, (left_ref, right_ref) = refs[:KVH], refs[KVH:]
    part = lax.axis_index("ctx") // cores
    for flip, in_ref in enumerate(in_refs):
        columns = pl.ds(pl.multiple_of((part ^ flip) * wide, HD), wide)
        left_ref[:, columns] = in_ref[:, :wide]
        right_ref[:, columns] = in_ref[:, wide:]


def pack_heads(left, right, cores):
    rows, wide = left.shape[0], left.shape[1] // KVH
    return pl.pallas_call(
        functools.partial(pack_heads_kernel, cores, wide),
        out_shape=[jax.ShapeDtypeStruct((rows, 2 * wide), left.dtype)] * KVH,
        in_specs=[VMEM] * 2,
        out_specs=[VMEM] * KVH,
    )(left, right)


def unpack_heads(pieces, cores):
    rows, wide = pieces[0].shape[0], pieces[0].shape[1] // 2
    return pl.pallas_call(
        functools.partial(unpack_heads_kernel, cores, wide),
        out_shape=[jax.ShapeDtypeStruct((rows, wide * KVH), pieces[0].dtype)] * 2,
        in_specs=[VMEM] * KVH,
        out_specs=[VMEM] * 2,
    )(*pieces)


def attention_kernel(cores, heads, tok, *refs):
    group = QH // KVH
    lanes = group * tok
    tile_rows = heads * tok
    kv_count = heads * cores
    lengths_ref, refs = refs[0], refs[1:]
    qd_refs, refs = refs[:KVH], refs[KVH:]
    kv_refs, refs = refs[:kv_count], refs[kv_count:]
    od_refs, refs = refs[:KVH], refs[KVH:]
    dkv_refs, refs = refs[:kv_count], refs[kv_count:]
    k_all, v_all, q_all, g_all, o_all, dq_all, dk_acc, dv_acc, score, acc = refs
    scaling = HD ** (-0.5)
    log_scale = scaling * math.log2(math.e)

    ctx_index, head_index = lax.axis_index("ctx"), lax.axis_index("head")
    part, core = ctx_index // cores, ctx_index % cores

    def rows_of(head_flip, core_flip, part_flip):
        tile = (part ^ part_flip) * cores + (core ^ core_flip)
        return pl.ds(pl.multiple_of((tile * heads + (head_index ^ head_flip)) * tok, tok), tok)

    for number, kv_ref in enumerate(kv_refs):
        for flip in range(KVH):
            rows = rows_of(number // cores, number % cores, flip)
            k_all[rows, :] = kv_ref[flip, :, :HD]
            v_all[rows, :] = kv_ref[flip, :, HD:]
    for flip, qd_ref in enumerate(qd_refs):
        for member in range(group):
            rows = slice(member * tok, (member + 1) * tok)
            q_all[flip, rows, :] = qd_ref[:, member * HD : (member + 1) * HD]
            g_all[flip, rows, :] = qd_ref[:, (group + member) * HD : (group + member + 1) * HD]
    dk_acc[...] = jnp.zeros_like(dk_acc)
    dv_acc[...] = jnp.zeros_like(dv_acc)

    def fold(values, combine):
        return combine(values.reshape(KEY_ROWS // 8, 8, lanes), axis=0)

    def query_block(flip, _):
        first = ((part ^ flip) * cores + core) * tile_rows + head_index * tok
        last = first + tok - 1
        query_pos = first + lax.broadcasted_iota(jnp.int32, (1, lanes), 1) % tok

        def document(number, carry):
            end, low, start_row = carry
            length = lengths_ref[number]
            end = end + length
            return (
                end,
                low + jnp.where(end <= first, length, 0),
                start_row + jnp.where(end <= query_pos, length, 0),
            )

        _, low, start_row = lax.fori_loop(
            0,
            lengths_ref.shape[0],
            document,
            (jnp.int32(0), jnp.int32(0), jnp.zeros((1, lanes), jnp.int32)),
        )
        key_block = low // KEY_ROWS
        count = last // KEY_ROWS + 1 - key_block
        q = q_all[flip]
        g = g_all[flip]

        def key_rows(step):
            return pl.ds(pl.multiple_of((key_block + step) * KEY_ROWS, KEY_ROWS), KEY_ROWS)

        def score_rows(step):
            return pl.ds(pl.multiple_of(step * KEY_ROWS, KEY_ROWS), KEY_ROWS)

        def scores_step(step, top):
            raw = lax.dot_general(
                k_all[key_rows(step), :], q, CONTRACT_LAST, preferred_element_type=jnp.float32
            )
            offset = (key_block + step) * KEY_ROWS
            key_pos = lax.broadcasted_iota(jnp.int32, (KEY_ROWS, lanes), 0)
            mask = (key_pos <= query_pos - offset) & (key_pos >= start_row - offset)
            raw = jnp.where(mask, raw, NEG_FILL)
            score[score_rows(step), :] = raw
            return jnp.maximum(top, fold(raw, jnp.max))

        top = lax.fori_loop(
            0, count, scores_step, jnp.full((8, lanes), NEG_FILL, jnp.float32)
        )
        top = jnp.max(top, axis=0, keepdims=True)
        acc[...] = jnp.zeros_like(acc)

        def out_step(step, total):
            prob = jnp.exp2((score[score_rows(step), :] - top) * log_scale)
            score[score_rows(step), :] = prob
            acc[...] += lax.dot_general(
                v_all[key_rows(step), :],
                prob.astype(jnp.bfloat16),
                CONTRACT_FIRST,
                preferred_element_type=jnp.float32,
            )
            return total + fold(prob, jnp.sum)

        total = lax.fori_loop(0, count, out_step, jnp.zeros((8, lanes), jnp.float32))
        inverse = 1.0 / jnp.sum(total, axis=0, keepdims=True)
        out = (acc[...] * inverse).T.astype(jnp.bfloat16)
        o_all[flip] = out
        delta = jnp.sum((out.astype(jnp.float32) * g.astype(jnp.float32)).T, axis=0, keepdims=True)
        acc[...] = jnp.zeros_like(acc)

        def grad_step(step, _):
            rows = key_rows(step)
            prob = score[score_rows(step), :] * inverse
            prob_grad = lax.dot_general(
                v_all[rows, :], g, CONTRACT_LAST, preferred_element_type=jnp.float32
            )
            score_grad = (prob * (prob_grad - delta)).astype(jnp.bfloat16)
            dv_acc[rows, :] += jnp.dot(
                prob.astype(jnp.bfloat16), g, preferred_element_type=jnp.float32
            )
            dk_acc[rows, :] += jnp.dot(score_grad, q, preferred_element_type=jnp.float32)
            acc[...] += lax.dot_general(
                k_all[rows, :], score_grad, CONTRACT_FIRST, preferred_element_type=jnp.float32
            )
            return 0

        lax.fori_loop(0, count, grad_step, 0)
        dq_all[flip] = (acc[...] * scaling).T.astype(jnp.bfloat16)
        return 0

    lax.fori_loop(0, KVH, query_block, 0)

    for flip, od_ref in enumerate(od_refs):
        for member in range(group):
            rows = slice(member * tok, (member + 1) * tok)
            od_ref[:, member * HD : (member + 1) * HD] = o_all[flip, rows, :]
            od_ref[:, (group + member) * HD : (group + member + 1) * HD] = dq_all[flip, rows, :]
    for number, dkv_ref in enumerate(dkv_refs):
        for flip in range(KVH):
            rows = rows_of(number // cores, number % cores, flip)
            dkv_ref[flip, :, :HD] = (dk_acc[rows, :] * scaling).astype(jnp.bfloat16)
            dkv_ref[flip, :, HD:] = dv_acc[rows, :].astype(jnp.bfloat16)


def attention(lengths, qd, kv, cores, heads):
    tok, group = qd[0].shape[0], QH // KVH
    total = KVH * cores * heads * tok
    window = (REACH * heads * tok + tok) // KEY_ROWS * KEY_ROWS + 2 * KEY_ROWS
    lanes = group * tok
    bf16, f32 = jnp.bfloat16, jnp.float32
    results = pl.pallas_call(
        functools.partial(attention_kernel, cores, heads, tok),
        out_shape=[jax.ShapeDtypeStruct(a.shape, a.dtype) for a in qd]
        + [jax.ShapeDtypeStruct(a.shape, a.dtype) for a in kv],
        in_specs=[SMEM] + [VMEM] * (len(qd) + len(kv)),
        out_specs=[VMEM] * (len(qd) + len(kv)),
        scratch_shapes=[
            pltpu.VMEM((total, HD), bf16),
            pltpu.VMEM((total, HD), bf16),
            pltpu.VMEM((KVH, lanes, HD), bf16),
            pltpu.VMEM((KVH, lanes, HD), bf16),
            pltpu.VMEM((KVH, lanes, HD), bf16),
            pltpu.VMEM((KVH, lanes, HD), bf16),
            pltpu.VMEM((total, HD), f32),
            pltpu.VMEM((total, HD), f32),
            pltpu.VMEM((window, lanes), f32),
            pltpu.VMEM((HD, lanes), f32),
        ],
        compiler_params=pltpu.CompilerParams(vmem_limit_bytes=40 * 1024 * 1024),
    )(lengths, *qd, *kv)
    return results[: len(qd)], results[len(qd) :]


def part_shards(queries, keys, values, d_out, lengths):
    heads = lax.axis_size("head")
    cores = lax.axis_size("ctx") // KVH

    def exchange(pieces):
        return [pieces[0]] + [flipped(pieces[s], "ctx", s * cores) for s in range(1, KVH)]

    kv_mine = jnp.stack(exchange(pack_heads(keys, values, cores)))
    qd = exchange(pack_heads(queries, d_out, cores))
    near, far = flipped(kv_mine, "head", 1), flipped(kv_mine, "head", 2)
    gathered = [kv_mine, near, far, flipped(far, "head", 1)]
    kv = []
    for piece in gathered:
        kv += [piece, flipped(piece, "ctx", 1)]
    od, dkv = attention(lengths, qd, kv, cores, heads)

    def summed(*terms):
        return sum(term.astype(jnp.float32) for term in terms).astype(jnp.bfloat16)

    both = [(dkv[2 * h], flipped(dkv[2 * h + 1], "ctx", 1)) for h in range(heads)]
    third = flipped(summed(*both[3]), "head", 1)
    second = flipped(summed(*both[2], third), "head", 2)
    first = flipped(summed(*both[1]), "head", 1)
    kv_total = summed(*both[0], first, second)
    attn_out, grad_queries = unpack_heads(exchange(od), cores)
    grad_keys, grad_values = unpack_heads(exchange([kv_total[s] for s in range(KVH)]), cores)
    return attn_out, grad_queries, grad_keys, grad_values


def solution(mesh):
    ctx_dev, head_dev = mesh.shape["ctx"], mesh.shape["head"]
    local = part_shards if ctx_dev == 2 * KVH and head_dev == 4 else shards
    rows = P(("ctx", "head"), None)
    return jax.shard_map(
        local,
        mesh=mesh,
        in_specs=(rows, rows, rows, rows, P()),
        out_specs=(rows, rows, rows, rows),
        check_vma=False,
    )
```

```python
import functools
import math

import jax
import jax.numpy as jnp
from jax import lax
from jax.experimental import pallas as pl
from jax.experimental.pallas import tpu as pltpu
from jax.sharding import PartitionSpec as P

QH = 16
KVH = 4
HD = 128
REACH = 4


NEG_FILL = -1e30


def shifted(value, axis, steps):
    count = lax.axis_size(axis)
    first, last = (max(0, -steps), min(count, count - steps))
    return lax.ppermute(value, axis, [(source, source + steps) for source in range(first, last)])


def doc_starts(lengths, first, count):
    doc_ends = jnp.cumsum(lengths)
    positions = first + jnp.arange(count, dtype=jnp.int32)
    passed = doc_ends[None, :] <= positions[:, None]
    return jnp.sum(jnp.where(passed, lengths[None, :], 0), axis=1)


def visible_pairs(query_first, key_first, start_rows, block_rows):
    query_pos = query_first + jnp.arange(block_rows, dtype=jnp.int32)
    key_pos = key_first + jnp.arange(block_rows, dtype=jnp.int32)
    mask = (key_pos[None, :] <= query_pos[:, None]) & (key_pos[None, :] >= start_rows[:, None])
    return mask[:, None, None, :]


def block_live(query_first, key_first, tile_starts, tile_first, block_rows):
    lowest = jnp.maximum(query_first, key_first)
    picked = jnp.clip(lowest - tile_first, 0, tile_starts.shape[0] - 1)
    first_start = lax.dynamic_index_in_dim(tile_starts, picked, 0, keepdims=False)
    return (lowest <= query_first + block_rows - 1) & (first_start <= key_first + block_rows - 1)


def shards(queries, keys, values, d_out, lengths):
    heads_dev = lax.axis_size("head")
    tok_dev = queries.shape[0]
    copies = max(1, heads_dev // KVH)
    kv_local = max(1, KVH // heads_dev)
    q_local = QH // heads_dev
    group_size = q_local // kv_local
    scaling = HD ** (-0.5)

    def spread(array_in):
        if copies > 1:
            return jnp.repeat(array_in.reshape(tok_dev, KVH, HD), copies, axis=1).reshape(
                tok_dev, KVH * copies * HD
            )
        return array_in

    q_tile, k_tile, v_tile = (
        lax.all_to_all(queries, "head", split_axis=1, concat_axis=0, tiled=True),
        lax.all_to_all(spread(keys), "head", split_axis=1, concat_axis=0, tiled=True),
        lax.all_to_all(spread(values), "head", split_axis=1, concat_axis=0, tiled=True),
    )
    tile_rows = q_tile.shape[0]
    block_rows = min(1024, tile_rows)
    block_count = tile_rows // block_rows
    ctx_index = lax.axis_index("ctx")
    tile_first = ctx_index * tile_rows
    tile_starts = doc_starts(lengths, tile_first, tile_rows)
    query_blocks = [
        q_tile[number * block_rows : (number + 1) * block_rows].reshape(
            block_rows, kv_local, group_size, HD
        )
        for number in range(block_count)
    ]
    start_blocks = [
        tile_starts[number * block_rows : (number + 1) * block_rows]
        for number in range(block_count)
    ]
    query_firsts = [tile_first + number * block_rows for number in range(block_count)]
    key_pair = jnp.stack([k_tile, v_tile])
    key_tiles = [key_pair]
    moving = key_pair
    for offset in range(1, REACH + 1):
        moving = shifted(moving, "ctx", 1)
        key_tiles.append(moving)

    def split_keys(tile_pair):
        key_list = [
            tile_pair[0, number * block_rows : (number + 1) * block_rows].reshape(
                block_rows, kv_local, HD
            )
            for number in range(block_count)
        ]
        value_list = [
            tile_pair[1, number * block_rows : (number + 1) * block_rows].reshape(
                block_rows, kv_local, HD
            )
            for number in range(block_count)
        ]
        return (key_list, value_list)

    states = [
        (
            jnp.full((block_rows, kv_local, group_size), NEG_FILL, jnp.float32),
            jnp.zeros((block_rows, kv_local, group_size), jnp.float32),
            jnp.zeros((block_rows, kv_local, group_size, HD), jnp.float32),
        )
        for number in range(block_count)
    ]
    for offset in range(REACH + 1):
        key_list, value_list = split_keys(key_tiles[offset])
        key_start = (ctx_index - offset) * tile_rows
        for query_number in range(block_count):
            query_block = query_blocks[query_number]
            query_first = query_firsts[query_number]
            start_rows = start_blocks[query_number]
            for key_number in range(block_count):
                key_block = key_list[key_number]
                value_block = value_list[key_number]
                key_first = key_start + key_number * block_rows

                def forward_block(
                    current,
                    query_block=query_block,
                    query_first=query_first,
                    start_rows=start_rows,
                    key_block=key_block,
                    value_block=value_block,
                    key_first=key_first,
                ):
                    max_old, sum_old, acc_old = current
                    mask = visible_pairs(query_first, key_first, start_rows, block_rows)
                    scores = (
                        jnp.einsum(
                            "qkgd,ckd->qkgc",
                            query_block,
                            key_block,
                            preferred_element_type=jnp.float32,
                        )
                        * scaling
                    )
                    scores = jnp.where(mask, scores, NEG_FILL)
                    max_new = jnp.maximum(max_old, jnp.max(scores, axis=-1))
                    prob_raw = jnp.where(mask, jnp.exp(scores - max_new[..., None]), 0.0)
                    rescale = jnp.exp(max_old - max_new)
                    sum_new = sum_old * rescale + jnp.sum(prob_raw, axis=-1)
                    acc_new = acc_old * rescale[..., None] + jnp.einsum(
                        "qkgc,ckd->qkgd",
                        prob_raw.astype(jnp.bfloat16),
                        value_block,
                        preferred_element_type=jnp.float32,
                    )
                    return (max_new, sum_new, acc_new)

                live = block_live(query_first, key_first, tile_starts, tile_first, block_rows)
                states[query_number] = lax.cond(
                    live, forward_block, lambda unchanged: unchanged, states[query_number]
                )
    out_blocks = [(state[2] / state[1][..., None]).astype(jnp.bfloat16) for state in states]
    lse_blocks = [state[0] + jnp.log(state[1]) for state in states]
    grad_tile = lax.all_to_all(d_out, "head", split_axis=1, concat_axis=0, tiled=True)
    grad_blocks = [
        grad_tile[number * block_rows : (number + 1) * block_rows].reshape(
            block_rows, kv_local, group_size, HD
        )
        for number in range(block_count)
    ]
    delta_blocks = [
        jnp.sum(
            grad_blocks[number].astype(jnp.float32) * out_blocks[number].astype(jnp.float32),
            axis=-1,
        )
        for number in range(block_count)
    ]
    query_totals = [
        jnp.zeros((block_rows, kv_local, group_size, HD), jnp.float32)
        for number in range(block_count)
    ]
    partial_grads = []
    for offset in range(REACH + 1):
        key_list, value_list = split_keys(key_tiles[offset])
        key_start = (ctx_index - offset) * tile_rows
        key_sums = [
            jnp.zeros((block_rows, kv_local, HD), jnp.float32) for number in range(block_count)
        ]
        value_sums = [
            jnp.zeros((block_rows, kv_local, HD), jnp.float32) for number in range(block_count)
        ]
        for query_number in range(block_count):
            query_block = query_blocks[query_number]
            grad_block = grad_blocks[query_number]
            query_first = query_firsts[query_number]
            start_rows = start_blocks[query_number]
            lse_rows = lse_blocks[query_number]
            delta_rows = delta_blocks[query_number]
            for key_number in range(block_count):
                key_block = key_list[key_number]
                value_block = value_list[key_number]
                key_first = key_start + key_number * block_rows

                def backward_block(
                    current,
                    query_block=query_block,
                    grad_block=grad_block,
                    query_first=query_first,
                    start_rows=start_rows,
                    lse_rows=lse_rows,
                    delta_rows=delta_rows,
                    key_block=key_block,
                    value_block=value_block,
                    key_first=key_first,
                ):
                    query_grad, key_grad, value_grad = current
                    mask = visible_pairs(query_first, key_first, start_rows, block_rows)
                    scores = (
                        jnp.einsum(
                            "qkgd,ckd->qkgc",
                            query_block,
                            key_block,
                            preferred_element_type=jnp.float32,
                        )
                        * scaling
                    )
                    prob_raw = jnp.where(mask, jnp.exp(scores - lse_rows[..., None]), 0.0)
                    weights = prob_raw.astype(jnp.bfloat16)
                    value_grad = value_grad + jnp.einsum(
                        "qkgc,qkgd->ckd", weights, grad_block, preferred_element_type=jnp.float32
                    )
                    prob_grad = jnp.einsum(
                        "qkgd,ckd->qkgc",
                        grad_block,
                        value_block,
                        preferred_element_type=jnp.float32,
                    )
                    score_grad = (prob_raw * (prob_grad - delta_rows[..., None]) * scaling).astype(
                        jnp.bfloat16
                    )
                    query_grad = query_grad + jnp.einsum(
                        "qkgc,ckd->qkgd", score_grad, key_block, preferred_element_type=jnp.float32
                    )
                    key_grad = key_grad + jnp.einsum(
                        "qkgc,qkgd->ckd",
                        score_grad,
                        query_block,
                        preferred_element_type=jnp.float32,
                    )
                    return (query_grad, key_grad, value_grad)

                live = block_live(query_first, key_first, tile_starts, tile_first, block_rows)
                current = (query_totals[query_number], key_sums[key_number], value_sums[key_number])
                query_totals[query_number], key_sums[key_number], value_sums[key_number] = lax.cond(
                    live, backward_block, lambda unchanged: unchanged, current
                )
        key_whole = jnp.concatenate(key_sums, axis=0).reshape(tile_rows, kv_local * HD)
        value_whole = jnp.concatenate(value_sums, axis=0).reshape(tile_rows, kv_local * HD)
        partial_grads.append(jnp.stack([key_whole, value_whole]))
    grad_total = partial_grads[REACH]
    for offset in range(REACH - 1, -1, -1):
        grad_total = (
            shifted(grad_total.astype(jnp.bfloat16), "ctx", -1).astype(grad_total.dtype)
            + partial_grads[offset]
        )
    out_tile = jnp.concatenate(out_blocks, axis=0).reshape(tile_rows, q_local * HD)
    query_tile = (
        jnp.concatenate(query_totals, axis=0).reshape(tile_rows, q_local * HD).astype(jnp.bfloat16)
    )
    attn_out, grad_queries = (
        lax.all_to_all(out_tile, "head", split_axis=0, concat_axis=1, tiled=True),
        lax.all_to_all(query_tile, "head", split_axis=0, concat_axis=1, tiled=True),
    )
    token_grads = lax.all_to_all(
        grad_total.astype(jnp.bfloat16), "head", split_axis=1, concat_axis=2, tiled=True
    ).astype(grad_total.dtype)
    if copies > 1:
        token_grads = jnp.sum(token_grads.reshape(2, tok_dev, KVH, copies, HD), axis=3).reshape(
            2, tok_dev, KVH * HD
        )
    token_grads = token_grads.astype(jnp.bfloat16)
    return (attn_out, grad_queries, token_grads[0], token_grads[1])


CHUNKS = ((0, 1, 2, 3),)
CONTRACT_LAST = (((1,), (1,)), ((), ()))
CONTRACT_FIRST = (((0,), (0,)), ((), ()))
VMEM = pl.BlockSpec(memory_space=pltpu.VMEM)
SMEM = pl.BlockSpec(memory_space=pltpu.SMEM)


def flipped(value, axis, bits):
    count = lax.axis_size(axis)
    return lax.ppermute(value, axis, [(source, source ^ bits) for source in range(count)])


def pack_heads_kernel(cores, wide, left_ref, right_ref, *out_refs):
    part = lax.axis_index("ctx") // cores
    for flip, out_ref in enumerate(out_refs):
        columns = pl.ds(pl.multiple_of((part ^ flip) * wide, HD), wide)
        out_ref[:, :wide] = left_ref[:, columns]
        out_ref[:, wide:] = right_ref[:, columns]


def unpack_heads_kernel(cores, wide, *refs):
    in_refs, (left_ref, right_ref) = refs[:KVH], refs[KVH:]
    part = lax.axis_index("ctx") // cores
    for flip, in_ref in enumerate(in_refs):
        columns = pl.ds(pl.multiple_of((part ^ flip) * wide, HD), wide)
        left_ref[:, columns] = in_ref[:, :wide]
        right_ref[:, columns] = in_ref[:, wide:]


def pack_heads(left, right, cores):
    rows, wide = left.shape[0], left.shape[1] // KVH
    return pl.pallas_call(
        functools.partial(pack_heads_kernel, cores, wide),
        out_shape=[jax.ShapeDtypeStruct((rows, 2 * wide), left.dtype)] * KVH,
        in_specs=[VMEM] * 2,
        out_specs=[VMEM] * KVH,
    )(left, right)


def unpack_heads(pieces, cores):
    rows, wide = pieces[0].shape[0], pieces[0].shape[1] // 2
    return pl.pallas_call(
        functools.partial(unpack_heads_kernel, cores, wide),
        out_shape=[jax.ShapeDtypeStruct((rows, wide * KVH), pieces[0].dtype)] * 2,
        in_specs=[VMEM] * KVH,
        out_specs=[VMEM] * 2,
    )(*pieces)


KEY_ROWS = 256
BATCH = 4
GRAD_BATCH = 4
MARKS = 128
HIDDEN = -(2.0**100)


def attention_kernel(cores, heads, tok, *refs):
    group = QH // KVH
    lanes = group * tok
    tile_rows = heads * tok
    kv_count = heads * cores * len(CHUNKS)
    lengths_ref, marks_ref, refs = refs[0], refs[1], refs[2:]
    docs = lengths_ref.shape[0]
    qd_refs, refs = refs[:KVH], refs[KVH:]
    kv_refs, refs = refs[:kv_count], refs[kv_count:]
    od_refs, refs = refs[:KVH], refs[KVH:]
    dkv_refs, refs = refs[: cores * len(CHUNKS)], refs[cores * len(CHUNKS) :]
    k_all, v_all, q_wide, g_wide, dk_acc, dv_acc, score, prob, tops, acc, table = refs
    scaling = HD ** (-0.5)
    log_scale = scaling * math.log2(math.e)
    f32, bf16 = jnp.float32, jnp.bfloat16

    ctx_index, head_index = lax.axis_index("ctx"), lax.axis_index("head")
    part, core = ctx_index // cores, ctx_index % cores

    def rows_of(head_flip, core_flip, part_flip):
        tile = (part ^ part_flip) * cores + (core ^ core_flip)
        return pl.ds(pl.multiple_of((tile * heads + (head_index ^ head_flip)) * tok, tok), tok)

    for chunk_number, chunk in enumerate(CHUNKS):
        for number in range(heads * cores):
            kv_ref = kv_refs[chunk_number * heads * cores + number]
            for place, flip in enumerate(chunk):
                rows = rows_of(number // cores, number % cores, flip)
                k_all[rows, :] = kv_ref[place, :, :HD]
                v_all[rows, :] = kv_ref[place, :, HD:]
    feature = lax.broadcasted_iota(jnp.int32, (tok, MARKS), 1)
    for flip, qd_ref in enumerate(qd_refs):
        own_marks = marks_ref[rows_of(0, 0, flip), :].astype(f32)
        bias = jnp.where(feature < docs, (1.0 - own_marks) * HIDDEN, 0.0).astype(bf16)
        for member in range(group):
            rows = slice(member * tok, (member + 1) * tok)
            q_wide[flip, rows, :HD] = qd_ref[:, member * HD : (member + 1) * HD]
            q_wide[flip, rows, HD:] = bias
            g_wide[flip, rows, :HD] = qd_ref[:, (group + member) * HD : (group + member + 1) * HD]
    dk_acc[...] = jnp.zeros_like(dk_acc)
    dv_acc[...] = jnp.zeros_like(dv_acc)
    tops[...] = jnp.full_like(tops, NEG_FILL)
    acc[...] = jnp.zeros_like(acc)

    def entry(number, flip, row, limit):
        table[0, number] = flip
        table[1, number] = row
        table[2, number] = limit

    total = jnp.int32(0)
    for flip in range(KVH):
        first = ((part ^ flip) * cores + core) * tile_rows + head_index * tok
        end, low = jnp.int32(0), jnp.int32(0)
        for number in range(docs):
            length = lengths_ref[number]
            end = end + length
            low = low + jnp.where(end <= first, length, 0)
        count = (first + tok - low // tok * tok + KEY_ROWS - 1) // KEY_ROWS
        begin = jnp.maximum(first + tok - count * KEY_ROWS, 0)

        def listed(step, _, flip=flip, first=first, begin=begin, total=total):
            row = begin + step * KEY_ROWS
            entry(total + step, flip, row, first - row)
            return 0

        lax.fori_loop(0, count, listed, 0)
        total = total + count
    for spare in range(BATCH - 1):
        entry(total + spare, 0, 0, -(1 << 20))
    rounds = (total + BATCH - 1) // BATCH

    def sweep(body, batch):
        def one_round(number, _):
            body([number * batch + place for place in range(batch)])
            return 0

        lax.fori_loop(0, rounds * (BATCH // batch), one_round, 0)

    def key_rows(item):
        return pl.ds(pl.multiple_of(table[1, item], tok), KEY_ROWS)

    def score_rows(item):
        return pl.ds(pl.multiple_of(item * KEY_ROWS, KEY_ROWS), KEY_ROWS)

    def wide(ref, rows):
        return jnp.concatenate([ref[rows, :], marks_ref[rows, :]], axis=1)

    key_row = lax.broadcasted_iota(jnp.int32, (KEY_ROWS, lanes), 0)
    query_row = lax.broadcasted_iota(jnp.int32, (1, lanes), 1) % tok

    def scores_round(items):
        raws = [
            lax.dot_general(
                wide(k_all, key_rows(item)),
                q_wide[table[0, item]],
                CONTRACT_LAST,
                preferred_element_type=f32,
            )
            for item in items
        ]
        for item, raw in zip(items, raws):
            raw = jnp.where(key_row <= query_row + table[2, item], raw, NEG_FILL)
            score[score_rows(item), :] = raw
            flip = table[0, item]
            tops[flip] = jnp.maximum(
                tops[flip], jnp.max(raw.reshape(KEY_ROWS // 8, 8, lanes), axis=0)
            )

    sweep(scores_round, BATCH)
    for flip in range(KVH):
        tops[flip] = jnp.broadcast_to(jnp.max(tops[flip], axis=0, keepdims=True), (8, lanes))

    ones = jnp.ones((acc.shape[1] - HD, KEY_ROWS), bf16)

    def out_round(items):
        weights = [
            jnp.exp2((score[score_rows(item), :] - tops[table[0, item], :1]) * log_scale).astype(bf16)
            for item in items
        ]
        for item, weight in zip(items, weights):
            prob[score_rows(item), :] = weight
        parts = [
            jnp.dot(
                jnp.concatenate([v_all[key_rows(item), :].T, ones], axis=0),
                weight,
                preferred_element_type=f32,
            )
            for item, weight in zip(items, weights)
        ]
        for item, value in zip(items, parts):
            acc[table[0, item]] += value

    sweep(out_round, BATCH)
    feature = lax.broadcasted_iota(jnp.int32, (lanes, MARKS), 1)
    for flip in range(KVH):
        inverse = 1.0 / acc[flip, HD : HD + 1, :]
        out = (acc[flip, :HD, :] * inverse).T.astype(bf16)
        g = g_wide[flip, :, :HD].astype(f32)
        g_scaled = (g * jnp.broadcast_to(inverse, (HD, lanes)).T).astype(bf16)
        delta = jnp.sum(out.astype(f32) * g_scaled.astype(f32), axis=1, keepdims=True)
        high = delta.astype(bf16).astype(f32)
        extra = jnp.where(feature == docs, -high, jnp.where(feature == docs + 1, high - delta, 0.0))
        g_wide[flip, :, :HD] = g_scaled
        g_wide[flip, :, HD:] = extra.astype(bf16)
        for member in range(group):
            rows = slice(member * tok, (member + 1) * tok)
            od_refs[flip][:, member * HD : (member + 1) * HD] = out[rows, :]
        acc[flip] = jnp.zeros_like(acc[flip])

    def grad_round(items):
        weights = [prob[score_rows(item), :] for item in items]
        slopes = [
            lax.dot_general(
                wide(v_all, key_rows(item)),
                g_wide[table[0, item]],
                CONTRACT_LAST,
                preferred_element_type=f32,
            )
            for item in items
        ]
        score_grads = [
            (weight.astype(f32) * slope).astype(bf16) for weight, slope in zip(weights, slopes)
        ]
        for item, weight, score_grad in zip(items, weights, score_grads):
            flip, rows = table[0, item], key_rows(item)
            dv_acc[rows, :] += jnp.dot(weight, g_wide[flip, :, :HD], preferred_element_type=f32)
            dk_acc[rows, :] += jnp.dot(score_grad, q_wide[flip, :, :HD], preferred_element_type=f32)
            acc[flip, :HD, :] += lax.dot_general(
                k_all[rows, :], score_grad, CONTRACT_FIRST, preferred_element_type=f32
            )

    sweep(grad_round, GRAD_BATCH)

    for flip, od_ref in enumerate(od_refs):
        turned = (acc[flip, :HD, :] * scaling).T.astype(bf16)
        for member in range(group):
            rows = slice(member * tok, (member + 1) * tok)
            od_ref[:, (group + member) * HD : (group + member + 1) * HD] = turned[rows, :]
    for chunk_number, chunk in enumerate(CHUNKS):
        for core_flip in range(cores):
            dkv_ref = dkv_refs[chunk_number * cores + core_flip]
            for head_flip in range(heads):
                for place, flip in enumerate(chunk):
                    rows = rows_of(head_flip, core_flip, flip)
                    dkv_ref[head_flip, place, :, :HD] = (dk_acc[rows, :] * scaling).astype(bf16)
                    dkv_ref[head_flip, place, :, HD:] = dv_acc[rows, :].astype(bf16)


def document_marks(lengths, total):
    docs = lengths.shape[0]
    ends = jnp.cumsum(lengths)
    begins = jnp.pad(ends - lengths, (0, MARKS - docs))
    lane = jnp.arange(MARKS)
    ends = jnp.where(lane < docs, jnp.pad(ends, (0, MARKS - docs)), jnp.where(lane < docs + 2, total, 0))
    position = jnp.arange(total, dtype=jnp.int32)[:, None]
    return ((position >= begins[None, :]) & (position < ends[None, :])).astype(jnp.bfloat16)


def attention(lengths, qd, kv, cores, heads):
    tok, group = qd[0].shape[0], QH // KVH
    total = KVH * cores * heads * tok
    lanes = group * tok
    reach = REACH * heads * tok
    pair = sum(-(-(keys + tok) // KEY_ROWS) for keys in (reach, reach // 2))
    items = -(-KVH // 2 * pair // BATCH) * BATCH
    bf16, f32 = jnp.bfloat16, jnp.float32
    results = pl.pallas_call(
        functools.partial(attention_kernel, cores, heads, tok),
        out_shape=[jax.ShapeDtypeStruct(a.shape, a.dtype) for a in qd]
        + [
            jax.ShapeDtypeStruct((heads, len(chunk), tok, 2 * HD), bf16)
            for chunk in CHUNKS
            for _ in range(cores)
        ],
        in_specs=[SMEM] + [VMEM] * (1 + len(qd) + len(kv)),
        out_specs=[VMEM] * (len(qd) + cores * len(CHUNKS)),
        scratch_shapes=[
            pltpu.VMEM((total, HD), bf16),
            pltpu.VMEM((total, HD), bf16),
            pltpu.VMEM((KVH, lanes, HD + MARKS), bf16),
            pltpu.VMEM((KVH, lanes, HD + MARKS), bf16),
            pltpu.VMEM((total, HD), f32),
            pltpu.VMEM((total, HD), f32),
            pltpu.VMEM((items * KEY_ROWS, lanes), f32),
            pltpu.VMEM((items * KEY_ROWS, lanes), bf16),
            pltpu.VMEM((KVH, 8, lanes), f32),
            pltpu.VMEM((KVH, HD + 16, lanes), f32),
            pltpu.SMEM((3, items + BATCH), jnp.int32),
        ],
        compiler_params=pltpu.CompilerParams(vmem_limit_bytes=48 * 1024 * 1024),
    )(lengths, document_marks(lengths, total), *qd, *kv)
    return results[: len(qd)], results[len(qd) :]


def part_shards(queries, keys, values, d_out, lengths):
    heads = lax.axis_size("head")
    cores = lax.axis_size("ctx") // KVH

    def exchange(pieces):
        return [pieces[0]] + [flipped(pieces[s], "ctx", s * cores) for s in range(1, KVH)]

    pieces = exchange(pack_heads(keys, values, cores))
    qd = exchange(pack_heads(queries, d_out, cores))
    kv = []
    for chunk in CHUNKS:
        own = jnp.stack([pieces[flip] for flip in chunk])
        far = flipped(own, "head", 2)
        near = flipped(own, "head", 1)
        for piece in (own, near, far, flipped(far, "head", 1)):
            kv += [piece, flipped(piece, "ctx", 1)]
    od, dkv = attention(lengths, qd, kv, cores, heads)

    def summed(*terms):
        return sum(term.astype(jnp.float32) for term in terms).astype(jnp.bfloat16)

    grads = [None] * KVH
    for number in reversed(range(len(CHUNKS))):
        both = (dkv[number * cores], flipped(dkv[number * cores + 1], "ctx", 1))
        third = flipped(summed(*(term[3] for term in both)), "head", 1)
        second = flipped(summed(*(term[2] for term in both), third), "head", 2)
        first, _ = lax.optimization_barrier((summed(*(term[1] for term in both)), third))
        first = flipped(first, "head", 1)
        for place, flip in enumerate(CHUNKS[number]):
            grads[flip] = summed(*(term[0, place] for term in both), first[place], second[place])
    attn_out, grad_queries = unpack_heads(exchange(od), cores)
    grad_keys, grad_values = unpack_heads(exchange(grads), cores)
    return attn_out, grad_queries, grad_keys, grad_values


def solution(mesh):
    ctx_dev, head_dev = mesh.shape["ctx"], mesh.shape["head"]
    local = part_shards if ctx_dev == 2 * KVH and head_dev == 4 else shards
    rows = P(("ctx", "head"), None)
    return jax.shard_map(
        local,
        mesh=mesh,
        in_specs=(rows, rows, rows, rows, P()),
        out_specs=(rows, rows, rows, rows),
        check_vma=False,
    )
```

```python
import functools
import math

import jax
import jax.numpy as jnp
from jax import lax
from jax.experimental import pallas as pl
from jax.experimental.pallas import tpu as pltpu
from jax.sharding import PartitionSpec as P

QH = 16
KVH = 4
HD = 128
REACH = 4


NEG_FILL = -1e30


def shifted(value, axis, steps):
    count = lax.axis_size(axis)
    first, last = (max(0, -steps), min(count, count - steps))
    return lax.ppermute(value, axis, [(source, source + steps) for source in range(first, last)])


def doc_starts(lengths, first, count):
    doc_ends = jnp.cumsum(lengths)
    positions = first + jnp.arange(count, dtype=jnp.int32)
    passed = doc_ends[None, :] <= positions[:, None]
    return jnp.sum(jnp.where(passed, lengths[None, :], 0), axis=1)


def visible_pairs(query_first, key_first, start_rows, block_rows):
    query_pos = query_first + jnp.arange(block_rows, dtype=jnp.int32)
    key_pos = key_first + jnp.arange(block_rows, dtype=jnp.int32)
    mask = (key_pos[None, :] <= query_pos[:, None]) & (key_pos[None, :] >= start_rows[:, None])
    return mask[:, None, None, :]


def block_live(query_first, key_first, tile_starts, tile_first, block_rows):
    lowest = jnp.maximum(query_first, key_first)
    picked = jnp.clip(lowest - tile_first, 0, tile_starts.shape[0] - 1)
    first_start = lax.dynamic_index_in_dim(tile_starts, picked, 0, keepdims=False)
    return (lowest <= query_first + block_rows - 1) & (first_start <= key_first + block_rows - 1)


def shards(queries, keys, values, d_out, lengths):
    heads_dev = lax.axis_size("head")
    tok_dev = queries.shape[0]
    copies = max(1, heads_dev // KVH)
    kv_local = max(1, KVH // heads_dev)
    q_local = QH // heads_dev
    group_size = q_local // kv_local
    scaling = HD ** (-0.5)

    def spread(array_in):
        if copies > 1:
            return jnp.repeat(array_in.reshape(tok_dev, KVH, HD), copies, axis=1).reshape(
                tok_dev, KVH * copies * HD
            )
        return array_in

    q_tile, k_tile, v_tile = (
        lax.all_to_all(queries, "head", split_axis=1, concat_axis=0, tiled=True),
        lax.all_to_all(spread(keys), "head", split_axis=1, concat_axis=0, tiled=True),
        lax.all_to_all(spread(values), "head", split_axis=1, concat_axis=0, tiled=True),
    )
    tile_rows = q_tile.shape[0]
    block_rows = min(1024, tile_rows)
    block_count = tile_rows // block_rows
    ctx_index = lax.axis_index("ctx")
    tile_first = ctx_index * tile_rows
    tile_starts = doc_starts(lengths, tile_first, tile_rows)
    query_blocks = [
        q_tile[number * block_rows : (number + 1) * block_rows].reshape(
            block_rows, kv_local, group_size, HD
        )
        for number in range(block_count)
    ]
    start_blocks = [
        tile_starts[number * block_rows : (number + 1) * block_rows]
        for number in range(block_count)
    ]
    query_firsts = [tile_first + number * block_rows for number in range(block_count)]
    key_pair = jnp.stack([k_tile, v_tile])
    key_tiles = [key_pair]
    moving = key_pair
    for offset in range(1, REACH + 1):
        moving = shifted(moving, "ctx", 1)
        key_tiles.append(moving)

    def split_keys(tile_pair):
        key_list = [
            tile_pair[0, number * block_rows : (number + 1) * block_rows].reshape(
                block_rows, kv_local, HD
            )
            for number in range(block_count)
        ]
        value_list = [
            tile_pair[1, number * block_rows : (number + 1) * block_rows].reshape(
                block_rows, kv_local, HD
            )
            for number in range(block_count)
        ]
        return (key_list, value_list)

    states = [
        (
            jnp.full((block_rows, kv_local, group_size), NEG_FILL, jnp.float32),
            jnp.zeros((block_rows, kv_local, group_size), jnp.float32),
            jnp.zeros((block_rows, kv_local, group_size, HD), jnp.float32),
        )
        for number in range(block_count)
    ]
    for offset in range(REACH + 1):
        key_list, value_list = split_keys(key_tiles[offset])
        key_start = (ctx_index - offset) * tile_rows
        for query_number in range(block_count):
            query_block = query_blocks[query_number]
            query_first = query_firsts[query_number]
            start_rows = start_blocks[query_number]
            for key_number in range(block_count):
                key_block = key_list[key_number]
                value_block = value_list[key_number]
                key_first = key_start + key_number * block_rows

                def forward_block(
                    current,
                    query_block=query_block,
                    query_first=query_first,
                    start_rows=start_rows,
                    key_block=key_block,
                    value_block=value_block,
                    key_first=key_first,
                ):
                    max_old, sum_old, acc_old = current
                    mask = visible_pairs(query_first, key_first, start_rows, block_rows)
                    scores = (
                        jnp.einsum(
                            "qkgd,ckd->qkgc",
                            query_block,
                            key_block,
                            preferred_element_type=jnp.float32,
                        )
                        * scaling
                    )
                    scores = jnp.where(mask, scores, NEG_FILL)
                    max_new = jnp.maximum(max_old, jnp.max(scores, axis=-1))
                    prob_raw = jnp.where(mask, jnp.exp(scores - max_new[..., None]), 0.0)
                    rescale = jnp.exp(max_old - max_new)
                    sum_new = sum_old * rescale + jnp.sum(prob_raw, axis=-1)
                    acc_new = acc_old * rescale[..., None] + jnp.einsum(
                        "qkgc,ckd->qkgd",
                        prob_raw.astype(jnp.bfloat16),
                        value_block,
                        preferred_element_type=jnp.float32,
                    )
                    return (max_new, sum_new, acc_new)

                live = block_live(query_first, key_first, tile_starts, tile_first, block_rows)
                states[query_number] = lax.cond(
                    live, forward_block, lambda unchanged: unchanged, states[query_number]
                )
    out_blocks = [(state[2] / state[1][..., None]).astype(jnp.bfloat16) for state in states]
    lse_blocks = [state[0] + jnp.log(state[1]) for state in states]
    grad_tile = lax.all_to_all(d_out, "head", split_axis=1, concat_axis=0, tiled=True)
    grad_blocks = [
        grad_tile[number * block_rows : (number + 1) * block_rows].reshape(
            block_rows, kv_local, group_size, HD
        )
        for number in range(block_count)
    ]
    delta_blocks = [
        jnp.sum(
            grad_blocks[number].astype(jnp.float32) * out_blocks[number].astype(jnp.float32),
            axis=-1,
        )
        for number in range(block_count)
    ]
    query_totals = [
        jnp.zeros((block_rows, kv_local, group_size, HD), jnp.float32)
        for number in range(block_count)
    ]
    partial_grads = []
    for offset in range(REACH + 1):
        key_list, value_list = split_keys(key_tiles[offset])
        key_start = (ctx_index - offset) * tile_rows
        key_sums = [
            jnp.zeros((block_rows, kv_local, HD), jnp.float32) for number in range(block_count)
        ]
        value_sums = [
            jnp.zeros((block_rows, kv_local, HD), jnp.float32) for number in range(block_count)
        ]
        for query_number in range(block_count):
            query_block = query_blocks[query_number]
            grad_block = grad_blocks[query_number]
            query_first = query_firsts[query_number]
            start_rows = start_blocks[query_number]
            lse_rows = lse_blocks[query_number]
            delta_rows = delta_blocks[query_number]
            for key_number in range(block_count):
                key_block = key_list[key_number]
                value_block = value_list[key_number]
                key_first = key_start + key_number * block_rows

                def backward_block(
                    current,
                    query_block=query_block,
                    grad_block=grad_block,
                    query_first=query_first,
                    start_rows=start_rows,
                    lse_rows=lse_rows,
                    delta_rows=delta_rows,
                    key_block=key_block,
                    value_block=value_block,
                    key_first=key_first,
                ):
                    query_grad, key_grad, value_grad = current
                    mask = visible_pairs(query_first, key_first, start_rows, block_rows)
                    scores = (
                        jnp.einsum(
                            "qkgd,ckd->qkgc",
                            query_block,
                            key_block,
                            preferred_element_type=jnp.float32,
                        )
                        * scaling
                    )
                    prob_raw = jnp.where(mask, jnp.exp(scores - lse_rows[..., None]), 0.0)
                    weights = prob_raw.astype(jnp.bfloat16)
                    value_grad = value_grad + jnp.einsum(
                        "qkgc,qkgd->ckd", weights, grad_block, preferred_element_type=jnp.float32
                    )
                    prob_grad = jnp.einsum(
                        "qkgd,ckd->qkgc",
                        grad_block,
                        value_block,
                        preferred_element_type=jnp.float32,
                    )
                    score_grad = (prob_raw * (prob_grad - delta_rows[..., None]) * scaling).astype(
                        jnp.bfloat16
                    )
                    query_grad = query_grad + jnp.einsum(
                        "qkgc,ckd->qkgd", score_grad, key_block, preferred_element_type=jnp.float32
                    )
                    key_grad = key_grad + jnp.einsum(
                        "qkgc,qkgd->ckd",
                        score_grad,
                        query_block,
                        preferred_element_type=jnp.float32,
                    )
                    return (query_grad, key_grad, value_grad)

                live = block_live(query_first, key_first, tile_starts, tile_first, block_rows)
                current = (query_totals[query_number], key_sums[key_number], value_sums[key_number])
                query_totals[query_number], key_sums[key_number], value_sums[key_number] = lax.cond(
                    live, backward_block, lambda unchanged: unchanged, current
                )
        key_whole = jnp.concatenate(key_sums, axis=0).reshape(tile_rows, kv_local * HD)
        value_whole = jnp.concatenate(value_sums, axis=0).reshape(tile_rows, kv_local * HD)
        partial_grads.append(jnp.stack([key_whole, value_whole]))
    grad_total = partial_grads[REACH]
    for offset in range(REACH - 1, -1, -1):
        grad_total = (
            shifted(grad_total.astype(jnp.bfloat16), "ctx", -1).astype(grad_total.dtype)
            + partial_grads[offset]
        )
    out_tile = jnp.concatenate(out_blocks, axis=0).reshape(tile_rows, q_local * HD)
    query_tile = (
        jnp.concatenate(query_totals, axis=0).reshape(tile_rows, q_local * HD).astype(jnp.bfloat16)
    )
    attn_out, grad_queries = (
        lax.all_to_all(out_tile, "head", split_axis=0, concat_axis=1, tiled=True),
        lax.all_to_all(query_tile, "head", split_axis=0, concat_axis=1, tiled=True),
    )
    token_grads = lax.all_to_all(
        grad_total.astype(jnp.bfloat16), "head", split_axis=1, concat_axis=2, tiled=True
    ).astype(grad_total.dtype)
    if copies > 1:
        token_grads = jnp.sum(token_grads.reshape(2, tok_dev, KVH, copies, HD), axis=3).reshape(
            2, tok_dev, KVH * HD
        )
    token_grads = token_grads.astype(jnp.bfloat16)
    return (attn_out, grad_queries, token_grads[0], token_grads[1])


CHUNKS = ((0, 1, 2, 3),)
CONTRACT_LAST = (((1,), (1,)), ((), ()))
CONTRACT_FIRST = (((0,), (0,)), ((), ()))
VMEM = pl.BlockSpec(memory_space=pltpu.VMEM)
SMEM = pl.BlockSpec(memory_space=pltpu.SMEM)
SMALL = pltpu.CompilerParams(vmem_limit_bytes=8 * 1024 * 1024)


def flipped(value, axis, bits):
    count = lax.axis_size(axis)
    return lax.ppermute(value, axis, [(source, source ^ bits) for source in range(count)])


def piece_columns(pieces, flip, wide):
    index = lax.axis_index("ctx") // (lax.axis_size("ctx") // pieces)
    return pl.ds(pl.multiple_of((index ^ flip) * wide, HD), wide)


def split_heads_kernel(pieces, wide, left_ref, right_ref, *piece_refs):
    for flip, piece_ref in enumerate(piece_refs):
        columns = piece_columns(pieces, flip, wide)
        piece_ref[:, :wide] = left_ref[:, columns]
        piece_ref[:, wide:] = right_ref[:, columns]


def join_heads_kernel(pieces, wide, *refs):
    piece_refs, (left_ref, right_ref) = refs[:pieces], refs[pieces:]
    for flip, piece_ref in enumerate(piece_refs):
        columns = piece_columns(pieces, flip, wide)
        left_ref[:, columns] = piece_ref[:, :wide]
        right_ref[:, columns] = piece_ref[:, wide:]


def split_heads(left, right, pieces):
    rows, wide = left.shape[0], left.shape[1] // pieces
    return pl.pallas_call(
        functools.partial(split_heads_kernel, pieces, wide),
        out_shape=[jax.ShapeDtypeStruct((rows, 2 * wide), left.dtype)] * pieces,
        in_specs=[VMEM] * 2,
        out_specs=[VMEM] * pieces,
        compiler_params=SMALL,
    )(left, right)


def join_heads(parts):
    pieces = len(parts)
    rows, wide = parts[0].shape[0], parts[0].shape[1] // 2
    return pl.pallas_call(
        functools.partial(join_heads_kernel, pieces, wide),
        out_shape=[jax.ShapeDtypeStruct((rows, wide * pieces), parts[0].dtype)] * 2,
        in_specs=[VMEM] * pieces,
        out_specs=[VMEM] * 2,
        compiler_params=SMALL,
    )(*parts)


def prepare_kernel(pieces, wide, lengths_ref, left_ref, right_ref, *out_refs):
    piece_refs, marks_ref = out_refs[:pieces], out_refs[pieces]
    split_heads_kernel(pieces, wide, left_ref, right_ref, *piece_refs)
    total, docs = marks_ref.shape[0], lengths_ref.shape[0]
    lane = lax.broadcasted_iota(jnp.int32, (1, MARKS), 1)
    begins = jnp.zeros((1, MARKS), jnp.int32)
    ends = jnp.where(lane < docs, total, 0)
    end = jnp.int32(0)
    for number in range(docs):
        begins = jnp.where(lane == number, end, begins)
        end = end + lengths_ref[number]
        ends = jnp.where(lane == number, end, ends)

    def some_rows(step, _):
        rows = pl.ds(pl.multiple_of(step * KEY_ROWS, KEY_ROWS), KEY_ROWS)
        position = step * KEY_ROWS + lax.broadcasted_iota(jnp.int32, (KEY_ROWS, MARKS), 0)
        inside = (position >= begins) & (position < ends)
        marks_ref[rows, :] = jnp.where(inside, 1.0, 0.0).astype(jnp.bfloat16)
        return 0

    lax.fori_loop(0, total // KEY_ROWS, some_rows, 0)


def prepare(lengths, left, right, pieces, total):
    rows, wide = left.shape[0], left.shape[1] // pieces
    results = pl.pallas_call(
        functools.partial(prepare_kernel, pieces, wide),
        out_shape=[jax.ShapeDtypeStruct((rows, 2 * wide), left.dtype)] * pieces
        + [jax.ShapeDtypeStruct((total, MARKS), jnp.bfloat16)],
        in_specs=[SMEM] + [VMEM] * 2,
        out_specs=[VMEM] * (pieces + 1),
        compiler_params=SMALL,
    )(lengths, left, right)
    return results[:pieces], results[pieces]


KEY_ROWS = 256
BATCH = 4
GRAD_BATCH = 4
MARKS = 128
HIDDEN = -(2.0**100)


def attention_kernel(cores, heads, tok, *refs):
    group = QH // KVH
    lanes = group * tok
    tile_rows = heads * tok
    kv_count = heads * cores * len(CHUNKS)
    lengths_ref, marks_ref, refs = refs[0], refs[1], refs[2:]
    docs = lengths_ref.shape[0]
    qd_refs, refs = refs[:KVH], refs[KVH:]
    kv_refs, refs = refs[:kv_count], refs[kv_count:]
    od_refs, refs = refs[:KVH], refs[KVH:]
    dkv_refs, refs = refs[: cores * len(CHUNKS)], refs[cores * len(CHUNKS) :]
    k_all, v_all, q_wide, g_all, dk_acc, dv_acc, score, prob, tops, acc, table = refs
    scaling = HD ** (-0.5)
    log_scale = scaling * math.log2(math.e)
    f32, bf16 = jnp.float32, jnp.bfloat16

    ctx_index, head_index = lax.axis_index("ctx"), lax.axis_index("head")
    part, core = ctx_index // cores, ctx_index % cores

    def rows_of(head_flip, core_flip, part_flip):
        tile = (part ^ part_flip) * cores + (core ^ core_flip)
        return pl.ds(pl.multiple_of((tile * heads + (head_index ^ head_flip)) * tok, tok), tok)

    for chunk_number, chunk in enumerate(CHUNKS):
        for number in range(heads * cores):
            kv_ref = kv_refs[chunk_number * heads * cores + number]
            for place, flip in enumerate(chunk):
                rows = rows_of(number // cores, number % cores, flip)
                k_all[rows, :] = kv_ref[place, :, :HD]
                v_all[rows, :] = kv_ref[place, :, HD:]
    feature = lax.broadcasted_iota(jnp.int32, (tok, MARKS), 1)
    for flip, qd_ref in enumerate(qd_refs):
        own_marks = marks_ref[rows_of(0, 0, flip), :].astype(f32)
        bias = jnp.where(feature < docs, (1.0 - own_marks) * HIDDEN, 0.0).astype(bf16)
        for member in range(group):
            rows = slice(member * tok, (member + 1) * tok)
            q_wide[flip, rows, :HD] = qd_ref[:, member * HD : (member + 1) * HD]
            q_wide[flip, rows, HD:] = bias
            g_all[flip, rows, :] = qd_ref[:, (group + member) * HD : (group + member + 1) * HD]
    dk_acc[...] = jnp.zeros_like(dk_acc)
    dv_acc[...] = jnp.zeros_like(dv_acc)
    tops[...] = jnp.full_like(tops, NEG_FILL)
    acc[...] = jnp.zeros_like(acc)

    def entry(number, flip, row, limit):
        table[0, number] = flip
        table[1, number] = row
        table[2, number] = limit

    total = jnp.int32(0)
    for flip in range(KVH):
        first = ((part ^ flip) * cores + core) * tile_rows + head_index * tok
        end, low = jnp.int32(0), jnp.int32(0)
        for number in range(docs):
            length = lengths_ref[number]
            end = end + length
            low = low + jnp.where(end <= first, length, 0)
        count = (first + tok - low // tok * tok + KEY_ROWS - 1) // KEY_ROWS
        begin = jnp.maximum(first + tok - count * KEY_ROWS, 0)

        def listed(step, _, flip=flip, first=first, begin=begin, total=total):
            row = begin + step * KEY_ROWS
            entry(total + step, flip, row, first - row)
            return 0

        lax.fori_loop(0, count, listed, 0)
        total = total + count
    for spare in range(BATCH - 1):
        entry(total + spare, 0, 0, -(1 << 20))
    rounds = (total + BATCH - 1) // BATCH

    def sweep(body, batch):
        def one_round(number, _):
            body([number * batch + place for place in range(batch)])
            return 0

        lax.fori_loop(0, rounds * (BATCH // batch), one_round, 0)

    def key_rows(item):
        return pl.ds(pl.multiple_of(table[1, item], tok), KEY_ROWS)

    def score_rows(item):
        return pl.ds(pl.multiple_of(item * KEY_ROWS, KEY_ROWS), KEY_ROWS)

    def wide(ref, rows):
        return jnp.concatenate([ref[rows, :], marks_ref[rows, :]], axis=1)

    key_row = lax.broadcasted_iota(jnp.int32, (KEY_ROWS, lanes), 0)
    query_row = lax.broadcasted_iota(jnp.int32, (1, lanes), 1) % tok

    def scores_round(items):
        raws = [
            lax.dot_general(
                wide(k_all, key_rows(item)),
                q_wide[table[0, item]],
                CONTRACT_LAST,
                preferred_element_type=f32,
            )
            for item in items
        ]
        for item, raw in zip(items, raws):
            raw = jnp.where(key_row <= query_row + table[2, item], raw, NEG_FILL)
            score[score_rows(item), :] = raw
            flip = table[0, item]
            tops[flip] = jnp.maximum(
                tops[flip], jnp.max(raw.reshape(KEY_ROWS // 8, 8, lanes), axis=0)
            )

    sweep(scores_round, BATCH)
    for flip in range(KVH):
        tops[flip] = jnp.broadcast_to(jnp.max(tops[flip], axis=0, keepdims=True), (8, lanes))

    ones = jnp.ones((acc.shape[1] - HD, KEY_ROWS), bf16)

    def out_round(items):
        weights = [
            jnp.exp2((score[score_rows(item), :] - tops[table[0, item], :1]) * log_scale).astype(bf16)
            for item in items
        ]
        for item, weight in zip(items, weights):
            prob[score_rows(item), :] = weight
        parts = [
            jnp.dot(
                jnp.concatenate([v_all[key_rows(item), :].T, ones], axis=0),
                weight,
                preferred_element_type=f32,
            )
            for item, weight in zip(items, weights)
        ]
        for item, value in zip(items, parts):
            acc[table[0, item]] += value

    sweep(out_round, BATCH)
    for flip in range(KVH):
        inverse = 1.0 / acc[flip, HD : HD + 1, :]
        turned = (acc[flip, :HD, :] * inverse).astype(bf16)
        out = turned.T
        g_turned = g_all[flip].T.astype(f32)
        delta = jnp.sum(turned.astype(f32) * g_turned, axis=0, keepdims=True)
        acc[flip, HD : HD + 1, :] = inverse
        acc[flip, HD + 1 : HD + 2, :] = delta
        acc[flip, :HD, :] = jnp.zeros((HD, lanes), f32)
        for member in range(group):
            rows = slice(member * tok, (member + 1) * tok)
            od_refs[flip][:, member * HD : (member + 1) * HD] = out[rows, :]

    def grad_round(items):
        slopes = [
            lax.dot_general(
                v_all[key_rows(item), :],
                g_all[table[0, item]],
                CONTRACT_LAST,
                preferred_element_type=f32,
            )
            for item in items
        ]
        probs = [
            prob[score_rows(item), :].astype(f32) * acc[table[0, item], HD : HD + 1, :]
            for item in items
        ]
        weights = [value.astype(bf16) for value in probs]
        score_grads = [
            (value * (slope - acc[table[0, item], HD + 1 : HD + 2, :])).astype(bf16)
            for item, value, slope in zip(items, probs, slopes)
        ]
        for item, weight, score_grad in zip(items, weights, score_grads):
            flip, rows = table[0, item], key_rows(item)
            dv_acc[rows, :] += jnp.dot(weight, g_all[flip], preferred_element_type=f32)
            dk_acc[rows, :] += jnp.dot(score_grad, q_wide[flip, :, :HD], preferred_element_type=f32)
            acc[flip, :HD, :] += lax.dot_general(
                k_all[rows, :], score_grad, CONTRACT_FIRST, preferred_element_type=f32
            )

    sweep(grad_round, GRAD_BATCH)

    for flip, od_ref in enumerate(od_refs):
        turned = (acc[flip, :HD, :] * scaling).astype(bf16).T
        for member in range(group):
            rows = slice(member * tok, (member + 1) * tok)
            od_ref[:, (group + member) * HD : (group + member + 1) * HD] = turned[rows, :]
    for chunk_number, chunk in enumerate(CHUNKS):
        for core_flip in range(cores):
            dkv_ref = dkv_refs[chunk_number * cores + core_flip]
            for head_flip in range(heads):
                for place, flip in enumerate(chunk):
                    rows = rows_of(head_flip, core_flip, flip)
                    dkv_ref[head_flip, place, :, :HD] = (dk_acc[rows, :] * scaling).astype(bf16)
                    dkv_ref[head_flip, place, :, HD:] = dv_acc[rows, :].astype(bf16)


def attention(lengths, marks, qd, kv, cores, heads):
    tok, group = qd[0].shape[0], QH // KVH
    total = KVH * cores * heads * tok
    lanes = group * tok
    reach = REACH * heads * tok
    pair = sum(-(-(keys + tok) // KEY_ROWS) for keys in (reach, reach // 2))
    items = -(-KVH // 2 * pair // BATCH) * BATCH
    bf16, f32 = jnp.bfloat16, jnp.float32
    results = pl.pallas_call(
        functools.partial(attention_kernel, cores, heads, tok),
        out_shape=[jax.ShapeDtypeStruct(a.shape, a.dtype) for a in qd]
        + [
            jax.ShapeDtypeStruct((heads, len(chunk), tok, 2 * HD), bf16)
            for chunk in CHUNKS
            for _ in range(cores)
        ],
        in_specs=[SMEM] + [VMEM] * (1 + len(qd) + len(kv)),
        out_specs=[VMEM] * (len(qd) + cores * len(CHUNKS)),
        scratch_shapes=[
            pltpu.VMEM((total, HD), bf16),
            pltpu.VMEM((total, HD), bf16),
            pltpu.VMEM((KVH, lanes, HD + MARKS), bf16),
            pltpu.VMEM((KVH, lanes, HD), bf16),
            pltpu.VMEM((total, HD), f32),
            pltpu.VMEM((total, HD), f32),
            pltpu.VMEM((items * KEY_ROWS, lanes), f32),
            pltpu.VMEM((items * KEY_ROWS, lanes), bf16),
            pltpu.VMEM((KVH, 8, lanes), f32),
            pltpu.VMEM((KVH, HD + 16, lanes), f32),
            pltpu.SMEM((3, items + BATCH), jnp.int32),
        ],
        compiler_params=pltpu.CompilerParams(vmem_limit_bytes=36 * 1024 * 1024),
    )(lengths, marks, *qd, *kv)
    return results[: len(qd)], results[len(qd) :]


def part_shards(queries, keys, values, d_out, lengths):
    heads, ctx = lax.axis_size("head"), lax.axis_size("ctx")
    cores = ctx // KVH
    total = queries.shape[0] * heads * ctx

    def exchange(pieces):
        span = ctx // len(pieces)
        return [pieces[0]] + [flipped(p, "ctx", (s + 1) * span) for s, p in enumerate(pieces[1:])]

    kv_mine = jnp.stack(exchange(split_heads(keys, values, KVH)))
    qd, marks = prepare(lengths, queries, d_out, KVH, total)
    qd = exchange(qd)
    near, far = flipped(kv_mine, "head", 1), flipped(kv_mine, "head", 2)
    kv = []
    for piece in (kv_mine, near, far, flipped(far, "head", 1)):
        kv += [piece, flipped(piece, "ctx", 1)]
    od, dkv = attention(lengths, marks, qd, kv, cores, heads)

    def summed(*terms):
        return sum(term.astype(jnp.float32) for term in terms).astype(jnp.bfloat16)

    both = (dkv[0], flipped(dkv[1], "ctx", 1))
    third = flipped(summed(*(term[3] for term in both)), "head", 1)
    second = flipped(summed(*(term[2] for term in both), third), "head", 2)
    first, _ = lax.optimization_barrier((summed(*(term[1] for term in both)), third))
    first = flipped(first, "head", 1)
    grads = [summed(*(term[0, s] for term in both), first[s], second[s]) for s in range(KVH)]
    attn_out, grad_queries = join_heads(exchange(od))
    grad_keys, grad_values = join_heads(exchange(grads))
    return attn_out, grad_queries, grad_keys, grad_values


def solution(mesh):
    ctx_dev, head_dev = mesh.shape["ctx"], mesh.shape["head"]
    local = part_shards if ctx_dev == 2 * KVH and head_dev == 4 else shards
    rows = P(("ctx", "head"), None)
    return jax.shard_map(
        local,
        mesh=mesh,
        in_specs=(rows, rows, rows, rows, P()),
        out_specs=(rows, rows, rows, rows),
        check_vma=False,
    )
```

```python
import functools
import math

import jax
import jax.numpy as jnp
from jax import lax
from jax.experimental import pallas as pl
from jax.experimental.pallas import tpu as pltpu
from jax.sharding import PartitionSpec as P

QH = 16
KVH = 4
HD = 128
REACH = 4


NEG_FILL = -1e30


def shifted(value, axis, steps):
    count = lax.axis_size(axis)
    first, last = (max(0, -steps), min(count, count - steps))
    return lax.ppermute(value, axis, [(source, source + steps) for source in range(first, last)])


def doc_starts(lengths, first, count):
    doc_ends = jnp.cumsum(lengths)
    positions = first + jnp.arange(count, dtype=jnp.int32)
    passed = doc_ends[None, :] <= positions[:, None]
    return jnp.sum(jnp.where(passed, lengths[None, :], 0), axis=1)


def visible_pairs(query_first, key_first, start_rows, block_rows):
    query_pos = query_first + jnp.arange(block_rows, dtype=jnp.int32)
    key_pos = key_first + jnp.arange(block_rows, dtype=jnp.int32)
    mask = (key_pos[None, :] <= query_pos[:, None]) & (key_pos[None, :] >= start_rows[:, None])
    return mask[:, None, None, :]


def block_live(query_first, key_first, tile_starts, tile_first, block_rows):
    lowest = jnp.maximum(query_first, key_first)
    picked = jnp.clip(lowest - tile_first, 0, tile_starts.shape[0] - 1)
    first_start = lax.dynamic_index_in_dim(tile_starts, picked, 0, keepdims=False)
    return (lowest <= query_first + block_rows - 1) & (first_start <= key_first + block_rows - 1)


def shards(queries, keys, values, d_out, lengths):
    heads_dev = lax.axis_size("head")
    tok_dev = queries.shape[0]
    copies = max(1, heads_dev // KVH)
    kv_local = max(1, KVH // heads_dev)
    q_local = QH // heads_dev
    group_size = q_local // kv_local
    scaling = HD ** (-0.5)

    def spread(array_in):
        if copies > 1:
            return jnp.repeat(array_in.reshape(tok_dev, KVH, HD), copies, axis=1).reshape(
                tok_dev, KVH * copies * HD
            )
        return array_in

    q_tile, k_tile, v_tile = (
        lax.all_to_all(queries, "head", split_axis=1, concat_axis=0, tiled=True),
        lax.all_to_all(spread(keys), "head", split_axis=1, concat_axis=0, tiled=True),
        lax.all_to_all(spread(values), "head", split_axis=1, concat_axis=0, tiled=True),
    )
    tile_rows = q_tile.shape[0]
    block_rows = min(1024, tile_rows)
    block_count = tile_rows // block_rows
    ctx_index = lax.axis_index("ctx")
    tile_first = ctx_index * tile_rows
    tile_starts = doc_starts(lengths, tile_first, tile_rows)
    query_blocks = [
        q_tile[number * block_rows : (number + 1) * block_rows].reshape(
            block_rows, kv_local, group_size, HD
        )
        for number in range(block_count)
    ]
    start_blocks = [
        tile_starts[number * block_rows : (number + 1) * block_rows]
        for number in range(block_count)
    ]
    query_firsts = [tile_first + number * block_rows for number in range(block_count)]
    key_pair = jnp.stack([k_tile, v_tile])
    key_tiles = [key_pair]
    moving = key_pair
    for offset in range(1, REACH + 1):
        moving = shifted(moving, "ctx", 1)
        key_tiles.append(moving)

    def split_keys(tile_pair):
        key_list = [
            tile_pair[0, number * block_rows : (number + 1) * block_rows].reshape(
                block_rows, kv_local, HD
            )
            for number in range(block_count)
        ]
        value_list = [
            tile_pair[1, number * block_rows : (number + 1) * block_rows].reshape(
                block_rows, kv_local, HD
            )
            for number in range(block_count)
        ]
        return (key_list, value_list)

    states = [
        (
            jnp.full((block_rows, kv_local, group_size), NEG_FILL, jnp.float32),
            jnp.zeros((block_rows, kv_local, group_size), jnp.float32),
            jnp.zeros((block_rows, kv_local, group_size, HD), jnp.float32),
        )
        for number in range(block_count)
    ]
    for offset in range(REACH + 1):
        key_list, value_list = split_keys(key_tiles[offset])
        key_start = (ctx_index - offset) * tile_rows
        for query_number in range(block_count):
            query_block = query_blocks[query_number]
            query_first = query_firsts[query_number]
            start_rows = start_blocks[query_number]
            for key_number in range(block_count):
                key_block = key_list[key_number]
                value_block = value_list[key_number]
                key_first = key_start + key_number * block_rows

                def forward_block(
                    current,
                    query_block=query_block,
                    query_first=query_first,
                    start_rows=start_rows,
                    key_block=key_block,
                    value_block=value_block,
                    key_first=key_first,
                ):
                    max_old, sum_old, acc_old = current
                    mask = visible_pairs(query_first, key_first, start_rows, block_rows)
                    scores = (
                        jnp.einsum(
                            "qkgd,ckd->qkgc",
                            query_block,
                            key_block,
                            preferred_element_type=jnp.float32,
                        )
                        * scaling
                    )
                    scores = jnp.where(mask, scores, NEG_FILL)
                    max_new = jnp.maximum(max_old, jnp.max(scores, axis=-1))
                    prob_raw = jnp.where(mask, jnp.exp(scores - max_new[..., None]), 0.0)
                    rescale = jnp.exp(max_old - max_new)
                    sum_new = sum_old * rescale + jnp.sum(prob_raw, axis=-1)
                    acc_new = acc_old * rescale[..., None] + jnp.einsum(
                        "qkgc,ckd->qkgd",
                        prob_raw.astype(jnp.bfloat16),
                        value_block,
                        preferred_element_type=jnp.float32,
                    )
                    return (max_new, sum_new, acc_new)

                live = block_live(query_first, key_first, tile_starts, tile_first, block_rows)
                states[query_number] = lax.cond(
                    live, forward_block, lambda unchanged: unchanged, states[query_number]
                )
    out_blocks = [(state[2] / state[1][..., None]).astype(jnp.bfloat16) for state in states]
    lse_blocks = [state[0] + jnp.log(state[1]) for state in states]
    grad_tile = lax.all_to_all(d_out, "head", split_axis=1, concat_axis=0, tiled=True)
    grad_blocks = [
        grad_tile[number * block_rows : (number + 1) * block_rows].reshape(
            block_rows, kv_local, group_size, HD
        )
        for number in range(block_count)
    ]
    delta_blocks = [
        jnp.sum(
            grad_blocks[number].astype(jnp.float32) * out_blocks[number].astype(jnp.float32),
            axis=-1,
        )
        for number in range(block_count)
    ]
    query_totals = [
        jnp.zeros((block_rows, kv_local, group_size, HD), jnp.float32)
        for number in range(block_count)
    ]
    partial_grads = []
    for offset in range(REACH + 1):
        key_list, value_list = split_keys(key_tiles[offset])
        key_start = (ctx_index - offset) * tile_rows
        key_sums = [
            jnp.zeros((block_rows, kv_local, HD), jnp.float32) for number in range(block_count)
        ]
        value_sums = [
            jnp.zeros((block_rows, kv_local, HD), jnp.float32) for number in range(block_count)
        ]
        for query_number in range(block_count):
            query_block = query_blocks[query_number]
            grad_block = grad_blocks[query_number]
            query_first = query_firsts[query_number]
            start_rows = start_blocks[query_number]
            lse_rows = lse_blocks[query_number]
            delta_rows = delta_blocks[query_number]
            for key_number in range(block_count):
                key_block = key_list[key_number]
                value_block = value_list[key_number]
                key_first = key_start + key_number * block_rows

                def backward_block(
                    current,
                    query_block=query_block,
                    grad_block=grad_block,
                    query_first=query_first,
                    start_rows=start_rows,
                    lse_rows=lse_rows,
                    delta_rows=delta_rows,
                    key_block=key_block,
                    value_block=value_block,
                    key_first=key_first,
                ):
                    query_grad, key_grad, value_grad = current
                    mask = visible_pairs(query_first, key_first, start_rows, block_rows)
                    scores = (
                        jnp.einsum(
                            "qkgd,ckd->qkgc",
                            query_block,
                            key_block,
                            preferred_element_type=jnp.float32,
                        )
                        * scaling
                    )
                    prob_raw = jnp.where(mask, jnp.exp(scores - lse_rows[..., None]), 0.0)
                    weights = prob_raw.astype(jnp.bfloat16)
                    value_grad = value_grad + jnp.einsum(
                        "qkgc,qkgd->ckd", weights, grad_block, preferred_element_type=jnp.float32
                    )
                    prob_grad = jnp.einsum(
                        "qkgd,ckd->qkgc",
                        grad_block,
                        value_block,
                        preferred_element_type=jnp.float32,
                    )
                    score_grad = (prob_raw * (prob_grad - delta_rows[..., None]) * scaling).astype(
                        jnp.bfloat16
                    )
                    query_grad = query_grad + jnp.einsum(
                        "qkgc,ckd->qkgd", score_grad, key_block, preferred_element_type=jnp.float32
                    )
                    key_grad = key_grad + jnp.einsum(
                        "qkgc,qkgd->ckd",
                        score_grad,
                        query_block,
                        preferred_element_type=jnp.float32,
                    )
                    return (query_grad, key_grad, value_grad)

                live = block_live(query_first, key_first, tile_starts, tile_first, block_rows)
                current = (query_totals[query_number], key_sums[key_number], value_sums[key_number])
                query_totals[query_number], key_sums[key_number], value_sums[key_number] = lax.cond(
                    live, backward_block, lambda unchanged: unchanged, current
                )
        key_whole = jnp.concatenate(key_sums, axis=0).reshape(tile_rows, kv_local * HD)
        value_whole = jnp.concatenate(value_sums, axis=0).reshape(tile_rows, kv_local * HD)
        partial_grads.append(jnp.stack([key_whole, value_whole]))
    grad_total = partial_grads[REACH]
    for offset in range(REACH - 1, -1, -1):
        grad_total = (
            shifted(grad_total.astype(jnp.bfloat16), "ctx", -1).astype(grad_total.dtype)
            + partial_grads[offset]
        )
    out_tile = jnp.concatenate(out_blocks, axis=0).reshape(tile_rows, q_local * HD)
    query_tile = (
        jnp.concatenate(query_totals, axis=0).reshape(tile_rows, q_local * HD).astype(jnp.bfloat16)
    )
    attn_out, grad_queries = (
        lax.all_to_all(out_tile, "head", split_axis=0, concat_axis=1, tiled=True),
        lax.all_to_all(query_tile, "head", split_axis=0, concat_axis=1, tiled=True),
    )
    token_grads = lax.all_to_all(
        grad_total.astype(jnp.bfloat16), "head", split_axis=1, concat_axis=2, tiled=True
    ).astype(grad_total.dtype)
    if copies > 1:
        token_grads = jnp.sum(token_grads.reshape(2, tok_dev, KVH, copies, HD), axis=3).reshape(
            2, tok_dev, KVH * HD
        )
    token_grads = token_grads.astype(jnp.bfloat16)
    return (attn_out, grad_queries, token_grads[0], token_grads[1])


CHUNKS = ((0, 1, 2, 3),)
CONTRACT_LAST = (((1,), (1,)), ((), ()))
CONTRACT_FIRST = (((0,), (0,)), ((), ()))
VMEM = pl.BlockSpec(memory_space=pltpu.VMEM)
SMEM = pl.BlockSpec(memory_space=pltpu.SMEM)
SMALL = pltpu.CompilerParams(vmem_limit_bytes=8 * 1024 * 1024)


def flipped(value, ctx_bits, head_bits):
    ctx, heads = lax.axis_size("ctx"), lax.axis_size("head")
    pairs = [
        (c * heads + h, (c ^ ctx_bits) * heads + (h ^ head_bits))
        for c in range(ctx)
        for h in range(heads)
    ]
    return lax.ppermute(value, ("ctx", "head"), pairs)


def piece_columns(pieces, flip, wide):
    index = lax.axis_index("ctx") // (lax.axis_size("ctx") // pieces)
    return pl.ds(pl.multiple_of((index ^ flip) * wide, HD), wide)


def split_heads_kernel(pieces, wide, left_ref, right_ref, *piece_refs):
    for flip, piece_ref in enumerate(piece_refs):
        columns = piece_columns(pieces, flip, wide)
        piece_ref[:, :wide] = left_ref[:, columns]
        piece_ref[:, wide:] = right_ref[:, columns]


def join_heads_kernel(pieces, wide, *refs):
    piece_refs, (left_ref, right_ref) = refs[:pieces], refs[pieces:]
    for flip, piece_ref in enumerate(piece_refs):
        columns = piece_columns(pieces, flip, wide)
        left_ref[:, columns] = piece_ref[:, :wide]
        right_ref[:, columns] = piece_ref[:, wide:]


def split_heads(left, right, pieces):
    rows, wide = left.shape[0], left.shape[1] // pieces
    return pl.pallas_call(
        functools.partial(split_heads_kernel, pieces, wide),
        out_shape=[jax.ShapeDtypeStruct((rows, 2 * wide), left.dtype)] * pieces,
        in_specs=[VMEM] * 2,
        out_specs=[VMEM] * pieces,
        compiler_params=SMALL,
    )(left, right)


def join_heads(parts):
    pieces = len(parts)
    rows, wide = parts[0].shape[0], parts[0].shape[1] // 2
    return pl.pallas_call(
        functools.partial(join_heads_kernel, pieces, wide),
        out_shape=[jax.ShapeDtypeStruct((rows, wide * pieces), parts[0].dtype)] * 2,
        in_specs=[VMEM] * pieces,
        out_specs=[VMEM] * 2,
        compiler_params=SMALL,
    )(*parts)


def prepare_kernel(pieces, wide, lengths_ref, left_ref, right_ref, *out_refs):
    piece_refs, marks_ref = out_refs[:pieces], out_refs[pieces]
    split_heads_kernel(pieces, wide, left_ref, right_ref, *piece_refs)
    total, docs = marks_ref.shape[0], lengths_ref.shape[0]
    lane = lax.broadcasted_iota(jnp.int32, (1, MARKS), 1)
    begins = jnp.zeros((1, MARKS), jnp.int32)
    ends = jnp.where(lane < docs, total, 0)
    end = jnp.int32(0)
    for number in range(docs):
        begins = jnp.where(lane == number, end, begins)
        end = end + lengths_ref[number]
        ends = jnp.where(lane == number, end, ends)

    def some_rows(step, _):
        rows = pl.ds(pl.multiple_of(step * KEY_ROWS, KEY_ROWS), KEY_ROWS)
        position = step * KEY_ROWS + lax.broadcasted_iota(jnp.int32, (KEY_ROWS, MARKS), 0)
        inside = (position >= begins) & (position < ends)
        marks_ref[rows, :] = jnp.where(inside, 1.0, 0.0).astype(jnp.bfloat16)
        return 0

    lax.fori_loop(0, total // KEY_ROWS, some_rows, 0)


def prepare(lengths, left, right, pieces, total):
    rows, wide = left.shape[0], left.shape[1] // pieces
    results = pl.pallas_call(
        functools.partial(prepare_kernel, pieces, wide),
        out_shape=[jax.ShapeDtypeStruct((rows, 2 * wide), left.dtype)] * pieces
        + [jax.ShapeDtypeStruct((total, MARKS), jnp.bfloat16)],
        in_specs=[SMEM] + [VMEM] * 2,
        out_specs=[VMEM] * (pieces + 1),
        compiler_params=SMALL,
    )(lengths, left, right)
    return results[:pieces], results[pieces]


KEY_ROWS = 256
BATCH = 4
MARKS = 128
HIDDEN = -(2.0**100)


def attention_kernel(cores, heads, tok, *refs):
    group = QH // KVH
    lanes = group * tok
    tile_rows = heads * tok
    kv_count = heads * cores * len(CHUNKS)
    lengths_ref, marks_ref, refs = refs[0], refs[1], refs[2:]
    docs = lengths_ref.shape[0]
    qd_refs, refs = refs[:KVH], refs[KVH:]
    kv_refs, refs = refs[:kv_count], refs[kv_count:]
    od_refs, refs = refs[:KVH], refs[KVH:]
    dkv_refs, refs = refs[: cores * len(CHUNKS)], refs[cores * len(CHUNKS) :]
    k_all, v_all, q_wide, g_all, dk_acc, dv_acc, score, prob, tops, acc, table = refs
    scaling = HD ** (-0.5)
    log_scale = scaling * math.log2(math.e)
    f32, bf16 = jnp.float32, jnp.bfloat16

    ctx_index, head_index = lax.axis_index("ctx"), lax.axis_index("head")
    part, core = ctx_index // cores, ctx_index % cores

    def rows_of(head_flip, core_flip, part_flip):
        tile = (part ^ part_flip) * cores + (core ^ core_flip)
        return pl.ds(pl.multiple_of((tile * heads + (head_index ^ head_flip)) * tok, tok), tok)

    for chunk_number, chunk in enumerate(CHUNKS):
        for number in range(heads * cores):
            kv_ref = kv_refs[chunk_number * heads * cores + number]
            for place, flip in enumerate(chunk):
                rows = rows_of(number // cores, number % cores, flip)
                k_all[rows, :] = kv_ref[place, :, :HD]
                v_all[rows, :] = kv_ref[place, :, HD:]
    feature = lax.broadcasted_iota(jnp.int32, (tok, MARKS), 1)
    for flip, qd_ref in enumerate(qd_refs):
        own_marks = marks_ref[rows_of(0, 0, flip), :].astype(f32)
        bias = jnp.where(feature < docs, (1.0 - own_marks) * HIDDEN, 0.0).astype(bf16)
        for member in range(group):
            rows = slice(member * tok, (member + 1) * tok)
            q_wide[flip, rows, :HD] = qd_ref[:, member * HD : (member + 1) * HD]
            q_wide[flip, rows, HD:] = bias
            g_all[flip, rows, :] = qd_ref[:, (group + member) * HD : (group + member + 1) * HD]
    dk_acc[...] = jnp.zeros_like(dk_acc)
    dv_acc[...] = jnp.zeros_like(dv_acc)
    tops[...] = jnp.full_like(tops, NEG_FILL)
    acc[...] = jnp.zeros_like(acc)

    def entry(number, flip, row, limit):
        table[0, number] = flip
        table[1, number] = row
        table[2, number] = limit

    total = jnp.int32(0)
    for flip in range(KVH):
        first = ((part ^ flip) * cores + core) * tile_rows + head_index * tok
        end, low = jnp.int32(0), jnp.int32(0)
        for number in range(docs):
            length = lengths_ref[number]
            end = end + length
            low = low + jnp.where(end <= first, length, 0)
        count = (first + tok - low // tok * tok + KEY_ROWS - 1) // KEY_ROWS
        begin = jnp.maximum(first + tok - count * KEY_ROWS, 0)

        def listed(step, _, flip=flip, first=first, begin=begin, total=total):
            row = begin + step * KEY_ROWS
            entry(total + step, flip, row, first - row)
            return 0

        lax.fori_loop(0, count, listed, 0)
        total = total + count
    for spare in range(BATCH - 1):
        entry(total + spare, 0, 0, -(1 << 20))
    rounds = (total + 1) // BATCH
    left_over = (total - rounds * BATCH + 1) // 2

    def sweep(body):
        def one_round(number, _):
            body([number * BATCH + place for place in range(BATCH)])
            return 0

        def one_pair(number, _):
            body([rounds * BATCH + number * 2 + place for place in range(2)])
            return 0

        lax.fori_loop(0, rounds, one_round, 0)
        lax.fori_loop(0, left_over, one_pair, 0)

    def key_rows(item):
        return pl.ds(pl.multiple_of(table[1, item], tok), KEY_ROWS)

    def score_rows(item):
        return pl.ds(pl.multiple_of(item * KEY_ROWS, KEY_ROWS), KEY_ROWS)

    def wide(ref, rows):
        return jnp.concatenate([ref[rows, :], marks_ref[rows, :]], axis=1)

    key_row = lax.broadcasted_iota(jnp.int32, (KEY_ROWS, lanes), 0)
    query_row = lax.broadcasted_iota(jnp.int32, (1, lanes), 1) % tok

    def scores_round(items):
        raws = [
            lax.dot_general(
                wide(k_all, key_rows(item)),
                q_wide[table[0, item]],
                CONTRACT_LAST,
                preferred_element_type=f32,
            )
            for item in items
        ]
        for item, raw in zip(items, raws):
            raw = jnp.where(key_row <= query_row + table[2, item], raw, NEG_FILL)
            score[score_rows(item), :] = raw
            flip = table[0, item]
            tops[flip] = jnp.maximum(
                tops[flip], jnp.max(raw.reshape(KEY_ROWS // 8, 8, lanes), axis=0)
            )

    sweep(scores_round)
    for flip in range(KVH):
        tops[flip] = jnp.broadcast_to(jnp.max(tops[flip], axis=0, keepdims=True), (8, lanes))

    ones = jnp.ones((acc.shape[1] - HD, KEY_ROWS), bf16)

    def out_round(items):
        weights = [
            jnp.exp2((score[score_rows(item), :] - tops[table[0, item], :1]) * log_scale).astype(bf16)
            for item in items
        ]
        for item, weight in zip(items, weights):
            prob[score_rows(item), :] = weight
        parts = [
            jnp.dot(
                jnp.concatenate([v_all[key_rows(item), :].T, ones], axis=0),
                weight,
                preferred_element_type=f32,
            )
            for item, weight in zip(items, weights)
        ]
        for item, value in zip(items, parts):
            acc[table[0, item]] += value

    sweep(out_round)
    for flip in range(KVH):
        inverse = 1.0 / acc[flip, HD : HD + 1, :]
        turned = (acc[flip, :HD, :] * inverse).astype(bf16)
        out = turned.T
        g_turned = g_all[flip].T.astype(f32)
        delta = jnp.sum(turned.astype(f32) * g_turned, axis=0, keepdims=True)
        acc[flip, HD : HD + 1, :] = inverse
        acc[flip, HD + 1 : HD + 2, :] = delta
        acc[flip, :HD, :] = jnp.zeros((HD, lanes), f32)
        for member in range(group):
            rows = slice(member * tok, (member + 1) * tok)
            od_refs[flip][:, member * HD : (member + 1) * HD] = out[rows, :]

    def grad_round(items):
        slopes = [
            lax.dot_general(
                v_all[key_rows(item), :],
                g_all[table[0, item]],
                CONTRACT_LAST,
                preferred_element_type=f32,
            )
            for item in items
        ]
        probs = [
            prob[score_rows(item), :].astype(f32) * acc[table[0, item], HD : HD + 1, :]
            for item in items
        ]
        weights = [value.astype(bf16) for value in probs]
        score_grads = [
            (value * (slope - acc[table[0, item], HD + 1 : HD + 2, :])).astype(bf16)
            for item, value, slope in zip(items, probs, slopes)
        ]
        for item, weight, score_grad in zip(items, weights, score_grads):
            flip, rows = table[0, item], key_rows(item)
            dv_acc[rows, :] += jnp.dot(weight, g_all[flip], preferred_element_type=f32)
            dk_acc[rows, :] += jnp.dot(score_grad, q_wide[flip, :, :HD], preferred_element_type=f32)
            acc[flip, :HD, :] += lax.dot_general(
                k_all[rows, :], score_grad, CONTRACT_FIRST, preferred_element_type=f32
            )

    sweep(grad_round)

    for flip, od_ref in enumerate(od_refs):
        turned = (acc[flip, :HD, :] * scaling).astype(bf16).T
        for member in range(group):
            rows = slice(member * tok, (member + 1) * tok)
            od_ref[:, (group + member) * HD : (group + member + 1) * HD] = turned[rows, :]
    for chunk_number, chunk in enumerate(CHUNKS):
        for core_flip in range(cores):
            dkv_ref = dkv_refs[chunk_number * cores + core_flip]
            for head_flip in range(heads):
                for place, flip in enumerate(chunk):
                    rows = rows_of(head_flip, core_flip, flip)
                    dkv_ref[head_flip, place, :, :HD] = (dk_acc[rows, :] * scaling).astype(bf16)
                    dkv_ref[head_flip, place, :, HD:] = dv_acc[rows, :].astype(bf16)


def attention(lengths, marks, qd, kv, cores, heads):
    tok, group = qd[0].shape[0], QH // KVH
    total = KVH * cores * heads * tok
    lanes = group * tok
    reach = REACH * heads * tok
    pair = sum(-(-(keys + tok) // KEY_ROWS) for keys in (reach, reach // 2))
    items = -(-KVH // 2 * pair // BATCH) * BATCH
    bf16, f32 = jnp.bfloat16, jnp.float32
    results = pl.pallas_call(
        functools.partial(attention_kernel, cores, heads, tok),
        out_shape=[jax.ShapeDtypeStruct(a.shape, a.dtype) for a in qd]
        + [
            jax.ShapeDtypeStruct((heads, len(chunk), tok, 2 * HD), bf16)
            for chunk in CHUNKS
            for _ in range(cores)
        ],
        in_specs=[SMEM] + [VMEM] * (1 + len(qd) + len(kv)),
        out_specs=[VMEM] * (len(qd) + cores * len(CHUNKS)),
        scratch_shapes=[
            pltpu.VMEM((total, HD), bf16),
            pltpu.VMEM((total, HD), bf16),
            pltpu.VMEM((KVH, lanes, HD + MARKS), bf16),
            pltpu.VMEM((KVH, lanes, HD), bf16),
            pltpu.VMEM((total, HD), f32),
            pltpu.VMEM((total, HD), f32),
            pltpu.VMEM((items * KEY_ROWS, lanes), f32),
            pltpu.VMEM((items * KEY_ROWS, lanes), bf16),
            pltpu.VMEM((KVH, 8, lanes), f32),
            pltpu.VMEM((KVH, HD + 16, lanes), f32),
            pltpu.SMEM((3, items + BATCH), jnp.int32),
        ],
        compiler_params=pltpu.CompilerParams(vmem_limit_bytes=36 * 1024 * 1024),
    )(lengths, marks, *qd, *kv)
    return results[: len(qd)], results[len(qd) :]


def part_shards(queries, keys, values, d_out, lengths):
    heads, ctx = lax.axis_size("head"), lax.axis_size("ctx")
    cores = ctx // KVH
    total = queries.shape[0] * heads * ctx
    together = lax.optimization_barrier

    def over_part(piece, flip):
        return flipped(piece, flip * cores, 0)

    def exchange(pieces):
        return [pieces[0]] + [over_part(piece, s + 1) for s, piece in enumerate(pieces[1:])]

    def summed(*terms):
        return sum(term.astype(jnp.float32) for term in terms).astype(jnp.bfloat16)

    kv_pieces = split_heads(keys, values, KVH)
    far_own = flipped(kv_pieces[0][None], 0, 2)
    kv_pieces = exchange(kv_pieces)
    kv_mine = jnp.stack(kv_pieces)
    far_rest = flipped(jnp.stack(kv_pieces[1:]), 0, 2)
    far = jnp.concatenate([far_own, far_rest])
    qd, marks = prepare(lengths, queries, d_out, KVH, total)
    qd = exchange(qd)
    near = flipped(kv_mine, 0, 1)
    kv = []
    for piece in (kv_mine, near, far, flipped(far, 0, 1)):
        kv += [piece, flipped(piece, 1, 0)]
    od, dkv = attention(lengths, marks, qd, kv, cores, heads)

    both = (dkv[0], flipped(dkv[1], 1, 0))
    third = flipped(summed(*(term[3] for term in both)), 0, 1)
    first, _ = together((summed(*(term[1] for term in both)), third))
    first, rest, od_moved = together(
        (
            flipped(first, 0, 1),
            flipped(summed(*(term[2, 1:] for term in both), third[1:]), 0, 2),
            exchange(od)[1:],
        )
    )
    own, grads = together(
        (
            summed(*(term[2, 0] for term in both), third[0]),
            [summed(*(term[0, s] for term in both), first[s], rest[s - 1]) for s in (1, 2, 3)],
        )
    )
    own = flipped(own, 0, 2)
    grads = [over_part(grad, s + 1) for s, grad in enumerate(grads)]
    attn_out, grad_queries = join_heads([od[0], *od_moved])
    grads = [summed(*(term[0, 0] for term in both), first[0], own), *grads]
    grad_keys, grad_values = join_heads(grads)
    return attn_out, grad_queries, grad_keys, grad_values


def solution(mesh):
    ctx_dev, head_dev = mesh.shape["ctx"], mesh.shape["head"]
    local = part_shards if ctx_dev == 2 * KVH and head_dev == 4 else shards
    rows = P(("ctx", "head"), None)
    return jax.shard_map(
        local,
        mesh=mesh,
        in_specs=(rows, rows, rows, rows, P()),
        out_specs=(rows, rows, rows, rows),
        check_vma=False,
    )
```

```python
import functools
import math

import jax
import jax.numpy as jnp
from jax import lax
from jax.experimental import pallas as pl
from jax.experimental.pallas import tpu as pltpu
from jax.sharding import PartitionSpec as P

QH = 16
KVH = 4
HD = 128
REACH = 4


NEG_FILL = -1e30


def shifted(value, axis, steps):
    count = lax.axis_size(axis)
    first, last = (max(0, -steps), min(count, count - steps))
    return lax.ppermute(value, axis, [(source, source + steps) for source in range(first, last)])


def doc_starts(lengths, first, count):
    doc_ends = jnp.cumsum(lengths)
    positions = first + jnp.arange(count, dtype=jnp.int32)
    passed = doc_ends[None, :] <= positions[:, None]
    return jnp.sum(jnp.where(passed, lengths[None, :], 0), axis=1)


def visible_pairs(query_first, key_first, start_rows, block_rows):
    query_pos = query_first + jnp.arange(block_rows, dtype=jnp.int32)
    key_pos = key_first + jnp.arange(block_rows, dtype=jnp.int32)
    mask = (key_pos[None, :] <= query_pos[:, None]) & (key_pos[None, :] >= start_rows[:, None])
    return mask[:, None, None, :]


def block_live(query_first, key_first, tile_starts, tile_first, block_rows):
    lowest = jnp.maximum(query_first, key_first)
    picked = jnp.clip(lowest - tile_first, 0, tile_starts.shape[0] - 1)
    first_start = lax.dynamic_index_in_dim(tile_starts, picked, 0, keepdims=False)
    return (lowest <= query_first + block_rows - 1) & (first_start <= key_first + block_rows - 1)


def shards(queries, keys, values, d_out, lengths):
    heads_dev = lax.axis_size("head")
    tok_dev = queries.shape[0]
    copies = max(1, heads_dev // KVH)
    kv_local = max(1, KVH // heads_dev)
    q_local = QH // heads_dev
    group_size = q_local // kv_local
    scaling = HD ** (-0.5)

    def spread(array_in):
        if copies > 1:
            return jnp.repeat(array_in.reshape(tok_dev, KVH, HD), copies, axis=1).reshape(
                tok_dev, KVH * copies * HD
            )
        return array_in

    q_tile, k_tile, v_tile = (
        lax.all_to_all(queries, "head", split_axis=1, concat_axis=0, tiled=True),
        lax.all_to_all(spread(keys), "head", split_axis=1, concat_axis=0, tiled=True),
        lax.all_to_all(spread(values), "head", split_axis=1, concat_axis=0, tiled=True),
    )
    tile_rows = q_tile.shape[0]
    block_rows = min(1024, tile_rows)
    block_count = tile_rows // block_rows
    ctx_index = lax.axis_index("ctx")
    tile_first = ctx_index * tile_rows
    tile_starts = doc_starts(lengths, tile_first, tile_rows)
    query_blocks = [
        q_tile[number * block_rows : (number + 1) * block_rows].reshape(
            block_rows, kv_local, group_size, HD
        )
        for number in range(block_count)
    ]
    start_blocks = [
        tile_starts[number * block_rows : (number + 1) * block_rows]
        for number in range(block_count)
    ]
    query_firsts = [tile_first + number * block_rows for number in range(block_count)]
    key_pair = jnp.stack([k_tile, v_tile])
    key_tiles = [key_pair]
    moving = key_pair
    for offset in range(1, REACH + 1):
        moving = shifted(moving, "ctx", 1)
        key_tiles.append(moving)

    def split_keys(tile_pair):
        key_list = [
            tile_pair[0, number * block_rows : (number + 1) * block_rows].reshape(
                block_rows, kv_local, HD
            )
            for number in range(block_count)
        ]
        value_list = [
            tile_pair[1, number * block_rows : (number + 1) * block_rows].reshape(
                block_rows, kv_local, HD
            )
            for number in range(block_count)
        ]
        return (key_list, value_list)

    states = [
        (
            jnp.full((block_rows, kv_local, group_size), NEG_FILL, jnp.float32),
            jnp.zeros((block_rows, kv_local, group_size), jnp.float32),
            jnp.zeros((block_rows, kv_local, group_size, HD), jnp.float32),
        )
        for number in range(block_count)
    ]
    for offset in range(REACH + 1):
        key_list, value_list = split_keys(key_tiles[offset])
        key_start = (ctx_index - offset) * tile_rows
        for query_number in range(block_count):
            query_block = query_blocks[query_number]
            query_first = query_firsts[query_number]
            start_rows = start_blocks[query_number]
            for key_number in range(block_count):
                key_block = key_list[key_number]
                value_block = value_list[key_number]
                key_first = key_start + key_number * block_rows

                def forward_block(
                    current,
                    query_block=query_block,
                    query_first=query_first,
                    start_rows=start_rows,
                    key_block=key_block,
                    value_block=value_block,
                    key_first=key_first,
                ):
                    max_old, sum_old, acc_old = current
                    mask = visible_pairs(query_first, key_first, start_rows, block_rows)
                    scores = (
                        jnp.einsum(
                            "qkgd,ckd->qkgc",
                            query_block,
                            key_block,
                            preferred_element_type=jnp.float32,
                        )
                        * scaling
                    )
                    scores = jnp.where(mask, scores, NEG_FILL)
                    max_new = jnp.maximum(max_old, jnp.max(scores, axis=-1))
                    prob_raw = jnp.where(mask, jnp.exp(scores - max_new[..., None]), 0.0)
                    rescale = jnp.exp(max_old - max_new)
                    sum_new = sum_old * rescale + jnp.sum(prob_raw, axis=-1)
                    acc_new = acc_old * rescale[..., None] + jnp.einsum(
                        "qkgc,ckd->qkgd",
                        prob_raw.astype(jnp.bfloat16),
                        value_block,
                        preferred_element_type=jnp.float32,
                    )
                    return (max_new, sum_new, acc_new)

                live = block_live(query_first, key_first, tile_starts, tile_first, block_rows)
                states[query_number] = lax.cond(
                    live, forward_block, lambda unchanged: unchanged, states[query_number]
                )
    out_blocks = [(state[2] / state[1][..., None]).astype(jnp.bfloat16) for state in states]
    lse_blocks = [state[0] + jnp.log(state[1]) for state in states]
    grad_tile = lax.all_to_all(d_out, "head", split_axis=1, concat_axis=0, tiled=True)
    grad_blocks = [
        grad_tile[number * block_rows : (number + 1) * block_rows].reshape(
            block_rows, kv_local, group_size, HD
        )
        for number in range(block_count)
    ]
    delta_blocks = [
        jnp.sum(
            grad_blocks[number].astype(jnp.float32) * out_blocks[number].astype(jnp.float32),
            axis=-1,
        )
        for number in range(block_count)
    ]
    query_totals = [
        jnp.zeros((block_rows, kv_local, group_size, HD), jnp.float32)
        for number in range(block_count)
    ]
    partial_grads = []
    for offset in range(REACH + 1):
        key_list, value_list = split_keys(key_tiles[offset])
        key_start = (ctx_index - offset) * tile_rows
        key_sums = [
            jnp.zeros((block_rows, kv_local, HD), jnp.float32) for number in range(block_count)
        ]
        value_sums = [
            jnp.zeros((block_rows, kv_local, HD), jnp.float32) for number in range(block_count)
        ]
        for query_number in range(block_count):
            query_block = query_blocks[query_number]
            grad_block = grad_blocks[query_number]
            query_first = query_firsts[query_number]
            start_rows = start_blocks[query_number]
            lse_rows = lse_blocks[query_number]
            delta_rows = delta_blocks[query_number]
            for key_number in range(block_count):
                key_block = key_list[key_number]
                value_block = value_list[key_number]
                key_first = key_start + key_number * block_rows

                def backward_block(
                    current,
                    query_block=query_block,
                    grad_block=grad_block,
                    query_first=query_first,
                    start_rows=start_rows,
                    lse_rows=lse_rows,
                    delta_rows=delta_rows,
                    key_block=key_block,
                    value_block=value_block,
                    key_first=key_first,
                ):
                    query_grad, key_grad, value_grad = current
                    mask = visible_pairs(query_first, key_first, start_rows, block_rows)
                    scores = (
                        jnp.einsum(
                            "qkgd,ckd->qkgc",
                            query_block,
                            key_block,
                            preferred_element_type=jnp.float32,
                        )
                        * scaling
                    )
                    prob_raw = jnp.where(mask, jnp.exp(scores - lse_rows[..., None]), 0.0)
                    weights = prob_raw.astype(jnp.bfloat16)
                    value_grad = value_grad + jnp.einsum(
                        "qkgc,qkgd->ckd", weights, grad_block, preferred_element_type=jnp.float32
                    )
                    prob_grad = jnp.einsum(
                        "qkgd,ckd->qkgc",
                        grad_block,
                        value_block,
                        preferred_element_type=jnp.float32,
                    )
                    score_grad = (prob_raw * (prob_grad - delta_rows[..., None]) * scaling).astype(
                        jnp.bfloat16
                    )
                    query_grad = query_grad + jnp.einsum(
                        "qkgc,ckd->qkgd", score_grad, key_block, preferred_element_type=jnp.float32
                    )
                    key_grad = key_grad + jnp.einsum(
                        "qkgc,qkgd->ckd",
                        score_grad,
                        query_block,
                        preferred_element_type=jnp.float32,
                    )
                    return (query_grad, key_grad, value_grad)

                live = block_live(query_first, key_first, tile_starts, tile_first, block_rows)
                current = (query_totals[query_number], key_sums[key_number], value_sums[key_number])
                query_totals[query_number], key_sums[key_number], value_sums[key_number] = lax.cond(
                    live, backward_block, lambda unchanged: unchanged, current
                )
        key_whole = jnp.concatenate(key_sums, axis=0).reshape(tile_rows, kv_local * HD)
        value_whole = jnp.concatenate(value_sums, axis=0).reshape(tile_rows, kv_local * HD)
        partial_grads.append(jnp.stack([key_whole, value_whole]))
    grad_total = partial_grads[REACH]
    for offset in range(REACH - 1, -1, -1):
        grad_total = (
            shifted(grad_total.astype(jnp.bfloat16), "ctx", -1).astype(grad_total.dtype)
            + partial_grads[offset]
        )
    out_tile = jnp.concatenate(out_blocks, axis=0).reshape(tile_rows, q_local * HD)
    query_tile = (
        jnp.concatenate(query_totals, axis=0).reshape(tile_rows, q_local * HD).astype(jnp.bfloat16)
    )
    attn_out, grad_queries = (
        lax.all_to_all(out_tile, "head", split_axis=0, concat_axis=1, tiled=True),
        lax.all_to_all(query_tile, "head", split_axis=0, concat_axis=1, tiled=True),
    )
    token_grads = lax.all_to_all(
        grad_total.astype(jnp.bfloat16), "head", split_axis=1, concat_axis=2, tiled=True
    ).astype(grad_total.dtype)
    if copies > 1:
        token_grads = jnp.sum(token_grads.reshape(2, tok_dev, KVH, copies, HD), axis=3).reshape(
            2, tok_dev, KVH * HD
        )
    token_grads = token_grads.astype(jnp.bfloat16)
    return (attn_out, grad_queries, token_grads[0], token_grads[1])


CHUNKS = ((0, 1, 2, 3),)
CONTRACT_LAST = (((1,), (1,)), ((), ()))
CONTRACT_FIRST = (((0,), (0,)), ((), ()))
VMEM = pl.BlockSpec(memory_space=pltpu.VMEM)
SMEM = pl.BlockSpec(memory_space=pltpu.SMEM)
SMALL = pltpu.CompilerParams(vmem_limit_bytes=8 * 1024 * 1024)


def flipped(value, ctx_bits, head_bits):
    ctx, heads = lax.axis_size("ctx"), lax.axis_size("head")
    pairs = [
        (c * heads + h, (c ^ ctx_bits) * heads + (h ^ head_bits))
        for c in range(ctx)
        for h in range(heads)
    ]
    return lax.ppermute(value, ("ctx", "head"), pairs)


def piece_columns(pieces, flip, wide, offset=0):
    index = lax.axis_index("ctx") // (lax.axis_size("ctx") // pieces)
    return pl.ds(pl.multiple_of(((index ^ flip) + offset) * wide, HD), wide)


def split_heads_kernel(pieces, wide, both_ref, *piece_refs):
    for flip, piece_ref in enumerate(piece_refs):
        for side in range(2):
            columns = piece_columns(pieces, flip, wide, side * pieces)
            piece_ref[:, side * wide : (side + 1) * wide] = both_ref[:, columns]


def join_heads_kernel(pieces, wide, *refs):
    piece_refs, (left_ref, right_ref) = refs[:pieces], refs[pieces:]
    for flip, piece_ref in enumerate(piece_refs):
        columns = piece_columns(pieces, flip, wide)
        left_ref[:, columns] = piece_ref[:, :wide]
        right_ref[:, columns] = piece_ref[:, wide:]


def split_heads(left, right, pieces):
    rows, wide = left.shape[0], left.shape[1] // pieces
    return pl.pallas_call(
        functools.partial(split_heads_kernel, pieces, wide),
        out_shape=[jax.ShapeDtypeStruct((rows, 2 * wide), left.dtype)] * pieces,
        in_specs=[VMEM],
        out_specs=[VMEM] * pieces,
        compiler_params=SMALL,
    )(jnp.concatenate([left, right], axis=1))


def join_heads(parts):
    pieces = len(parts)
    rows, wide = parts[0].shape[0], parts[0].shape[1] // 2
    return pl.pallas_call(
        functools.partial(join_heads_kernel, pieces, wide),
        out_shape=[jax.ShapeDtypeStruct((rows, wide * pieces), parts[0].dtype)] * 2,
        in_specs=[VMEM] * pieces,
        out_specs=[VMEM] * 2,
        compiler_params=SMALL,
    )(*parts)


def prepare_kernel(pieces, wide, lengths_ref, both_ref, *out_refs):
    piece_refs, marks_ref = out_refs[:pieces], out_refs[pieces]
    split_heads_kernel(pieces, wide, both_ref, *piece_refs)
    total, docs = marks_ref.shape[0], lengths_ref.shape[0]
    lane = lax.broadcasted_iota(jnp.int32, (1, MARKS), 1)
    begins = jnp.zeros((1, MARKS), jnp.int32)
    ends = jnp.where(lane < docs, total, 0)
    end = jnp.int32(0)
    for number in range(docs):
        begins = jnp.where(lane == number, end, begins)
        end = end + lengths_ref[number]
        ends = jnp.where(lane == number, end, ends)

    def some_rows(step, _):
        rows = pl.ds(pl.multiple_of(step * KEY_ROWS, KEY_ROWS), KEY_ROWS)
        position = step * KEY_ROWS + lax.broadcasted_iota(jnp.int32, (KEY_ROWS, MARKS), 0)
        inside = (position >= begins) & (position < ends)
        marks_ref[rows, :] = jnp.where(inside, 1.0, 0.0).astype(jnp.bfloat16)
        return 0

    lax.fori_loop(0, total // KEY_ROWS, some_rows, 0)


def prepare(lengths, left, right, pieces, total):
    rows, wide = left.shape[0], left.shape[1] // pieces
    results = pl.pallas_call(
        functools.partial(prepare_kernel, pieces, wide),
        out_shape=[jax.ShapeDtypeStruct((rows, 2 * wide), left.dtype)] * pieces
        + [jax.ShapeDtypeStruct((total, MARKS), jnp.bfloat16)],
        in_specs=[SMEM, VMEM],
        out_specs=[VMEM] * (pieces + 1),
        compiler_params=SMALL,
    )(lengths, jnp.concatenate([left, right], axis=1))
    return results[:pieces], results[pieces]


KEY_ROWS = 256
BATCH = 4
MARKS = 128
HIDDEN = -(2.0**100)


def attention_kernel(cores, heads, tok, *refs):
    group = QH // KVH
    lanes = group * tok
    tile_rows = heads * tok
    kv_count = heads * cores * len(CHUNKS)
    lengths_ref, marks_ref, refs = refs[0], refs[1], refs[2:]
    docs = lengths_ref.shape[0]
    qd_refs, refs = refs[:KVH], refs[KVH:]
    kv_refs, refs = refs[:kv_count], refs[kv_count:]
    od_refs, refs = refs[:KVH], refs[KVH:]
    dkv_refs, refs = refs[: cores * len(CHUNKS)], refs[cores * len(CHUNKS) :]
    k_all, v_all, q_wide, g_all, dk_acc, dv_acc, score, prob, tops, acc, table = refs
    scaling = HD ** (-0.5)
    log_scale = scaling * math.log2(math.e)
    f32, bf16 = jnp.float32, jnp.bfloat16

    ctx_index, head_index = lax.axis_index("ctx"), lax.axis_index("head")
    part, core = ctx_index // cores, ctx_index % cores

    def rows_of(head_flip, core_flip, part_flip):
        tile = (part ^ part_flip) * cores + (core ^ core_flip)
        return pl.ds(pl.multiple_of((tile * heads + (head_index ^ head_flip)) * tok, tok), tok)

    for chunk_number, chunk in enumerate(CHUNKS):
        for number in range(heads * cores):
            kv_ref = kv_refs[chunk_number * heads * cores + number]
            for place, flip in enumerate(chunk):
                rows = rows_of(number // cores, number % cores, flip)
                k_all[rows, :] = kv_ref[place, :, :HD]
                v_all[rows, :] = kv_ref[place, :, HD:]
    feature = lax.broadcasted_iota(jnp.int32, (tok, MARKS), 1)
    for flip, qd_ref in enumerate(qd_refs):
        own_marks = marks_ref[rows_of(0, 0, flip), :].astype(f32)
        bias = jnp.where(feature < docs, (1.0 - own_marks) * HIDDEN, 0.0).astype(bf16)
        for member in range(group):
            rows = slice(member * tok, (member + 1) * tok)
            q_wide[flip, rows, :HD] = qd_ref[:, member * HD : (member + 1) * HD]
            q_wide[flip, rows, HD:] = bias
            g_all[flip, rows, :] = qd_ref[:, (group + member) * HD : (group + member + 1) * HD]
    dk_acc[...] = jnp.zeros_like(dk_acc)
    dv_acc[...] = jnp.zeros_like(dv_acc)
    tops[...] = jnp.full_like(tops, NEG_FILL)
    acc[...] = jnp.zeros_like(acc)

    def entry(number, flip, row, limit):
        table[0, number] = flip
        table[1, number] = row
        table[2, number] = limit

    total = jnp.int32(0)
    for flip in range(KVH):
        first = ((part ^ flip) * cores + core) * tile_rows + head_index * tok
        end, low = jnp.int32(0), jnp.int32(0)
        for number in range(docs):
            length = lengths_ref[number]
            end = end + length
            low = low + jnp.where(end <= first, length, 0)
        count = (first + tok - low // tok * tok + KEY_ROWS - 1) // KEY_ROWS
        begin = jnp.maximum(first + tok - count * KEY_ROWS, 0)

        def listed(step, _, flip=flip, first=first, begin=begin, total=total):
            row = begin + step * KEY_ROWS
            entry(total + step, flip, row, first - row)
            return 0

        lax.fori_loop(0, count, listed, 0)
        total = total + count
    for spare in range(BATCH - 1):
        entry(total + spare, 0, 0, -(1 << 20))
    rounds = (total + 1) // BATCH
    left_over = (total - rounds * BATCH + 1) // 2

    def sweep(body):
        def one_round(number, _):
            body([number * BATCH + place for place in range(BATCH)])
            return 0

        def one_pair(number, _):
            body([rounds * BATCH + number * 2 + place for place in range(2)])
            return 0

        lax.fori_loop(0, rounds, one_round, 0)
        lax.fori_loop(0, left_over, one_pair, 0)

    def key_rows(item):
        return pl.ds(pl.multiple_of(table[1, item], tok), KEY_ROWS)

    def score_rows(item):
        return pl.ds(pl.multiple_of(item * KEY_ROWS, KEY_ROWS), KEY_ROWS)

    def wide(ref, rows):
        return jnp.concatenate([ref[rows, :], marks_ref[rows, :]], axis=1)

    key_row = lax.broadcasted_iota(jnp.int32, (KEY_ROWS, lanes), 0)
    query_row = lax.broadcasted_iota(jnp.int32, (1, lanes), 1) % tok

    def scores_round(items):
        raws = [
            lax.dot_general(
                wide(k_all, key_rows(item)),
                q_wide[table[0, item]],
                CONTRACT_LAST,
                preferred_element_type=f32,
            )
            for item in items
        ]
        for item, raw in zip(items, raws):
            raw = jnp.where(key_row <= query_row + table[2, item], raw, NEG_FILL)
            score[score_rows(item), :] = raw
            flip = table[0, item]
            tops[flip] = jnp.maximum(
                tops[flip], jnp.max(raw.reshape(KEY_ROWS // 8, 8, lanes), axis=0)
            )

    sweep(scores_round)
    for flip in range(KVH):
        tops[flip] = jnp.broadcast_to(jnp.max(tops[flip], axis=0, keepdims=True), (8, lanes))

    ones = jnp.ones((acc.shape[1] - HD, KEY_ROWS), bf16)

    def out_round(items):
        weights = [
            jnp.exp2((score[score_rows(item), :] - tops[table[0, item], :1]) * log_scale).astype(bf16)
            for item in items
        ]
        for item, weight in zip(items, weights):
            prob[score_rows(item), :] = weight
        parts = [
            jnp.dot(
                jnp.concatenate([v_all[key_rows(item), :].T, ones], axis=0),
                weight,
                preferred_element_type=f32,
            )
            for item, weight in zip(items, weights)
        ]
        for item, value in zip(items, parts):
            acc[table[0, item]] += value

    sweep(out_round)
    for flip in range(KVH):
        inverse = 1.0 / acc[flip, HD : HD + 1, :]
        turned = (acc[flip, :HD, :] * inverse).astype(bf16)
        out = turned.T
        g_turned = g_all[flip].T.astype(f32)
        delta = jnp.sum(turned.astype(f32) * g_turned, axis=0, keepdims=True)
        acc[flip, HD : HD + 1, :] = inverse
        acc[flip, HD + 1 : HD + 2, :] = delta
        acc[flip, :HD, :] = jnp.zeros((HD, lanes), f32)
        for member in range(group):
            rows = slice(member * tok, (member + 1) * tok)
            od_refs[flip][:, member * HD : (member + 1) * HD] = out[rows, :]

    def grad_round(items):
        slopes = [
            lax.dot_general(
                v_all[key_rows(item), :],
                g_all[table[0, item]],
                CONTRACT_LAST,
                preferred_element_type=f32,
            )
            for item in items
        ]
        probs = [
            prob[score_rows(item), :].astype(f32) * acc[table[0, item], HD : HD + 1, :]
            for item in items
        ]
        weights = [value.astype(bf16) for value in probs]
        score_grads = [
            (value * (slope - acc[table[0, item], HD + 1 : HD + 2, :])).astype(bf16)
            for item, value, slope in zip(items, probs, slopes)
        ]
        for item, weight, score_grad in zip(items, weights, score_grads):
            flip, rows = table[0, item], key_rows(item)
            dv_acc[rows, :] += jnp.dot(weight, g_all[flip], preferred_element_type=f32)
            dk_acc[rows, :] += jnp.dot(score_grad, q_wide[flip, :, :HD], preferred_element_type=f32)
            acc[flip, :HD, :] += lax.dot_general(
                k_all[rows, :], score_grad, CONTRACT_FIRST, preferred_element_type=f32
            )

    sweep(grad_round)

    for flip, od_ref in enumerate(od_refs):
        turned = (acc[flip, :HD, :] * scaling).astype(bf16).T
        for member in range(group):
            rows = slice(member * tok, (member + 1) * tok)
            od_ref[:, (group + member) * HD : (group + member + 1) * HD] = turned[rows, :]
    for chunk_number, chunk in enumerate(CHUNKS):
        for core_flip in range(cores):
            dkv_ref = dkv_refs[chunk_number * cores + core_flip]
            for head_flip in range(heads):
                for place, flip in enumerate(chunk):
                    rows = rows_of(head_flip, core_flip, flip)
                    dkv_ref[head_flip, place, :, :HD] = (dk_acc[rows, :] * scaling).astype(bf16)
                    dkv_ref[head_flip, place, :, HD:] = dv_acc[rows, :].astype(bf16)


def attention(lengths, marks, qd, kv, cores, heads):
    tok, group = qd[0].shape[0], QH // KVH
    total = KVH * cores * heads * tok
    lanes = group * tok
    reach = REACH * heads * tok
    pair = sum(-(-(keys + tok) // KEY_ROWS) for keys in (reach, reach // 2))
    items = -(-KVH // 2 * pair // BATCH) * BATCH
    bf16, f32 = jnp.bfloat16, jnp.float32
    results = pl.pallas_call(
        functools.partial(attention_kernel, cores, heads, tok),
        out_shape=[jax.ShapeDtypeStruct(a.shape, a.dtype) for a in qd]
        + [
            jax.ShapeDtypeStruct((heads, len(chunk), tok, 2 * HD), bf16)
            for chunk in CHUNKS
            for _ in range(cores)
        ],
        in_specs=[SMEM] + [VMEM] * (1 + len(qd) + len(kv)),
        out_specs=[VMEM] * (len(qd) + cores * len(CHUNKS)),
        scratch_shapes=[
            pltpu.VMEM((total, HD), bf16),
            pltpu.VMEM((total, HD), bf16),
            pltpu.VMEM((KVH, lanes, HD + MARKS), bf16),
            pltpu.VMEM((KVH, lanes, HD), bf16),
            pltpu.VMEM((total, HD), f32),
            pltpu.VMEM((total, HD), f32),
            pltpu.VMEM((items * KEY_ROWS, lanes), f32),
            pltpu.VMEM((items * KEY_ROWS, lanes), bf16),
            pltpu.VMEM((KVH, 8, lanes), f32),
            pltpu.VMEM((KVH, HD + 16, lanes), f32),
            pltpu.SMEM((3, items + BATCH), jnp.int32),
        ],
        compiler_params=pltpu.CompilerParams(vmem_limit_bytes=36 * 1024 * 1024),
    )(lengths, marks, *qd, *kv)
    return results[: len(qd)], results[len(qd) :]


def part_shards(queries, keys, values, d_out, lengths):
    heads, ctx = lax.axis_size("head"), lax.axis_size("ctx")
    cores = ctx // KVH
    total = queries.shape[0] * heads * ctx
    together = lax.optimization_barrier

    def over_part(piece, flip):
        return flipped(piece, flip * cores, 0)

    def exchange(pieces):
        return [pieces[0]] + [over_part(piece, s + 1) for s, piece in enumerate(pieces[1:])]

    def summed(*terms):
        return sum(term.astype(jnp.float32) for term in terms).astype(jnp.bfloat16)

    kv_pieces = split_heads(keys, values, KVH)
    far_own = flipped(kv_pieces[0][None], 0, 2)
    kv_pieces = exchange(kv_pieces)
    kv_mine = jnp.stack(kv_pieces)
    far_rest = flipped(jnp.stack(kv_pieces[1:]), 0, 2)
    far = jnp.concatenate([far_own, far_rest])
    qd, marks = prepare(lengths, queries, d_out, KVH, total)
    qd = exchange(qd)
    near = flipped(kv_mine, 0, 1)
    kv = []
    for piece in (kv_mine, near, far, flipped(far, 0, 1)):
        kv += [piece, flipped(piece, 1, 0)]
    od, dkv = attention(lengths, marks, qd, kv, cores, heads)

    both = (dkv[0], flipped(dkv[1], 1, 0))
    third = flipped(summed(*(term[3] for term in both)), 0, 1)
    first, _ = together((summed(*(term[1] for term in both)), third))
    first, rest, od_moved = together(
        (
            flipped(first, 0, 1),
            flipped(summed(*(term[2, 1:] for term in both), third[1:]), 0, 2),
            exchange(od)[1:],
        )
    )
    own, grads = together(
        (
            summed(*(term[2, 0] for term in both), third[0]),
            [summed(*(term[0, s] for term in both), first[s], rest[s - 1]) for s in (1, 2, 3)],
        )
    )
    own = flipped(own, 0, 2)
    grads = [over_part(grad, s + 1) for s, grad in enumerate(grads)]
    attn_out, grad_queries = join_heads([od[0], *od_moved])
    grads = [summed(*(term[0, 0] for term in both), first[0], own), *grads]
    grad_keys, grad_values = join_heads(grads)
    return attn_out, grad_queries, grad_keys, grad_values


def solution(mesh):
    ctx_dev, head_dev = mesh.shape["ctx"], mesh.shape["head"]
    local = part_shards if ctx_dev == 2 * KVH and head_dev == 4 else shards
    rows = P(("ctx", "head"), None)
    return jax.shard_map(
        local,
        mesh=mesh,
        in_specs=(rows, rows, rows, rows, P()),
        out_specs=(rows, rows, rows, rows),
        check_vma=False,
    )
```

```python
import functools
import math

import jax
import jax.numpy as jnp
from jax import lax
from jax.experimental import pallas as pl
from jax.experimental.pallas import tpu as pltpu
from jax.sharding import PartitionSpec as P

QH = 16
KVH = 4
HD = 128
REACH = 4


NEG_FILL = -1e30


def shifted(value, axis, steps):
    count = lax.axis_size(axis)
    first, last = (max(0, -steps), min(count, count - steps))
    return lax.ppermute(value, axis, [(source, source + steps) for source in range(first, last)])


def doc_starts(lengths, first, count):
    doc_ends = jnp.cumsum(lengths)
    positions = first + jnp.arange(count, dtype=jnp.int32)
    passed = doc_ends[None, :] <= positions[:, None]
    return jnp.sum(jnp.where(passed, lengths[None, :], 0), axis=1)


def visible_pairs(query_first, key_first, start_rows, block_rows):
    query_pos = query_first + jnp.arange(block_rows, dtype=jnp.int32)
    key_pos = key_first + jnp.arange(block_rows, dtype=jnp.int32)
    mask = (key_pos[None, :] <= query_pos[:, None]) & (key_pos[None, :] >= start_rows[:, None])
    return mask[:, None, None, :]


def block_live(query_first, key_first, tile_starts, tile_first, block_rows):
    lowest = jnp.maximum(query_first, key_first)
    picked = jnp.clip(lowest - tile_first, 0, tile_starts.shape[0] - 1)
    first_start = lax.dynamic_index_in_dim(tile_starts, picked, 0, keepdims=False)
    return (lowest <= query_first + block_rows - 1) & (first_start <= key_first + block_rows - 1)


def shards(queries, keys, values, d_out, lengths):
    heads_dev = lax.axis_size("head")
    tok_dev = queries.shape[0]
    copies = max(1, heads_dev // KVH)
    kv_local = max(1, KVH // heads_dev)
    q_local = QH // heads_dev
    group_size = q_local // kv_local
    scaling = HD ** (-0.5)

    def spread(array_in):
        if copies > 1:
            return jnp.repeat(array_in.reshape(tok_dev, KVH, HD), copies, axis=1).reshape(
                tok_dev, KVH * copies * HD
            )
        return array_in

    q_tile, k_tile, v_tile = (
        lax.all_to_all(queries, "head", split_axis=1, concat_axis=0, tiled=True),
        lax.all_to_all(spread(keys), "head", split_axis=1, concat_axis=0, tiled=True),
        lax.all_to_all(spread(values), "head", split_axis=1, concat_axis=0, tiled=True),
    )
    tile_rows = q_tile.shape[0]
    block_rows = min(1024, tile_rows)
    block_count = tile_rows // block_rows
    ctx_index = lax.axis_index("ctx")
    tile_first = ctx_index * tile_rows
    tile_starts = doc_starts(lengths, tile_first, tile_rows)
    query_blocks = [
        q_tile[number * block_rows : (number + 1) * block_rows].reshape(
            block_rows, kv_local, group_size, HD
        )
        for number in range(block_count)
    ]
    start_blocks = [
        tile_starts[number * block_rows : (number + 1) * block_rows]
        for number in range(block_count)
    ]
    query_firsts = [tile_first + number * block_rows for number in range(block_count)]
    key_pair = jnp.stack([k_tile, v_tile])
    key_tiles = [key_pair]
    moving = key_pair
    for offset in range(1, REACH + 1):
        moving = shifted(moving, "ctx", 1)
        key_tiles.append(moving)

    def split_keys(tile_pair):
        key_list = [
            tile_pair[0, number * block_rows : (number + 1) * block_rows].reshape(
                block_rows, kv_local, HD
            )
            for number in range(block_count)
        ]
        value_list = [
            tile_pair[1, number * block_rows : (number + 1) * block_rows].reshape(
                block_rows, kv_local, HD
            )
            for number in range(block_count)
        ]
        return (key_list, value_list)

    states = [
        (
            jnp.full((block_rows, kv_local, group_size), NEG_FILL, jnp.float32),
            jnp.zeros((block_rows, kv_local, group_size), jnp.float32),
            jnp.zeros((block_rows, kv_local, group_size, HD), jnp.float32),
        )
        for number in range(block_count)
    ]
    for offset in range(REACH + 1):
        key_list, value_list = split_keys(key_tiles[offset])
        key_start = (ctx_index - offset) * tile_rows
        for query_number in range(block_count):
            query_block = query_blocks[query_number]
            query_first = query_firsts[query_number]
            start_rows = start_blocks[query_number]
            for key_number in range(block_count):
                key_block = key_list[key_number]
                value_block = value_list[key_number]
                key_first = key_start + key_number * block_rows

                def forward_block(
                    current,
                    query_block=query_block,
                    query_first=query_first,
                    start_rows=start_rows,
                    key_block=key_block,
                    value_block=value_block,
                    key_first=key_first,
                ):
                    max_old, sum_old, acc_old = current
                    mask = visible_pairs(query_first, key_first, start_rows, block_rows)
                    scores = (
                        jnp.einsum(
                            "qkgd,ckd->qkgc",
                            query_block,
                            key_block,
                            preferred_element_type=jnp.float32,
                        )
                        * scaling
                    )
                    scores = jnp.where(mask, scores, NEG_FILL)
                    max_new = jnp.maximum(max_old, jnp.max(scores, axis=-1))
                    prob_raw = jnp.where(mask, jnp.exp(scores - max_new[..., None]), 0.0)
                    rescale = jnp.exp(max_old - max_new)
                    sum_new = sum_old * rescale + jnp.sum(prob_raw, axis=-1)
                    acc_new = acc_old * rescale[..., None] + jnp.einsum(
                        "qkgc,ckd->qkgd",
                        prob_raw.astype(jnp.bfloat16),
                        value_block,
                        preferred_element_type=jnp.float32,
                    )
                    return (max_new, sum_new, acc_new)

                live = block_live(query_first, key_first, tile_starts, tile_first, block_rows)
                states[query_number] = lax.cond(
                    live, forward_block, lambda unchanged: unchanged, states[query_number]
                )
    out_blocks = [(state[2] / state[1][..., None]).astype(jnp.bfloat16) for state in states]
    lse_blocks = [state[0] + jnp.log(state[1]) for state in states]
    grad_tile = lax.all_to_all(d_out, "head", split_axis=1, concat_axis=0, tiled=True)
    grad_blocks = [
        grad_tile[number * block_rows : (number + 1) * block_rows].reshape(
            block_rows, kv_local, group_size, HD
        )
        for number in range(block_count)
    ]
    delta_blocks = [
        jnp.sum(
            grad_blocks[number].astype(jnp.float32) * out_blocks[number].astype(jnp.float32),
            axis=-1,
        )
        for number in range(block_count)
    ]
    query_totals = [
        jnp.zeros((block_rows, kv_local, group_size, HD), jnp.float32)
        for number in range(block_count)
    ]
    partial_grads = []
    for offset in range(REACH + 1):
        key_list, value_list = split_keys(key_tiles[offset])
        key_start = (ctx_index - offset) * tile_rows
        key_sums = [
            jnp.zeros((block_rows, kv_local, HD), jnp.float32) for number in range(block_count)
        ]
        value_sums = [
            jnp.zeros((block_rows, kv_local, HD), jnp.float32) for number in range(block_count)
        ]
        for query_number in range(block_count):
            query_block = query_blocks[query_number]
            grad_block = grad_blocks[query_number]
            query_first = query_firsts[query_number]
            start_rows = start_blocks[query_number]
            lse_rows = lse_blocks[query_number]
            delta_rows = delta_blocks[query_number]
            for key_number in range(block_count):
                key_block = key_list[key_number]
                value_block = value_list[key_number]
                key_first = key_start + key_number * block_rows

                def backward_block(
                    current,
                    query_block=query_block,
                    grad_block=grad_block,
                    query_first=query_first,
                    start_rows=start_rows,
                    lse_rows=lse_rows,
                    delta_rows=delta_rows,
                    key_block=key_block,
                    value_block=value_block,
                    key_first=key_first,
                ):
                    query_grad, key_grad, value_grad = current
                    mask = visible_pairs(query_first, key_first, start_rows, block_rows)
                    scores = (
                        jnp.einsum(
                            "qkgd,ckd->qkgc",
                            query_block,
                            key_block,
                            preferred_element_type=jnp.float32,
                        )
                        * scaling
                    )
                    prob_raw = jnp.where(mask, jnp.exp(scores - lse_rows[..., None]), 0.0)
                    weights = prob_raw.astype(jnp.bfloat16)
                    value_grad = value_grad + jnp.einsum(
                        "qkgc,qkgd->ckd", weights, grad_block, preferred_element_type=jnp.float32
                    )
                    prob_grad = jnp.einsum(
                        "qkgd,ckd->qkgc",
                        grad_block,
                        value_block,
                        preferred_element_type=jnp.float32,
                    )
                    score_grad = (prob_raw * (prob_grad - delta_rows[..., None]) * scaling).astype(
                        jnp.bfloat16
                    )
                    query_grad = query_grad + jnp.einsum(
                        "qkgc,ckd->qkgd", score_grad, key_block, preferred_element_type=jnp.float32
                    )
                    key_grad = key_grad + jnp.einsum(
                        "qkgc,qkgd->ckd",
                        score_grad,
                        query_block,
                        preferred_element_type=jnp.float32,
                    )
                    return (query_grad, key_grad, value_grad)

                live = block_live(query_first, key_first, tile_starts, tile_first, block_rows)
                current = (query_totals[query_number], key_sums[key_number], value_sums[key_number])
                query_totals[query_number], key_sums[key_number], value_sums[key_number] = lax.cond(
                    live, backward_block, lambda unchanged: unchanged, current
                )
        key_whole = jnp.concatenate(key_sums, axis=0).reshape(tile_rows, kv_local * HD)
        value_whole = jnp.concatenate(value_sums, axis=0).reshape(tile_rows, kv_local * HD)
        partial_grads.append(jnp.stack([key_whole, value_whole]))
    grad_total = partial_grads[REACH]
    for offset in range(REACH - 1, -1, -1):
        grad_total = (
            shifted(grad_total.astype(jnp.bfloat16), "ctx", -1).astype(grad_total.dtype)
            + partial_grads[offset]
        )
    out_tile = jnp.concatenate(out_blocks, axis=0).reshape(tile_rows, q_local * HD)
    query_tile = (
        jnp.concatenate(query_totals, axis=0).reshape(tile_rows, q_local * HD).astype(jnp.bfloat16)
    )
    attn_out, grad_queries = (
        lax.all_to_all(out_tile, "head", split_axis=0, concat_axis=1, tiled=True),
        lax.all_to_all(query_tile, "head", split_axis=0, concat_axis=1, tiled=True),
    )
    token_grads = lax.all_to_all(
        grad_total.astype(jnp.bfloat16), "head", split_axis=1, concat_axis=2, tiled=True
    ).astype(grad_total.dtype)
    if copies > 1:
        token_grads = jnp.sum(token_grads.reshape(2, tok_dev, KVH, copies, HD), axis=3).reshape(
            2, tok_dev, KVH * HD
        )
    token_grads = token_grads.astype(jnp.bfloat16)
    return (attn_out, grad_queries, token_grads[0], token_grads[1])


CHUNKS = ((0, 1, 2, 3),)
CONTRACT_LAST = (((1,), (1,)), ((), ()))
CONTRACT_FIRST = (((0,), (0,)), ((), ()))
VMEM = pl.BlockSpec(memory_space=pltpu.VMEM)
SMEM = pl.BlockSpec(memory_space=pltpu.SMEM)
SMALL = pltpu.CompilerParams(vmem_limit_bytes=8 * 1024 * 1024)


def flipped(value, ctx_bits, head_bits):
    ctx, heads = lax.axis_size("ctx"), lax.axis_size("head")
    pairs = [
        (c * heads + h, (c ^ ctx_bits) * heads + (h ^ head_bits))
        for c in range(ctx)
        for h in range(heads)
    ]
    return lax.ppermute(value, ("ctx", "head"), pairs)


def piece_columns(pieces, flip, wide, offset=0):
    index = lax.axis_index("ctx") // (lax.axis_size("ctx") // pieces)
    return pl.ds(pl.multiple_of(((index ^ flip) + offset) * wide, HD), wide)


def split_heads_kernel(pieces, wide, both_ref, *piece_refs):
    for flip, piece_ref in enumerate(piece_refs):
        for side in range(2):
            columns = piece_columns(pieces, flip, wide, side * pieces)
            piece_ref[:, side * wide : (side + 1) * wide] = both_ref[:, columns]


def join_heads_kernel(pieces, wide, *refs):
    piece_refs, (left_ref, right_ref) = refs[:pieces], refs[pieces:]
    for flip, piece_ref in enumerate(piece_refs):
        columns = piece_columns(pieces, flip, wide)
        left_ref[:, columns] = piece_ref[:, :wide]
        right_ref[:, columns] = piece_ref[:, wide:]


def split_heads(left, right, pieces):
    rows, wide = left.shape[0], left.shape[1] // pieces
    return pl.pallas_call(
        functools.partial(split_heads_kernel, pieces, wide),
        out_shape=[jax.ShapeDtypeStruct((rows, 2 * wide), left.dtype)] * pieces,
        in_specs=[VMEM],
        out_specs=[VMEM] * pieces,
        compiler_params=SMALL,
    )(jnp.concatenate([left, right], axis=1))


def join_heads(parts):
    pieces = len(parts)
    rows, wide = parts[0].shape[0], parts[0].shape[1] // 2
    return pl.pallas_call(
        functools.partial(join_heads_kernel, pieces, wide),
        out_shape=[jax.ShapeDtypeStruct((rows, wide * pieces), parts[0].dtype)] * 2,
        in_specs=[VMEM] * pieces,
        out_specs=[VMEM] * 2,
        compiler_params=SMALL,
    )(*parts)


def prepare_kernel(pieces, wide, lengths_ref, both_ref, *out_refs):
    piece_refs, marks_ref = out_refs[:pieces], out_refs[pieces]
    split_heads_kernel(pieces, wide, both_ref, *piece_refs)
    total, docs = marks_ref.shape[0], lengths_ref.shape[0]
    lane = lax.broadcasted_iota(jnp.int32, (1, MARKS), 1)
    begins = jnp.zeros((1, MARKS), jnp.int32)
    ends = jnp.where(lane < docs, total, 0)
    end = jnp.int32(0)
    for number in range(docs):
        begins = jnp.where(lane == number, end, begins)
        end = end + lengths_ref[number]
        ends = jnp.where(lane == number, end, ends)

    def some_rows(step, _):
        rows = pl.ds(pl.multiple_of(step * KEY_ROWS, KEY_ROWS), KEY_ROWS)
        position = step * KEY_ROWS + lax.broadcasted_iota(jnp.int32, (KEY_ROWS, MARKS), 0)
        inside = (position >= begins) & (position < ends)
        marks_ref[rows, :] = jnp.where(inside, 1.0, 0.0).astype(jnp.bfloat16)
        return 0

    lax.fori_loop(0, total // KEY_ROWS, some_rows, 0)


def prepare(lengths, left, right, pieces, total):
    rows, wide = left.shape[0], left.shape[1] // pieces
    results = pl.pallas_call(
        functools.partial(prepare_kernel, pieces, wide),
        out_shape=[jax.ShapeDtypeStruct((rows, 2 * wide), left.dtype)] * pieces
        + [jax.ShapeDtypeStruct((total, MARKS), jnp.bfloat16)],
        in_specs=[SMEM, VMEM],
        out_specs=[VMEM] * (pieces + 1),
        compiler_params=SMALL,
    )(lengths, jnp.concatenate([left, right], axis=1))
    return results[:pieces], results[pieces]


KEY_ROWS = 256
BATCH = 4
MARKS = 128
HIDDEN = -(2.0**100)


def attention_kernel(cores, heads, tok, *refs):
    group = QH // KVH
    lanes = group * tok
    tile_rows = heads * tok
    kv_count = heads * cores * len(CHUNKS)
    lengths_ref, marks_ref, refs = refs[0], refs[1], refs[2:]
    docs = lengths_ref.shape[0]
    qd_refs, refs = refs[:KVH], refs[KVH:]
    kv_refs, refs = refs[:kv_count], refs[kv_count:]
    od_refs, refs = refs[:KVH], refs[KVH:]
    dkv_refs, refs = refs[: cores * len(CHUNKS)], refs[cores * len(CHUNKS) :]
    k_all, v_all, q_wide, g_all, dk_acc, dv_acc, score, prob, tops, acc, table = refs
    scaling = HD ** (-0.5)
    log_scale = scaling * math.log2(math.e)
    f32, bf16 = jnp.float32, jnp.bfloat16

    ctx_index, head_index = lax.axis_index("ctx"), lax.axis_index("head")
    part, core = ctx_index // cores, ctx_index % cores

    def rows_of(head_flip, core_flip, part_flip):
        tile = (part ^ part_flip) * cores + (core ^ core_flip)
        return pl.ds(pl.multiple_of((tile * heads + (head_index ^ head_flip)) * tok, tok), tok)

    for chunk_number, chunk in enumerate(CHUNKS):
        for number in range(heads * cores):
            kv_ref = kv_refs[chunk_number * heads * cores + number]
            for place, flip in enumerate(chunk):
                rows = rows_of(number // cores, number % cores, flip)
                k_all[rows, :] = kv_ref[place, :, :HD]
                v_all[rows, :] = kv_ref[place, :, HD:]
    feature = lax.broadcasted_iota(jnp.int32, (tok, MARKS), 1)
    for flip, qd_ref in enumerate(qd_refs):
        own_marks = marks_ref[rows_of(0, 0, flip), :].astype(f32)
        bias = jnp.where(feature < docs, (1.0 - own_marks) * HIDDEN, 0.0).astype(bf16)
        for member in range(group):
            rows = slice(member * tok, (member + 1) * tok)
            q_wide[flip, rows, :HD] = qd_ref[:, member * HD : (member + 1) * HD]
            q_wide[flip, rows, HD:] = bias
            g_all[flip, rows, :] = qd_ref[:, (group + member) * HD : (group + member + 1) * HD]
    dk_acc[...] = jnp.zeros_like(dk_acc)
    dv_acc[...] = jnp.zeros_like(dv_acc)
    tops[...] = jnp.full_like(tops, NEG_FILL)
    acc[...] = jnp.zeros_like(acc)

    def entry(number, flip, row, limit):
        table[0, number] = flip
        table[1, number] = row
        table[2, number] = limit

    total = jnp.int32(0)
    for flip in range(KVH):
        first = ((part ^ flip) * cores + core) * tile_rows + head_index * tok
        end, low = jnp.int32(0), jnp.int32(0)
        for number in range(docs):
            length = lengths_ref[number]
            end = end + length
            low = low + jnp.where(end <= first, length, 0)
        count = (first + tok - low // tok * tok + KEY_ROWS - 1) // KEY_ROWS
        begin = jnp.maximum(first + tok - count * KEY_ROWS, 0)

        def listed(step, _, flip=flip, first=first, begin=begin, total=total):
            row = begin + step * KEY_ROWS
            entry(total + step, flip, row, first - row)
            return 0

        lax.fori_loop(0, count, listed, 0)
        total = total + count
    for spare in range(BATCH - 1):
        entry(total + spare, 0, 0, -(1 << 20))
    rounds = (total + 1) // BATCH
    left_over = (total - rounds * BATCH + 1) // 2

    def sweep(body):
        def one_round(number, _):
            body([number * BATCH + place for place in range(BATCH)])
            return 0

        def one_pair(number, _):
            body([rounds * BATCH + number * 2 + place for place in range(2)])
            return 0

        lax.fori_loop(0, rounds, one_round, 0)
        lax.fori_loop(0, left_over, one_pair, 0)

    def key_rows(item):
        return pl.ds(pl.multiple_of(table[1, item], tok), KEY_ROWS)

    def score_rows(item):
        return pl.ds(pl.multiple_of(item * KEY_ROWS, KEY_ROWS), KEY_ROWS)

    def wide(ref, rows):
        return jnp.concatenate([ref[rows, :], marks_ref[rows, :]], axis=1)

    key_row = lax.broadcasted_iota(jnp.int32, (KEY_ROWS, lanes), 0)
    query_row = lax.broadcasted_iota(jnp.int32, (1, lanes), 1) % tok

    def scores_round(items):
        raws = [
            lax.dot_general(
                wide(k_all, key_rows(item)),
                q_wide[table[0, item]],
                CONTRACT_LAST,
                preferred_element_type=f32,
            )
            for item in items
        ]
        for item, raw in zip(items, raws):
            raw = jnp.where(key_row <= query_row + table[2, item], raw, NEG_FILL)
            score[score_rows(item), :] = raw
            flip = table[0, item]
            tops[flip] = jnp.maximum(
                tops[flip], jnp.max(raw.reshape(KEY_ROWS // 8, 8, lanes), axis=0)
            )

    sweep(scores_round)
    for flip in range(KVH):
        tops[flip] = jnp.broadcast_to(jnp.max(tops[flip], axis=0, keepdims=True), (8, lanes))

    ones = jnp.ones((acc.shape[1] - HD, KEY_ROWS), bf16)

    def out_round(items):
        weights = [
            jnp.exp2((score[score_rows(item), :] - tops[table[0, item], :1]) * log_scale).astype(bf16)
            for item in items
        ]
        for item, weight in zip(items, weights):
            prob[score_rows(item), :] = weight
        parts = [
            jnp.dot(
                jnp.concatenate([v_all[key_rows(item), :].T, ones], axis=0),
                weight,
                preferred_element_type=f32,
            )
            for item, weight in zip(items, weights)
        ]
        for item, value in zip(items, parts):
            acc[table[0, item]] += value

    sweep(out_round)
    for flip in range(KVH):
        inverse = 1.0 / acc[flip, HD : HD + 1, :]
        turned = (acc[flip, :HD, :] * inverse).astype(bf16)
        out = turned.T
        g_turned = g_all[flip].T.astype(f32)
        delta = jnp.sum(turned.astype(f32) * g_turned, axis=0, keepdims=True)
        acc[flip, HD : HD + 1, :] = inverse
        acc[flip, HD + 1 : HD + 2, :] = delta
        acc[flip, :HD, :] = jnp.zeros((HD, lanes), f32)
        for member in range(group):
            rows = slice(member * tok, (member + 1) * tok)
            od_refs[flip][:, member * HD : (member + 1) * HD] = out[rows, :]

    def grad_round(items):
        slopes = [
            lax.dot_general(
                v_all[key_rows(item), :],
                g_all[table[0, item]],
                CONTRACT_LAST,
                preferred_element_type=f32,
            )
            for item in items
        ]
        probs = [
            prob[score_rows(item), :].astype(f32) * acc[table[0, item], HD : HD + 1, :]
            for item in items
        ]
        weights = [value.astype(bf16) for value in probs]
        score_grads = [
            (value * (slope - acc[table[0, item], HD + 1 : HD + 2, :])).astype(bf16)
            for item, value, slope in zip(items, probs, slopes)
        ]
        for item, weight, score_grad in zip(items, weights, score_grads):
            flip, rows = table[0, item], key_rows(item)
            dv_acc[rows, :] += jnp.dot(weight, g_all[flip], preferred_element_type=f32)
            dk_acc[rows, :] += jnp.dot(score_grad, q_wide[flip, :, :HD], preferred_element_type=f32)
            acc[flip, :HD, :] += lax.dot_general(
                k_all[rows, :], score_grad, CONTRACT_FIRST, preferred_element_type=f32
            )

    sweep(grad_round)

    for flip, od_ref in enumerate(od_refs):
        turned = (acc[flip, :HD, :] * scaling).astype(bf16).T
        for member in range(group):
            rows = slice(member * tok, (member + 1) * tok)
            od_ref[:, (group + member) * HD : (group + member + 1) * HD] = turned[rows, :]
    for chunk_number, chunk in enumerate(CHUNKS):
        for core_flip in range(cores):
            dkv_ref = dkv_refs[chunk_number * cores + core_flip]
            for head_flip in range(heads):
                for place, flip in enumerate(chunk):
                    rows = rows_of(head_flip, core_flip, flip)
                    dkv_ref[head_flip, place, :, :HD] = (dk_acc[rows, :] * scaling).astype(bf16)
                    dkv_ref[head_flip, place, :, HD:] = dv_acc[rows, :].astype(bf16)


def attention(lengths, marks, qd, kv, cores, heads):
    tok, group = qd[0].shape[0], QH // KVH
    total = KVH * cores * heads * tok
    lanes = group * tok
    reach = REACH * heads * tok
    pair = sum(-(-(keys + tok) // KEY_ROWS) for keys in (reach, reach // 2))
    items = -(-KVH // 2 * pair // BATCH) * BATCH
    bf16, f32 = jnp.bfloat16, jnp.float32
    results = pl.pallas_call(
        functools.partial(attention_kernel, cores, heads, tok),
        out_shape=[jax.ShapeDtypeStruct(a.shape, a.dtype) for a in qd]
        + [
            jax.ShapeDtypeStruct((heads, len(chunk), tok, 2 * HD), bf16)
            for chunk in CHUNKS
            for _ in range(cores)
        ],
        in_specs=[SMEM] + [VMEM] * (1 + len(qd) + len(kv)),
        out_specs=[VMEM] * (len(qd) + cores * len(CHUNKS)),
        scratch_shapes=[
            pltpu.VMEM((total, HD), bf16),
            pltpu.VMEM((total, HD), bf16),
            pltpu.VMEM((KVH, lanes, HD + MARKS), bf16),
            pltpu.VMEM((KVH, lanes, HD), bf16),
            pltpu.VMEM((total, HD), f32),
            pltpu.VMEM((total, HD), f32),
            pltpu.VMEM((items * KEY_ROWS, lanes), f32),
            pltpu.VMEM((items * KEY_ROWS, lanes), bf16),
            pltpu.VMEM((KVH, 8, lanes), f32),
            pltpu.VMEM((KVH, HD + 16, lanes), f32),
            pltpu.SMEM((3, items + BATCH), jnp.int32),
        ],
        compiler_params=pltpu.CompilerParams(vmem_limit_bytes=36 * 1024 * 1024),
    )(lengths, marks, *qd, *kv)
    return results[: len(qd)], results[len(qd) :]


def part_shards(queries, keys, values, d_out, lengths):
    heads, ctx = lax.axis_size("head"), lax.axis_size("ctx")
    cores = ctx // KVH
    total = queries.shape[0] * heads * ctx
    together = lax.optimization_barrier

    def over_part(piece, flip):
        return flipped(piece, flip * cores, 0)

    def exchange(pieces):
        return [pieces[0]] + [over_part(piece, s + 1) for s, piece in enumerate(pieces[1:])]

    def summed(*terms):
        return sum(term.astype(jnp.float32) for term in terms).astype(jnp.bfloat16)

    kv_pieces = split_heads(keys, values, KVH)
    far_own = flipped(kv_pieces[0][None], 0, 2)
    kv_pieces = exchange(kv_pieces)
    kv_mine = jnp.stack(kv_pieces)
    far_rest = flipped(jnp.stack(kv_pieces[1:]), 0, 2)
    far = jnp.concatenate([far_own, far_rest])
    qd, marks = prepare(lengths, queries, d_out, KVH, total)
    qd = exchange(qd)
    near = flipped(kv_mine, 0, 1)
    kv = []
    for piece in (kv_mine, near, far, flipped(far, 0, 1)):
        kv += [piece, flipped(piece, 1, 0)]
    od, dkv = attention(lengths, marks, qd, kv, cores, heads)

    both = (dkv[0], flipped(dkv[1], 1, 0))
    third_rest = flipped(summed(*(term[3, 1:] for term in both)), 0, 1)
    first, last, _ = together(
        (
            summed(*(term[1] for term in both)),
            summed(*(term[3, 0] for term in both)),
            third_rest,
        )
    )
    first, third_own, rest, od_moved = together(
        (
            flipped(first, 0, 1),
            flipped(last, 0, 1),
            flipped(summed(*(term[2, 1:] for term in both), third_rest), 0, 2),
            exchange(od)[1:],
        )
    )
    own, grads = together(
        (
            summed(*(term[2, 0] for term in both), third_own),
            [summed(*(term[0, s] for term in both), first[s], rest[s - 1]) for s in (1, 2, 3)],
        )
    )
    own = flipped(own, 0, 2)
    grads = [over_part(grad, s + 1) for s, grad in enumerate(grads)]
    attn_out, grad_queries = join_heads([od[0], *od_moved])
    grads = [summed(*(term[0, 0] for term in both), first[0], own), *grads]
    grad_keys, grad_values = join_heads(grads)
    return attn_out, grad_queries, grad_keys, grad_values


def solution(mesh):
    ctx_dev, head_dev = mesh.shape["ctx"], mesh.shape["head"]
    local = part_shards if ctx_dev == 2 * KVH and head_dev == 4 else shards
    rows = P(("ctx", "head"), None)
    return jax.shard_map(
        local,
        mesh=mesh,
        in_specs=(rows, rows, rows, rows, P()),
        out_specs=(rows, rows, rows, rows),
        check_vma=False,
    )
```

```python
import functools
import math

import jax
import jax.numpy as jnp
from jax import lax
from jax.experimental import pallas as pl
from jax.experimental.pallas import tpu as pltpu
from jax.sharding import PartitionSpec as P

QH = 16
KVH = 4
HD = 128
REACH = 4


NEG_FILL = -1e30


def shifted(value, axis, steps):
    count = lax.axis_size(axis)
    first, last = (max(0, -steps), min(count, count - steps))
    return lax.ppermute(value, axis, [(source, source + steps) for source in range(first, last)])


def doc_starts(lengths, first, count):
    doc_ends = jnp.cumsum(lengths)
    positions = first + jnp.arange(count, dtype=jnp.int32)
    passed = doc_ends[None, :] <= positions[:, None]
    return jnp.sum(jnp.where(passed, lengths[None, :], 0), axis=1)


def visible_pairs(query_first, key_first, start_rows, block_rows):
    query_pos = query_first + jnp.arange(block_rows, dtype=jnp.int32)
    key_pos = key_first + jnp.arange(block_rows, dtype=jnp.int32)
    mask = (key_pos[None, :] <= query_pos[:, None]) & (key_pos[None, :] >= start_rows[:, None])
    return mask[:, None, None, :]


def block_live(query_first, key_first, tile_starts, tile_first, block_rows):
    lowest = jnp.maximum(query_first, key_first)
    picked = jnp.clip(lowest - tile_first, 0, tile_starts.shape[0] - 1)
    first_start = lax.dynamic_index_in_dim(tile_starts, picked, 0, keepdims=False)
    return (lowest <= query_first + block_rows - 1) & (first_start <= key_first + block_rows - 1)


def shards(queries, keys, values, d_out, lengths):
    heads_dev = lax.axis_size("head")
    tok_dev = queries.shape[0]
    copies = max(1, heads_dev // KVH)
    kv_local = max(1, KVH // heads_dev)
    q_local = QH // heads_dev
    group_size = q_local // kv_local
    scaling = HD ** (-0.5)

    def spread(array_in):
        if copies > 1:
            return jnp.repeat(array_in.reshape(tok_dev, KVH, HD), copies, axis=1).reshape(
                tok_dev, KVH * copies * HD
            )
        return array_in

    q_tile, k_tile, v_tile = (
        lax.all_to_all(queries, "head", split_axis=1, concat_axis=0, tiled=True),
        lax.all_to_all(spread(keys), "head", split_axis=1, concat_axis=0, tiled=True),
        lax.all_to_all(spread(values), "head", split_axis=1, concat_axis=0, tiled=True),
    )
    tile_rows = q_tile.shape[0]
    block_rows = min(1024, tile_rows)
    block_count = tile_rows // block_rows
    ctx_index = lax.axis_index("ctx")
    tile_first = ctx_index * tile_rows
    tile_starts = doc_starts(lengths, tile_first, tile_rows)
    query_blocks = [
        q_tile[number * block_rows : (number + 1) * block_rows].reshape(
            block_rows, kv_local, group_size, HD
        )
        for number in range(block_count)
    ]
    start_blocks = [
        tile_starts[number * block_rows : (number + 1) * block_rows]
        for number in range(block_count)
    ]
    query_firsts = [tile_first + number * block_rows for number in range(block_count)]
    key_pair = jnp.stack([k_tile, v_tile])
    key_tiles = [key_pair]
    moving = key_pair
    for offset in range(1, REACH + 1):
        moving = shifted(moving, "ctx", 1)
        key_tiles.append(moving)

    def split_keys(tile_pair):
        key_list = [
            tile_pair[0, number * block_rows : (number + 1) * block_rows].reshape(
                block_rows, kv_local, HD
            )
            for number in range(block_count)
        ]
        value_list = [
            tile_pair[1, number * block_rows : (number + 1) * block_rows].reshape(
                block_rows, kv_local, HD
            )
            for number in range(block_count)
        ]
        return (key_list, value_list)

    states = [
        (
            jnp.full((block_rows, kv_local, group_size), NEG_FILL, jnp.float32),
            jnp.zeros((block_rows, kv_local, group_size), jnp.float32),
            jnp.zeros((block_rows, kv_local, group_size, HD), jnp.float32),
        )
        for number in range(block_count)
    ]
    for offset in range(REACH + 1):
        key_list, value_list = split_keys(key_tiles[offset])
        key_start = (ctx_index - offset) * tile_rows
        for query_number in range(block_count):
            query_block = query_blocks[query_number]
            query_first = query_firsts[query_number]
            start_rows = start_blocks[query_number]
            for key_number in range(block_count):
                key_block = key_list[key_number]
                value_block = value_list[key_number]
                key_first = key_start + key_number * block_rows

                def forward_block(
                    current,
                    query_block=query_block,
                    query_first=query_first,
                    start_rows=start_rows,
                    key_block=key_block,
                    value_block=value_block,
                    key_first=key_first,
                ):
                    max_old, sum_old, acc_old = current
                    mask = visible_pairs(query_first, key_first, start_rows, block_rows)
                    scores = (
                        jnp.einsum(
                            "qkgd,ckd->qkgc",
                            query_block,
                            key_block,
                            preferred_element_type=jnp.float32,
                        )
                        * scaling
                    )
                    scores = jnp.where(mask, scores, NEG_FILL)
                    max_new = jnp.maximum(max_old, jnp.max(scores, axis=-1))
                    prob_raw = jnp.where(mask, jnp.exp(scores - max_new[..., None]), 0.0)
                    rescale = jnp.exp(max_old - max_new)
                    sum_new = sum_old * rescale + jnp.sum(prob_raw, axis=-1)
                    acc_new = acc_old * rescale[..., None] + jnp.einsum(
                        "qkgc,ckd->qkgd",
                        prob_raw.astype(jnp.bfloat16),
                        value_block,
                        preferred_element_type=jnp.float32,
                    )
                    return (max_new, sum_new, acc_new)

                live = block_live(query_first, key_first, tile_starts, tile_first, block_rows)
                states[query_number] = lax.cond(
                    live, forward_block, lambda unchanged: unchanged, states[query_number]
                )
    out_blocks = [(state[2] / state[1][..., None]).astype(jnp.bfloat16) for state in states]
    lse_blocks = [state[0] + jnp.log(state[1]) for state in states]
    grad_tile = lax.all_to_all(d_out, "head", split_axis=1, concat_axis=0, tiled=True)
    grad_blocks = [
        grad_tile[number * block_rows : (number + 1) * block_rows].reshape(
            block_rows, kv_local, group_size, HD
        )
        for number in range(block_count)
    ]
    delta_blocks = [
        jnp.sum(
            grad_blocks[number].astype(jnp.float32) * out_blocks[number].astype(jnp.float32),
            axis=-1,
        )
        for number in range(block_count)
    ]
    query_totals = [
        jnp.zeros((block_rows, kv_local, group_size, HD), jnp.float32)
        for number in range(block_count)
    ]
    partial_grads = []
    for offset in range(REACH + 1):
        key_list, value_list = split_keys(key_tiles[offset])
        key_start = (ctx_index - offset) * tile_rows
        key_sums = [
            jnp.zeros((block_rows, kv_local, HD), jnp.float32) for number in range(block_count)
        ]
        value_sums = [
            jnp.zeros((block_rows, kv_local, HD), jnp.float32) for number in range(block_count)
        ]
        for query_number in range(block_count):
            query_block = query_blocks[query_number]
            grad_block = grad_blocks[query_number]
            query_first = query_firsts[query_number]
            start_rows = start_blocks[query_number]
            lse_rows = lse_blocks[query_number]
            delta_rows = delta_blocks[query_number]
            for key_number in range(block_count):
                key_block = key_list[key_number]
                value_block = value_list[key_number]
                key_first = key_start + key_number * block_rows

                def backward_block(
                    current,
                    query_block=query_block,
                    grad_block=grad_block,
                    query_first=query_first,
                    start_rows=start_rows,
                    lse_rows=lse_rows,
                    delta_rows=delta_rows,
                    key_block=key_block,
                    value_block=value_block,
                    key_first=key_first,
                ):
                    query_grad, key_grad, value_grad = current
                    mask = visible_pairs(query_first, key_first, start_rows, block_rows)
                    scores = (
                        jnp.einsum(
                            "qkgd,ckd->qkgc",
                            query_block,
                            key_block,
                            preferred_element_type=jnp.float32,
                        )
                        * scaling
                    )
                    prob_raw = jnp.where(mask, jnp.exp(scores - lse_rows[..., None]), 0.0)
                    weights = prob_raw.astype(jnp.bfloat16)
                    value_grad = value_grad + jnp.einsum(
                        "qkgc,qkgd->ckd", weights, grad_block, preferred_element_type=jnp.float32
                    )
                    prob_grad = jnp.einsum(
                        "qkgd,ckd->qkgc",
                        grad_block,
                        value_block,
                        preferred_element_type=jnp.float32,
                    )
                    score_grad = (prob_raw * (prob_grad - delta_rows[..., None]) * scaling).astype(
                        jnp.bfloat16
                    )
                    query_grad = query_grad + jnp.einsum(
                        "qkgc,ckd->qkgd", score_grad, key_block, preferred_element_type=jnp.float32
                    )
                    key_grad = key_grad + jnp.einsum(
                        "qkgc,qkgd->ckd",
                        score_grad,
                        query_block,
                        preferred_element_type=jnp.float32,
                    )
                    return (query_grad, key_grad, value_grad)

                live = block_live(query_first, key_first, tile_starts, tile_first, block_rows)
                current = (query_totals[query_number], key_sums[key_number], value_sums[key_number])
                query_totals[query_number], key_sums[key_number], value_sums[key_number] = lax.cond(
                    live, backward_block, lambda unchanged: unchanged, current
                )
        key_whole = jnp.concatenate(key_sums, axis=0).reshape(tile_rows, kv_local * HD)
        value_whole = jnp.concatenate(value_sums, axis=0).reshape(tile_rows, kv_local * HD)
        partial_grads.append(jnp.stack([key_whole, value_whole]))
    grad_total = partial_grads[REACH]
    for offset in range(REACH - 1, -1, -1):
        grad_total = (
            shifted(grad_total.astype(jnp.bfloat16), "ctx", -1).astype(grad_total.dtype)
            + partial_grads[offset]
        )
    out_tile = jnp.concatenate(out_blocks, axis=0).reshape(tile_rows, q_local * HD)
    query_tile = (
        jnp.concatenate(query_totals, axis=0).reshape(tile_rows, q_local * HD).astype(jnp.bfloat16)
    )
    attn_out, grad_queries = (
        lax.all_to_all(out_tile, "head", split_axis=0, concat_axis=1, tiled=True),
        lax.all_to_all(query_tile, "head", split_axis=0, concat_axis=1, tiled=True),
    )
    token_grads = lax.all_to_all(
        grad_total.astype(jnp.bfloat16), "head", split_axis=1, concat_axis=2, tiled=True
    ).astype(grad_total.dtype)
    if copies > 1:
        token_grads = jnp.sum(token_grads.reshape(2, tok_dev, KVH, copies, HD), axis=3).reshape(
            2, tok_dev, KVH * HD
        )
    token_grads = token_grads.astype(jnp.bfloat16)
    return (attn_out, grad_queries, token_grads[0], token_grads[1])


CHUNKS = ((0, 1, 2, 3),)
CONTRACT_LAST = (((1,), (1,)), ((), ()))
CONTRACT_FIRST = (((0,), (0,)), ((), ()))
VMEM = pl.BlockSpec(memory_space=pltpu.VMEM)
SMEM = pl.BlockSpec(memory_space=pltpu.SMEM)
SMALL = pltpu.CompilerParams(vmem_limit_bytes=8 * 1024 * 1024)


def flipped(value, ctx_bits, head_bits):
    ctx, heads = lax.axis_size("ctx"), lax.axis_size("head")
    pairs = [
        (c * heads + h, (c ^ ctx_bits) * heads + (h ^ head_bits))
        for c in range(ctx)
        for h in range(heads)
    ]
    return lax.ppermute(value, ("ctx", "head"), pairs)


def piece_columns(pieces, flip, wide, offset=0):
    index = lax.axis_index("ctx") // (lax.axis_size("ctx") // pieces)
    return pl.ds(pl.multiple_of(((index ^ flip) + offset) * wide, HD), wide)


def split_heads_kernel(pieces, wide, both_ref, *piece_refs):
    for flip, piece_ref in enumerate(piece_refs):
        for side in range(2):
            columns = piece_columns(pieces, flip, wide, side * pieces)
            piece_ref[:, side * wide : (side + 1) * wide] = both_ref[:, columns]


def join_heads_kernel(pieces, wide, *refs):
    piece_refs, (left_ref, right_ref) = refs[:pieces], refs[pieces:]
    for flip, piece_ref in enumerate(piece_refs):
        columns = piece_columns(pieces, flip, wide)
        left_ref[:, columns] = piece_ref[:, :wide]
        right_ref[:, columns] = piece_ref[:, wide:]


def split_heads(left, right, pieces):
    rows, wide = left.shape[0], left.shape[1] // pieces
    return pl.pallas_call(
        functools.partial(split_heads_kernel, pieces, wide),
        out_shape=[jax.ShapeDtypeStruct((rows, 2 * wide), left.dtype)] * pieces,
        in_specs=[VMEM],
        out_specs=[VMEM] * pieces,
        compiler_params=SMALL,
    )(jnp.concatenate([left, right], axis=1))


def join_heads(parts):
    pieces = len(parts)
    rows, wide = parts[0].shape[0], parts[0].shape[1] // 2
    return pl.pallas_call(
        functools.partial(join_heads_kernel, pieces, wide),
        out_shape=[jax.ShapeDtypeStruct((rows, wide * pieces), parts[0].dtype)] * 2,
        in_specs=[VMEM] * pieces,
        out_specs=[VMEM] * 2,
        compiler_params=SMALL,
    )(*parts)


def prepare_kernel(pieces, wide, lengths_ref, both_ref, *out_refs):
    piece_refs, marks_ref = out_refs[:pieces], out_refs[pieces]
    split_heads_kernel(pieces, wide, both_ref, *piece_refs)
    total, docs = marks_ref.shape[0], lengths_ref.shape[0]
    lane = lax.broadcasted_iota(jnp.int32, (1, MARKS), 1)
    ends = jnp.zeros((1, MARKS), jnp.int32)
    end = jnp.int32(0)
    for number in range(docs):
        end = end + lengths_ref[number]
        ends = jnp.where(lane == number, end, ends)

    def some_rows(step, _):
        rows = pl.ds(pl.multiple_of(step * KEY_ROWS, KEY_ROWS), KEY_ROWS)
        position = step * KEY_ROWS + lax.broadcasted_iota(jnp.int32, (KEY_ROWS, MARKS), 0)
        marks_ref[rows, :] = jnp.where(position < ends, 1.0, 0.0).astype(jnp.bfloat16)
        return 0

    lax.fori_loop(0, total // KEY_ROWS, some_rows, 0)


def prepare(lengths, left, right, pieces, total):
    rows, wide = left.shape[0], left.shape[1] // pieces
    results = pl.pallas_call(
        functools.partial(prepare_kernel, pieces, wide),
        out_shape=[jax.ShapeDtypeStruct((rows, 2 * wide), left.dtype)] * pieces
        + [jax.ShapeDtypeStruct((total, MARKS), jnp.bfloat16)],
        in_specs=[SMEM, VMEM],
        out_specs=[VMEM] * (pieces + 1),
        compiler_params=SMALL,
    )(lengths, jnp.concatenate([left, right], axis=1))
    return results[:pieces], results[pieces]


KEY_ROWS = 256
BATCH = 6
MARKS = 128
HIDDEN = -(2.0**100)


def attention_kernel(cores, heads, tok, *refs):
    group = QH // KVH
    lanes = group * tok
    tile_rows = heads * tok
    kv_count = heads * cores * len(CHUNKS)
    lengths_ref, marks_ref, refs = refs[0], refs[1], refs[2:]
    docs = lengths_ref.shape[0]
    qd_refs, refs = refs[:KVH], refs[KVH:]
    kv_refs, refs = refs[:kv_count], refs[kv_count:]
    od_refs, refs = refs[:KVH], refs[KVH:]
    dkv_refs, refs = refs[: cores * len(CHUNKS)], refs[cores * len(CHUNKS) :]
    k_all, v_all, q_wide, g_all, dk_acc, dv_acc, score, prob, tops, acc, table = refs
    scaling = HD ** (-0.5)
    log_scale = scaling * math.log2(math.e)
    f32, bf16 = jnp.float32, jnp.bfloat16

    ctx_index, head_index = lax.axis_index("ctx"), lax.axis_index("head")
    part, core = ctx_index // cores, ctx_index % cores

    def rows_of(head_flip, core_flip, part_flip):
        tile = (part ^ part_flip) * cores + (core ^ core_flip)
        return pl.ds(pl.multiple_of((tile * heads + (head_index ^ head_flip)) * tok, tok), tok)

    for chunk_number, chunk in enumerate(CHUNKS):
        for number in range(heads * cores):
            kv_ref = kv_refs[chunk_number * heads * cores + number]
            for place, flip in enumerate(chunk):
                rows = rows_of(number // cores, number % cores, flip)
                k_all[rows, :] = kv_ref[place, :, :HD]
                v_all[rows, :] = kv_ref[place, :, HD:]
    feature = lax.broadcasted_iota(jnp.int32, (tok, MARKS), 1)
    for flip, qd_ref in enumerate(qd_refs):
        own_marks = marks_ref[rows_of(0, 0, flip), :].astype(f32)
        bias = jnp.where(feature < docs, (1.0 - own_marks) * HIDDEN, 0.0).astype(bf16)
        for member in range(group):
            rows = slice(member * tok, (member + 1) * tok)
            q_wide[flip, rows, :HD] = qd_ref[:, member * HD : (member + 1) * HD]
            q_wide[flip, rows, HD:] = bias
            g_all[flip, rows, :] = qd_ref[:, (group + member) * HD : (group + member + 1) * HD]
    dk_acc[...] = jnp.zeros_like(dk_acc)
    dv_acc[...] = jnp.zeros_like(dv_acc)
    tops[...] = jnp.full_like(tops, NEG_FILL)
    acc[...] = jnp.zeros_like(acc)

    def entry(number, flip, row, limit):
        table[0, number] = flip
        table[1, number] = row
        table[2, number] = limit

    total = jnp.int32(0)
    for flip in range(KVH):
        first = ((part ^ flip) * cores + core) * tile_rows + head_index * tok
        end, low = jnp.int32(0), jnp.int32(0)
        for number in range(docs):
            length = lengths_ref[number]
            end = end + length
            low = low + jnp.where(end <= first, length, 0)
        count = (first + tok - low // tok * tok + KEY_ROWS - 1) // KEY_ROWS
        begin = jnp.maximum(first + tok - count * KEY_ROWS, 0)

        def listed(step, _, flip=flip, first=first, begin=begin, total=total):
            row = begin + step * KEY_ROWS
            entry(total + step, flip, row, first - row)
            return 0

        lax.fori_loop(0, count, listed, 0)
        total = total + count
    for spare in range(BATCH - 1):
        entry(total + spare, 0, 0, -(1 << 20))
    rounds = (total + 1) // BATCH
    left_over = (total - rounds * BATCH + 1) // 2

    def sweep(body):
        def one_round(number, _):
            body([number * BATCH + place for place in range(BATCH)])
            return 0

        def one_pair(number, _):
            body([rounds * BATCH + number * 2 + place for place in range(2)])
            return 0

        lax.fori_loop(0, rounds, one_round, 0)
        lax.fori_loop(0, left_over, one_pair, 0)

    def key_rows(item):
        return pl.ds(pl.multiple_of(table[1, item], tok), KEY_ROWS)

    def score_rows(item):
        return pl.ds(pl.multiple_of(item * KEY_ROWS, KEY_ROWS), KEY_ROWS)

    def wide(ref, rows):
        return jnp.concatenate([ref[rows, :], marks_ref[rows, :]], axis=1)

    key_row = lax.broadcasted_iota(jnp.int32, (KEY_ROWS, lanes), 0)
    query_row = lax.broadcasted_iota(jnp.int32, (1, lanes), 1) % tok

    def scores_round(items):
        raws = [
            lax.dot_general(
                wide(k_all, key_rows(item)),
                q_wide[table[0, item]],
                CONTRACT_LAST,
                preferred_element_type=f32,
            )
            for item in items
        ]
        for item, raw in zip(items, raws):
            raw = jnp.where(key_row <= query_row + table[2, item], raw, NEG_FILL)
            score[score_rows(item), :] = raw
            flip = table[0, item]
            tops[flip] = jnp.maximum(
                tops[flip], jnp.max(raw.reshape(KEY_ROWS // 8, 8, lanes), axis=0)
            )

    sweep(scores_round)
    for flip in range(KVH):
        tops[flip] = jnp.broadcast_to(jnp.max(tops[flip], axis=0, keepdims=True), (8, lanes))

    ones = jnp.ones((acc.shape[1] - HD, KEY_ROWS), bf16)

    def out_round(items):
        weights = [
            jnp.exp2((score[score_rows(item), :] - tops[table[0, item], :1]) * log_scale).astype(bf16)
            for item in items
        ]
        for item, weight in zip(items, weights):
            prob[score_rows(item), :] = weight
        parts = [
            jnp.dot(
                jnp.concatenate([v_all[key_rows(item), :].T, ones], axis=0),
                weight,
                preferred_element_type=f32,
            )
            for item, weight in zip(items, weights)
        ]
        for item, value in zip(items, parts):
            acc[table[0, item]] += value

    sweep(out_round)
    for flip in range(KVH):
        inverse = 1.0 / acc[flip, HD : HD + 1, :]
        turned = (acc[flip, :HD, :] * inverse).astype(bf16)
        out = turned.T
        g_turned = g_all[flip].T.astype(f32)
        delta = jnp.sum(turned.astype(f32) * g_turned, axis=0, keepdims=True)
        acc[flip, HD : HD + 1, :] = inverse
        acc[flip, HD + 1 : HD + 2, :] = delta
        acc[flip, :HD, :] = jnp.zeros((HD, lanes), f32)
        for member in range(group):
            rows = slice(member * tok, (member + 1) * tok)
            od_refs[flip][:, member * HD : (member + 1) * HD] = out[rows, :]

    def grad_round(items):
        slopes = [
            lax.dot_general(
                v_all[key_rows(item), :],
                g_all[table[0, item]],
                CONTRACT_LAST,
                preferred_element_type=f32,
            )
            for item in items
        ]
        probs = [
            prob[score_rows(item), :].astype(f32) * acc[table[0, item], HD : HD + 1, :]
            for item in items
        ]
        weights = [value.astype(bf16) for value in probs]
        score_grads = [
            (value * (slope - acc[table[0, item], HD + 1 : HD + 2, :])).astype(bf16)
            for item, value, slope in zip(items, probs, slopes)
        ]
        for item, weight, score_grad in zip(items, weights, score_grads):
            flip, rows = table[0, item], key_rows(item)
            dv_acc[rows, :] += jnp.dot(weight, g_all[flip], preferred_element_type=f32)
            dk_acc[rows, :] += jnp.dot(score_grad, q_wide[flip, :, :HD], preferred_element_type=f32)
            acc[flip, :HD, :] += lax.dot_general(
                k_all[rows, :], score_grad, CONTRACT_FIRST, preferred_element_type=f32
            )

    sweep(grad_round)

    for flip, od_ref in enumerate(od_refs):
        turned = (acc[flip, :HD, :] * scaling).astype(bf16).T
        for member in range(group):
            rows = slice(member * tok, (member + 1) * tok)
            od_ref[:, (group + member) * HD : (group + member + 1) * HD] = turned[rows, :]
    for chunk_number, chunk in enumerate(CHUNKS):
        for core_flip in range(cores):
            dkv_ref = dkv_refs[chunk_number * cores + core_flip]
            for head_flip in range(heads):
                for place, flip in enumerate(chunk):
                    rows = rows_of(head_flip, core_flip, flip)
                    dkv_ref[head_flip, place, :, :HD] = (dk_acc[rows, :] * scaling).astype(bf16)
                    dkv_ref[head_flip, place, :, HD:] = dv_acc[rows, :].astype(bf16)


def attention(lengths, marks, qd, kv, cores, heads):
    tok, group = qd[0].shape[0], QH // KVH
    total = KVH * cores * heads * tok
    lanes = group * tok
    reach = REACH * heads * tok
    pair = sum(-(-(keys + tok) // KEY_ROWS) for keys in (reach, reach // 2))
    items = KVH // 2 * pair
    bf16, f32 = jnp.bfloat16, jnp.float32
    results = pl.pallas_call(
        functools.partial(attention_kernel, cores, heads, tok),
        out_shape=[jax.ShapeDtypeStruct(a.shape, a.dtype) for a in qd]
        + [
            jax.ShapeDtypeStruct((heads, len(chunk), tok, 2 * HD), bf16)
            for chunk in CHUNKS
            for _ in range(cores)
        ],
        in_specs=[SMEM] + [VMEM] * (1 + len(qd) + len(kv)),
        out_specs=[VMEM] * (len(qd) + cores * len(CHUNKS)),
        scratch_shapes=[
            pltpu.VMEM((total, HD), bf16),
            pltpu.VMEM((total, HD), bf16),
            pltpu.VMEM((KVH, lanes, HD + MARKS), bf16),
            pltpu.VMEM((KVH, lanes, HD), bf16),
            pltpu.VMEM((total, HD), f32),
            pltpu.VMEM((total, HD), f32),
            pltpu.VMEM((items * KEY_ROWS, lanes), f32),
            pltpu.VMEM((items * KEY_ROWS, lanes), bf16),
            pltpu.VMEM((KVH, 8, lanes), f32),
            pltpu.VMEM((KVH, HD + 16, lanes), f32),
            pltpu.SMEM((3, items + BATCH), jnp.int32),
        ],
        compiler_params=pltpu.CompilerParams(vmem_limit_bytes=42 * 1024 * 1024),
    )(lengths, marks, *qd, *kv)
    return results[: len(qd)], results[len(qd) :]


def part_shards(queries, keys, values, d_out, lengths):
    heads, ctx = lax.axis_size("head"), lax.axis_size("ctx")
    cores = ctx // KVH
    total = queries.shape[0] * heads * ctx
    together = lax.optimization_barrier

    def over_part(piece, flip):
        return flipped(piece, flip * cores, 0)

    def exchange(pieces):
        return [pieces[0]] + [over_part(piece, s + 1) for s, piece in enumerate(pieces[1:])]

    def summed(*terms):
        return sum(term.astype(jnp.float32) for term in terms).astype(jnp.bfloat16)

    kv_pieces = split_heads(keys, values, KVH)
    far_own = flipped(kv_pieces[0][None], 0, 2)
    kv_pieces = exchange(kv_pieces)
    kv_mine = jnp.stack(kv_pieces)
    far_rest = flipped(jnp.stack(kv_pieces[1:]), 0, 2)
    far = jnp.concatenate([far_own, far_rest])
    qd, marks = prepare(lengths, queries, d_out, KVH, total)
    qd = exchange(qd)
    near = flipped(kv_mine, 0, 1)
    kv = []
    for piece in (kv_mine, near, far, flipped(far, 0, 1)):
        kv += [piece, flipped(piece, 1, 0)]
    od, dkv = attention(lengths, marks, qd, kv, cores, heads)

    both = (dkv[0], flipped(dkv[1], 1, 0))
    third_rest = flipped(summed(*(term[3, 1:] for term in both)), 0, 1)
    first, last, _ = together(
        (
            summed(*(term[1] for term in both)),
            summed(*(term[3, 0] for term in both)),
            third_rest,
        )
    )
    first, third_own, rest, od_moved = together(
        (
            flipped(first, 0, 1),
            flipped(last, 0, 1),
            flipped(summed(*(term[2, 1:] for term in both), third_rest), 0, 2),
            exchange(od)[1:],
        )
    )
    own, grads = together(
        (
            summed(*(term[2, 0] for term in both), third_own),
            [summed(*(term[0, s] for term in both), first[s], rest[s - 1]) for s in (1, 2, 3)],
        )
    )
    own = flipped(own, 0, 2)
    grads = [over_part(grad, s + 1) for s, grad in enumerate(grads)]
    attn_out, grad_queries = join_heads([od[0], *od_moved])
    grads = [summed(*(term[0, 0] for term in both), first[0], own), *grads]
    grad_keys, grad_values = join_heads(grads)
    return attn_out, grad_queries, grad_keys, grad_values


def solution(mesh):
    ctx_dev, head_dev = mesh.shape["ctx"], mesh.shape["head"]
    local = part_shards if ctx_dev == 2 * KVH and head_dev == 4 else shards
    rows = P(("ctx", "head"), None)
    return jax.shard_map(
        local,
        mesh=mesh,
        in_specs=(rows, rows, rows, rows, P()),
        out_specs=(rows, rows, rows, rows),
        check_vma=False,
    )
```

```python
import functools
import math

import jax
import jax.numpy as jnp
from jax import lax
from jax.experimental import pallas as pl
from jax.experimental.pallas import tpu as pltpu
from jax.sharding import PartitionSpec as P

QH = 16
KVH = 4
HD = 128
REACH = 4


NEG_FILL = -1e30


def shifted(value, axis, steps):
    count = lax.axis_size(axis)
    first, last = (max(0, -steps), min(count, count - steps))
    return lax.ppermute(value, axis, [(source, source + steps) for source in range(first, last)])


def doc_starts(lengths, first, count):
    doc_ends = jnp.cumsum(lengths)
    positions = first + jnp.arange(count, dtype=jnp.int32)
    passed = doc_ends[None, :] <= positions[:, None]
    return jnp.sum(jnp.where(passed, lengths[None, :], 0), axis=1)


def visible_pairs(query_first, key_first, start_rows, block_rows):
    query_pos = query_first + jnp.arange(block_rows, dtype=jnp.int32)
    key_pos = key_first + jnp.arange(block_rows, dtype=jnp.int32)
    mask = (key_pos[None, :] <= query_pos[:, None]) & (key_pos[None, :] >= start_rows[:, None])
    return mask[:, None, None, :]


def block_live(query_first, key_first, tile_starts, tile_first, block_rows):
    lowest = jnp.maximum(query_first, key_first)
    picked = jnp.clip(lowest - tile_first, 0, tile_starts.shape[0] - 1)
    first_start = lax.dynamic_index_in_dim(tile_starts, picked, 0, keepdims=False)
    return (lowest <= query_first + block_rows - 1) & (first_start <= key_first + block_rows - 1)


def shards(queries, keys, values, d_out, lengths):
    heads_dev = lax.axis_size("head")
    tok_dev = queries.shape[0]
    copies = max(1, heads_dev // KVH)
    kv_local = max(1, KVH // heads_dev)
    q_local = QH // heads_dev
    group_size = q_local // kv_local
    scaling = HD ** (-0.5)

    def spread(array_in):
        if copies > 1:
            return jnp.repeat(array_in.reshape(tok_dev, KVH, HD), copies, axis=1).reshape(
                tok_dev, KVH * copies * HD
            )
        return array_in

    q_tile, k_tile, v_tile = (
        lax.all_to_all(queries, "head", split_axis=1, concat_axis=0, tiled=True),
        lax.all_to_all(spread(keys), "head", split_axis=1, concat_axis=0, tiled=True),
        lax.all_to_all(spread(values), "head", split_axis=1, concat_axis=0, tiled=True),
    )
    tile_rows = q_tile.shape[0]
    block_rows = min(1024, tile_rows)
    block_count = tile_rows // block_rows
    ctx_index = lax.axis_index("ctx")
    tile_first = ctx_index * tile_rows
    tile_starts = doc_starts(lengths, tile_first, tile_rows)
    query_blocks = [
        q_tile[number * block_rows : (number + 1) * block_rows].reshape(
            block_rows, kv_local, group_size, HD
        )
        for number in range(block_count)
    ]
    start_blocks = [
        tile_starts[number * block_rows : (number + 1) * block_rows]
        for number in range(block_count)
    ]
    query_firsts = [tile_first + number * block_rows for number in range(block_count)]
    key_pair = jnp.stack([k_tile, v_tile])
    key_tiles = [key_pair]
    moving = key_pair
    for offset in range(1, REACH + 1):
        moving = shifted(moving, "ctx", 1)
        key_tiles.append(moving)

    def split_keys(tile_pair):
        key_list = [
            tile_pair[0, number * block_rows : (number + 1) * block_rows].reshape(
                block_rows, kv_local, HD
            )
            for number in range(block_count)
        ]
        value_list = [
            tile_pair[1, number * block_rows : (number + 1) * block_rows].reshape(
                block_rows, kv_local, HD
            )
            for number in range(block_count)
        ]
        return (key_list, value_list)

    states = [
        (
            jnp.full((block_rows, kv_local, group_size), NEG_FILL, jnp.float32),
            jnp.zeros((block_rows, kv_local, group_size), jnp.float32),
            jnp.zeros((block_rows, kv_local, group_size, HD), jnp.float32),
        )
        for number in range(block_count)
    ]
    for offset in range(REACH + 1):
        key_list, value_list = split_keys(key_tiles[offset])
        key_start = (ctx_index - offset) * tile_rows
        for query_number in range(block_count):
            query_block = query_blocks[query_number]
            query_first = query_firsts[query_number]
            start_rows = start_blocks[query_number]
            for key_number in range(block_count):
                key_block = key_list[key_number]
                value_block = value_list[key_number]
                key_first = key_start + key_number * block_rows

                def forward_block(
                    current,
                    query_block=query_block,
                    query_first=query_first,
                    start_rows=start_rows,
                    key_block=key_block,
                    value_block=value_block,
                    key_first=key_first,
                ):
                    max_old, sum_old, acc_old = current
                    mask = visible_pairs(query_first, key_first, start_rows, block_rows)
                    scores = (
                        jnp.einsum(
                            "qkgd,ckd->qkgc",
                            query_block,
                            key_block,
                            preferred_element_type=jnp.float32,
                        )
                        * scaling
                    )
                    scores = jnp.where(mask, scores, NEG_FILL)
                    max_new = jnp.maximum(max_old, jnp.max(scores, axis=-1))
                    prob_raw = jnp.where(mask, jnp.exp(scores - max_new[..., None]), 0.0)
                    rescale = jnp.exp(max_old - max_new)
                    sum_new = sum_old * rescale + jnp.sum(prob_raw, axis=-1)
                    acc_new = acc_old * rescale[..., None] + jnp.einsum(
                        "qkgc,ckd->qkgd",
                        prob_raw.astype(jnp.bfloat16),
                        value_block,
                        preferred_element_type=jnp.float32,
                    )
                    return (max_new, sum_new, acc_new)

                live = block_live(query_first, key_first, tile_starts, tile_first, block_rows)
                states[query_number] = lax.cond(
                    live, forward_block, lambda unchanged: unchanged, states[query_number]
                )
    out_blocks = [(state[2] / state[1][..., None]).astype(jnp.bfloat16) for state in states]
    lse_blocks = [state[0] + jnp.log(state[1]) for state in states]
    grad_tile = lax.all_to_all(d_out, "head", split_axis=1, concat_axis=0, tiled=True)
    grad_blocks = [
        grad_tile[number * block_rows : (number + 1) * block_rows].reshape(
            block_rows, kv_local, group_size, HD
        )
        for number in range(block_count)
    ]
    delta_blocks = [
        jnp.sum(
            grad_blocks[number].astype(jnp.float32) * out_blocks[number].astype(jnp.float32),
            axis=-1,
        )
        for number in range(block_count)
    ]
    query_totals = [
        jnp.zeros((block_rows, kv_local, group_size, HD), jnp.float32)
        for number in range(block_count)
    ]
    partial_grads = []
    for offset in range(REACH + 1):
        key_list, value_list = split_keys(key_tiles[offset])
        key_start = (ctx_index - offset) * tile_rows
        key_sums = [
            jnp.zeros((block_rows, kv_local, HD), jnp.float32) for number in range(block_count)
        ]
        value_sums = [
            jnp.zeros((block_rows, kv_local, HD), jnp.float32) for number in range(block_count)
        ]
        for query_number in range(block_count):
            query_block = query_blocks[query_number]
            grad_block = grad_blocks[query_number]
            query_first = query_firsts[query_number]
            start_rows = start_blocks[query_number]
            lse_rows = lse_blocks[query_number]
            delta_rows = delta_blocks[query_number]
            for key_number in range(block_count):
                key_block = key_list[key_number]
                value_block = value_list[key_number]
                key_first = key_start + key_number * block_rows

                def backward_block(
                    current,
                    query_block=query_block,
                    grad_block=grad_block,
                    query_first=query_first,
                    start_rows=start_rows,
                    lse_rows=lse_rows,
                    delta_rows=delta_rows,
                    key_block=key_block,
                    value_block=value_block,
                    key_first=key_first,
                ):
                    query_grad, key_grad, value_grad = current
                    mask = visible_pairs(query_first, key_first, start_rows, block_rows)
                    scores = (
                        jnp.einsum(
                            "qkgd,ckd->qkgc",
                            query_block,
                            key_block,
                            preferred_element_type=jnp.float32,
                        )
                        * scaling
                    )
                    prob_raw = jnp.where(mask, jnp.exp(scores - lse_rows[..., None]), 0.0)
                    weights = prob_raw.astype(jnp.bfloat16)
                    value_grad = value_grad + jnp.einsum(
                        "qkgc,qkgd->ckd", weights, grad_block, preferred_element_type=jnp.float32
                    )
                    prob_grad = jnp.einsum(
                        "qkgd,ckd->qkgc",
                        grad_block,
                        value_block,
                        preferred_element_type=jnp.float32,
                    )
                    score_grad = (prob_raw * (prob_grad - delta_rows[..., None]) * scaling).astype(
                        jnp.bfloat16
                    )
                    query_grad = query_grad + jnp.einsum(
                        "qkgc,ckd->qkgd", score_grad, key_block, preferred_element_type=jnp.float32
                    )
                    key_grad = key_grad + jnp.einsum(
                        "qkgc,qkgd->ckd",
                        score_grad,
                        query_block,
                        preferred_element_type=jnp.float32,
                    )
                    return (query_grad, key_grad, value_grad)

                live = block_live(query_first, key_first, tile_starts, tile_first, block_rows)
                current = (query_totals[query_number], key_sums[key_number], value_sums[key_number])
                query_totals[query_number], key_sums[key_number], value_sums[key_number] = lax.cond(
                    live, backward_block, lambda unchanged: unchanged, current
                )
        key_whole = jnp.concatenate(key_sums, axis=0).reshape(tile_rows, kv_local * HD)
        value_whole = jnp.concatenate(value_sums, axis=0).reshape(tile_rows, kv_local * HD)
        partial_grads.append(jnp.stack([key_whole, value_whole]))
    grad_total = partial_grads[REACH]
    for offset in range(REACH - 1, -1, -1):
        grad_total = (
            shifted(grad_total.astype(jnp.bfloat16), "ctx", -1).astype(grad_total.dtype)
            + partial_grads[offset]
        )
    out_tile = jnp.concatenate(out_blocks, axis=0).reshape(tile_rows, q_local * HD)
    query_tile = (
        jnp.concatenate(query_totals, axis=0).reshape(tile_rows, q_local * HD).astype(jnp.bfloat16)
    )
    attn_out, grad_queries = (
        lax.all_to_all(out_tile, "head", split_axis=0, concat_axis=1, tiled=True),
        lax.all_to_all(query_tile, "head", split_axis=0, concat_axis=1, tiled=True),
    )
    token_grads = lax.all_to_all(
        grad_total.astype(jnp.bfloat16), "head", split_axis=1, concat_axis=2, tiled=True
    ).astype(grad_total.dtype)
    if copies > 1:
        token_grads = jnp.sum(token_grads.reshape(2, tok_dev, KVH, copies, HD), axis=3).reshape(
            2, tok_dev, KVH * HD
        )
    token_grads = token_grads.astype(jnp.bfloat16)
    return (attn_out, grad_queries, token_grads[0], token_grads[1])


CHUNKS = ((0, 1, 2, 3),)
CONTRACT_LAST = (((1,), (1,)), ((), ()))
CONTRACT_FIRST = (((0,), (0,)), ((), ()))
VMEM = pl.BlockSpec(memory_space=pltpu.VMEM)
SMEM = pl.BlockSpec(memory_space=pltpu.SMEM)
SMALL = pltpu.CompilerParams(vmem_limit_bytes=8 * 1024 * 1024)


def flipped(value, ctx_bits, head_bits):
    ctx, heads = lax.axis_size("ctx"), lax.axis_size("head")
    pairs = [
        (c * heads + h, (c ^ ctx_bits) * heads + (h ^ head_bits))
        for c in range(ctx)
        for h in range(heads)
    ]
    return lax.ppermute(value, ("ctx", "head"), pairs)


def piece_columns(pieces, flip, wide, offset=0):
    index = lax.axis_index("ctx") // (lax.axis_size("ctx") // pieces)
    return pl.ds(pl.multiple_of(((index ^ flip) + offset) * wide, HD), wide)


def split_heads_kernel(pieces, wide, both_ref, *piece_refs):
    for flip, piece_ref in enumerate(piece_refs):
        for side in range(2):
            columns = piece_columns(pieces, flip, wide, side * pieces)
            piece_ref[:, side * wide : (side + 1) * wide] = both_ref[:, columns]


def join_heads_kernel(pieces, wide, *refs):
    piece_refs, (left_ref, right_ref) = refs[:pieces], refs[pieces:]
    for flip, piece_ref in enumerate(piece_refs):
        columns = piece_columns(pieces, flip, wide)
        left_ref[:, columns] = piece_ref[:, :wide]
        right_ref[:, columns] = piece_ref[:, wide:]


def split_heads(left, right, pieces):
    rows, wide = left.shape[0], left.shape[1] // pieces
    return pl.pallas_call(
        functools.partial(split_heads_kernel, pieces, wide),
        out_shape=[jax.ShapeDtypeStruct((rows, 2 * wide), left.dtype)] * pieces,
        in_specs=[VMEM],
        out_specs=[VMEM] * pieces,
        compiler_params=SMALL,
    )(jnp.concatenate([left, right], axis=1))


def join_heads(parts):
    pieces = len(parts)
    rows, wide = parts[0].shape[0], parts[0].shape[1] // 2
    return pl.pallas_call(
        functools.partial(join_heads_kernel, pieces, wide),
        out_shape=[jax.ShapeDtypeStruct((rows, wide * pieces), parts[0].dtype)] * 2,
        in_specs=[VMEM] * pieces,
        out_specs=[VMEM] * 2,
        compiler_params=SMALL,
    )(*parts)


def marks_kernel(lengths_ref, marks_ref):
    total, docs = marks_ref.shape[0], lengths_ref.shape[0]
    lane = lax.broadcasted_iota(jnp.int32, (1, MARKS), 1)
    ends = jnp.zeros((1, MARKS), jnp.int32)
    end = jnp.int32(0)
    for number in range(docs):
        end = end + lengths_ref[number]
        ends = jnp.where(lane == number, end, ends)

    def some_rows(step, _):
        rows = pl.ds(pl.multiple_of(step * 4 * KEY_ROWS, KEY_ROWS), 4 * KEY_ROWS)
        position = lax.broadcasted_iota(jnp.int32, (4 * KEY_ROWS, MARKS), 0)
        marks_ref[rows, :] = jnp.where(position < ends - step * 4 * KEY_ROWS, 1.0, 0.0).astype(jnp.bfloat16)
        return 0

    lax.fori_loop(0, total // (4 * KEY_ROWS), some_rows, 0)


def document_marks(lengths, total):
    return pl.pallas_call(
        marks_kernel,
        out_shape=jax.ShapeDtypeStruct((total, MARKS), jnp.bfloat16),
        in_specs=[SMEM],
        out_specs=VMEM,
        compiler_params=SMALL,
    )(lengths)


KEY_ROWS = 256
BATCH = 6
MARKS = 128
HIDDEN = -(2.0**100)


def attention_kernel(cores, heads, tok, *refs):
    group = QH // KVH
    lanes = group * tok
    tile_rows = heads * tok
    kv_count = heads * cores * len(CHUNKS)
    lengths_ref, marks_ref, refs = refs[0], refs[1], refs[2:]
    docs = lengths_ref.shape[0]
    qd_refs, refs = refs[:KVH], refs[KVH:]
    kv_refs, refs = refs[:kv_count], refs[kv_count:]
    od_refs, refs = refs[:KVH], refs[KVH:]
    dkv_refs, refs = refs[: cores * len(CHUNKS)], refs[cores * len(CHUNKS) :]
    k_all, v_all, q_wide, g_all, dk_acc, dv_acc, score, prob, tops, acc, table = refs
    scaling = HD ** (-0.5)
    log_scale = scaling * math.log2(math.e)
    f32, bf16 = jnp.float32, jnp.bfloat16

    ctx_index, head_index = lax.axis_index("ctx"), lax.axis_index("head")
    part, core = ctx_index // cores, ctx_index % cores

    def rows_of(head_flip, core_flip, part_flip):
        tile = (part ^ part_flip) * cores + (core ^ core_flip)
        return pl.ds(pl.multiple_of((tile * heads + (head_index ^ head_flip)) * tok, tok), tok)

    for chunk_number, chunk in enumerate(CHUNKS):
        for number in range(heads * cores):
            kv_ref = kv_refs[chunk_number * heads * cores + number]
            for place, flip in enumerate(chunk):
                rows = rows_of(number // cores, number % cores, flip)
                k_all[rows, :] = kv_ref[place, :, :HD]
                v_all[rows, :] = kv_ref[place, :, HD:]
    feature = lax.broadcasted_iota(jnp.int32, (tok, MARKS), 1)
    for flip, qd_ref in enumerate(qd_refs):
        own_marks = marks_ref[rows_of(0, 0, flip), :].astype(f32)
        bias = jnp.where(feature < docs, (1.0 - own_marks) * HIDDEN, 0.0).astype(bf16)
        for member in range(group):
            rows = slice(member * tok, (member + 1) * tok)
            q_wide[flip, rows, :HD] = qd_ref[:, member * HD : (member + 1) * HD]
            q_wide[flip, rows, HD:] = bias
            g_all[flip, rows, :] = qd_ref[:, (group + member) * HD : (group + member + 1) * HD]
    dk_acc[...] = jnp.zeros_like(dk_acc)
    dv_acc[...] = jnp.zeros_like(dv_acc)
    tops[...] = jnp.full_like(tops, NEG_FILL)
    acc[...] = jnp.zeros_like(acc)

    def entry(number, flip, row, limit):
        table[0, number] = flip
        table[1, number] = row
        table[2, number] = limit

    total = jnp.int32(0)
    for flip in range(KVH):
        first = ((part ^ flip) * cores + core) * tile_rows + head_index * tok
        end, low = jnp.int32(0), jnp.int32(0)
        for number in range(docs):
            length = lengths_ref[number]
            end = end + length
            low = low + jnp.where(end <= first, length, 0)
        count = (first + tok - low // tok * tok + KEY_ROWS - 1) // KEY_ROWS
        begin = jnp.maximum(first + tok - count * KEY_ROWS, 0)

        def listed(step, _, flip=flip, first=first, begin=begin, total=total):
            row = begin + step * KEY_ROWS
            entry(total + step, flip, row, first - row)
            return 0

        lax.fori_loop(0, count, listed, 0)
        total = total + count
    for spare in range(BATCH - 1):
        entry(total + spare, 0, 0, -(1 << 20))
    rounds = (total + 1) // BATCH
    left_over = (total - rounds * BATCH + 1) // 2

    def sweep(body):
        def one_round(number, _):
            body([number * BATCH + place for place in range(BATCH)])
            return 0

        def one_pair(number, _):
            body([rounds * BATCH + number * 2 + place for place in range(2)])
            return 0

        lax.fori_loop(0, rounds, one_round, 0)
        lax.fori_loop(0, left_over, one_pair, 0)

    def key_rows(item):
        return pl.ds(pl.multiple_of(table[1, item], tok), KEY_ROWS)

    def score_rows(item):
        return pl.ds(pl.multiple_of(item * KEY_ROWS, KEY_ROWS), KEY_ROWS)

    def wide(ref, rows):
        return jnp.concatenate([ref[rows, :], marks_ref[rows, :]], axis=1)

    key_row = lax.broadcasted_iota(jnp.int32, (KEY_ROWS, lanes), 0)
    query_row = lax.broadcasted_iota(jnp.int32, (1, lanes), 1) % tok

    def scores_round(items):
        raws = [
            lax.dot_general(
                wide(k_all, key_rows(item)),
                q_wide[table[0, item]],
                CONTRACT_LAST,
                preferred_element_type=f32,
            )
            for item in items
        ]
        for item, raw in zip(items, raws):
            raw = jnp.where(key_row <= query_row + table[2, item], raw, NEG_FILL)
            score[score_rows(item), :] = raw
            flip = table[0, item]
            tops[flip] = jnp.maximum(
                tops[flip], jnp.max(raw.reshape(KEY_ROWS // 8, 8, lanes), axis=0)
            )

    sweep(scores_round)
    for flip in range(KVH):
        tops[flip] = jnp.broadcast_to(jnp.max(tops[flip], axis=0, keepdims=True), (8, lanes))

    ones = jnp.ones((acc.shape[1] - HD, KEY_ROWS), bf16)

    def out_round(items):
        weights = [
            jnp.exp2((score[score_rows(item), :] - tops[table[0, item], :1]) * log_scale).astype(bf16)
            for item in items
        ]
        for item, weight in zip(items, weights):
            prob[score_rows(item), :] = weight
        parts = [
            jnp.dot(
                jnp.concatenate([v_all[key_rows(item), :].T, ones], axis=0),
                weight,
                preferred_element_type=f32,
            )
            for item, weight in zip(items, weights)
        ]
        for item, value in zip(items, parts):
            acc[table[0, item]] += value

    sweep(out_round)
    for flip in range(KVH):
        inverse = 1.0 / acc[flip, HD : HD + 1, :]
        turned = (acc[flip, :HD, :] * inverse).astype(bf16)
        out = turned.T
        g_turned = g_all[flip].T.astype(f32)
        delta = jnp.sum(turned.astype(f32) * g_turned, axis=0, keepdims=True)
        acc[flip, HD : HD + 1, :] = inverse
        acc[flip, HD + 1 : HD + 2, :] = delta
        acc[flip, :HD, :] = jnp.zeros((HD, lanes), f32)
        for member in range(group):
            rows = slice(member * tok, (member + 1) * tok)
            od_refs[flip][:, member * HD : (member + 1) * HD] = out[rows, :]

    def grad_round(items):
        slopes = [
            lax.dot_general(
                v_all[key_rows(item), :],
                g_all[table[0, item]],
                CONTRACT_LAST,
                preferred_element_type=f32,
            )
            for item in items
        ]
        probs = [
            prob[score_rows(item), :].astype(f32) * acc[table[0, item], HD : HD + 1, :]
            for item in items
        ]
        weights = [value.astype(bf16) for value in probs]
        score_grads = [
            (value * (slope - acc[table[0, item], HD + 1 : HD + 2, :])).astype(bf16)
            for item, value, slope in zip(items, probs, slopes)
        ]
        for item, weight, score_grad in zip(items, weights, score_grads):
            flip, rows = table[0, item], key_rows(item)
            dv_acc[rows, :] += jnp.dot(weight, g_all[flip], preferred_element_type=f32)
            dk_acc[rows, :] += jnp.dot(score_grad, q_wide[flip, :, :HD], preferred_element_type=f32)
            acc[flip, :HD, :] += lax.dot_general(
                k_all[rows, :], score_grad, CONTRACT_FIRST, preferred_element_type=f32
            )

    sweep(grad_round)

    for flip, od_ref in enumerate(od_refs):
        turned = (acc[flip, :HD, :] * scaling).astype(bf16).T
        for member in range(group):
            rows = slice(member * tok, (member + 1) * tok)
            od_ref[:, (group + member) * HD : (group + member + 1) * HD] = turned[rows, :]
    for chunk_number, chunk in enumerate(CHUNKS):
        for core_flip in range(cores):
            dkv_ref = dkv_refs[chunk_number * cores + core_flip]
            for head_flip in range(heads):
                for place, flip in enumerate(chunk):
                    rows = rows_of(head_flip, core_flip, flip)
                    dkv_ref[head_flip, place, :, :HD] = (dk_acc[rows, :] * scaling).astype(bf16)
                    dkv_ref[head_flip, place, :, HD:] = dv_acc[rows, :].astype(bf16)


def attention(lengths, marks, qd, kv, cores, heads):
    tok, group = qd[0].shape[0], QH // KVH
    total = KVH * cores * heads * tok
    lanes = group * tok
    reach = REACH * heads * tok
    pair = sum(-(-(keys + tok) // KEY_ROWS) for keys in (reach, reach // 2))
    items = KVH // 2 * pair
    bf16, f32 = jnp.bfloat16, jnp.float32
    results = pl.pallas_call(
        functools.partial(attention_kernel, cores, heads, tok),
        out_shape=[jax.ShapeDtypeStruct(a.shape, a.dtype) for a in qd]
        + [
            jax.ShapeDtypeStruct((heads, len(chunk), tok, 2 * HD), bf16)
            for chunk in CHUNKS
            for _ in range(cores)
        ],
        in_specs=[SMEM] + [VMEM] * (1 + len(qd) + len(kv)),
        out_specs=[VMEM] * (len(qd) + cores * len(CHUNKS)),
        scratch_shapes=[
            pltpu.VMEM((total, HD), bf16),
            pltpu.VMEM((total, HD), bf16),
            pltpu.VMEM((KVH, lanes, HD + MARKS), bf16),
            pltpu.VMEM((KVH, lanes, HD), bf16),
            pltpu.VMEM((total, HD), f32),
            pltpu.VMEM((total, HD), f32),
            pltpu.VMEM((items * KEY_ROWS, lanes), f32),
            pltpu.VMEM((items * KEY_ROWS, lanes), bf16),
            pltpu.VMEM((KVH, 8, lanes), f32),
            pltpu.VMEM((KVH, HD + 16, lanes), f32),
            pltpu.SMEM((3, items + BATCH), jnp.int32),
        ],
        compiler_params=pltpu.CompilerParams(vmem_limit_bytes=42 * 1024 * 1024),
    )(lengths, marks, *qd, *kv)
    return results[: len(qd)], results[len(qd) :]


def part_shards(queries, keys, values, d_out, lengths):
    heads, ctx = lax.axis_size("head"), lax.axis_size("ctx")
    cores = ctx // KVH
    total = queries.shape[0] * heads * ctx
    together = lax.optimization_barrier

    def over_part(piece, flip):
        return flipped(piece, flip * cores, 0)

    def exchange(pieces):
        return [pieces[0]] + [over_part(piece, s + 1) for s, piece in enumerate(pieces[1:])]

    def summed(*terms):
        return sum(term.astype(jnp.float32) for term in terms).astype(jnp.bfloat16)

    kv_pieces = split_heads(keys, values, KVH)
    far_own = flipped(kv_pieces[0][None], 0, 2)
    kv_pieces = exchange(kv_pieces)
    kv_mine = jnp.stack(kv_pieces)
    far_rest = flipped(jnp.stack(kv_pieces[1:]), 0, 2)
    far = jnp.concatenate([far_own, far_rest])
    qd = exchange(split_heads(queries, d_out, KVH))
    marks = document_marks(together((lengths, far))[0], total)
    near = flipped(kv_mine, 0, 1)
    kv = []
    for piece in (kv_mine, near, far, flipped(far, 0, 1)):
        kv += [piece, flipped(piece, 1, 0)]
    od, dkv = attention(lengths, marks, qd, kv, cores, heads)

    both = (dkv[0], flipped(dkv[1], 1, 0))
    third_rest = flipped(summed(*(term[3, 1:] for term in both)), 0, 1)
    first, last, _ = together(
        (
            summed(*(term[1] for term in both)),
            summed(*(term[3, 0] for term in both)),
            third_rest,
        )
    )
    first, third_own, rest, od_moved = together(
        (
            flipped(first, 0, 1),
            flipped(last, 0, 1),
            flipped(summed(*(term[2, 1:] for term in both), third_rest), 0, 2),
            exchange(od)[1:],
        )
    )
    own, grads = together(
        (
            summed(*(term[2, 0] for term in both), third_own),
            [summed(*(term[0, s] for term in both), first[s], rest[s - 1]) for s in (1, 2, 3)],
        )
    )
    own = flipped(own, 0, 2)
    grads = [over_part(grad, s + 1) for s, grad in enumerate(grads)]
    attn_out, grad_queries = join_heads([od[0], *od_moved])
    grads = [summed(*(term[0, 0] for term in both), first[0], own), *grads]
    grad_keys, grad_values = join_heads(grads)
    return attn_out, grad_queries, grad_keys, grad_values


def solution(mesh):
    ctx_dev, head_dev = mesh.shape["ctx"], mesh.shape["head"]
    local = part_shards if ctx_dev == 2 * KVH and head_dev == 4 else shards
    rows = P(("ctx", "head"), None)
    return jax.shard_map(
        local,
        mesh=mesh,
        in_specs=(rows, rows, rows, rows, P()),
        out_specs=(rows, rows, rows, rows),
        check_vma=False,
    )
```

```python
import functools
import math

import jax
import jax.numpy as jnp
from jax import lax
from jax.experimental import pallas as pl
from jax.experimental.pallas import tpu as pltpu
from jax.sharding import PartitionSpec as P

QH = 16
KVH = 4
HD = 128
REACH = 4


NEG_FILL = -1e30


def shifted(value, axis, steps):
    count = lax.axis_size(axis)
    first, last = (max(0, -steps), min(count, count - steps))
    return lax.ppermute(value, axis, [(source, source + steps) for source in range(first, last)])


def doc_starts(lengths, first, count):
    doc_ends = jnp.cumsum(lengths)
    positions = first + jnp.arange(count, dtype=jnp.int32)
    passed = doc_ends[None, :] <= positions[:, None]
    return jnp.sum(jnp.where(passed, lengths[None, :], 0), axis=1)


def visible_pairs(query_first, key_first, start_rows, block_rows):
    query_pos = query_first + jnp.arange(block_rows, dtype=jnp.int32)
    key_pos = key_first + jnp.arange(block_rows, dtype=jnp.int32)
    mask = (key_pos[None, :] <= query_pos[:, None]) & (key_pos[None, :] >= start_rows[:, None])
    return mask[:, None, None, :]


def block_live(query_first, key_first, tile_starts, tile_first, block_rows):
    lowest = jnp.maximum(query_first, key_first)
    picked = jnp.clip(lowest - tile_first, 0, tile_starts.shape[0] - 1)
    first_start = lax.dynamic_index_in_dim(tile_starts, picked, 0, keepdims=False)
    return (lowest <= query_first + block_rows - 1) & (first_start <= key_first + block_rows - 1)


def shards(queries, keys, values, d_out, lengths):
    heads_dev = lax.axis_size("head")
    tok_dev = queries.shape[0]
    copies = max(1, heads_dev // KVH)
    kv_local = max(1, KVH // heads_dev)
    q_local = QH // heads_dev
    group_size = q_local // kv_local
    scaling = HD ** (-0.5)

    def spread(array_in):
        if copies > 1:
            return jnp.repeat(array_in.reshape(tok_dev, KVH, HD), copies, axis=1).reshape(
                tok_dev, KVH * copies * HD
            )
        return array_in

    q_tile, k_tile, v_tile = (
        lax.all_to_all(queries, "head", split_axis=1, concat_axis=0, tiled=True),
        lax.all_to_all(spread(keys), "head", split_axis=1, concat_axis=0, tiled=True),
        lax.all_to_all(spread(values), "head", split_axis=1, concat_axis=0, tiled=True),
    )
    tile_rows = q_tile.shape[0]
    block_rows = min(1024, tile_rows)
    block_count = tile_rows // block_rows
    ctx_index = lax.axis_index("ctx")
    tile_first = ctx_index * tile_rows
    tile_starts = doc_starts(lengths, tile_first, tile_rows)
    query_blocks = [
        q_tile[number * block_rows : (number + 1) * block_rows].reshape(
            block_rows, kv_local, group_size, HD
        )
        for number in range(block_count)
    ]
    start_blocks = [
        tile_starts[number * block_rows : (number + 1) * block_rows]
        for number in range(block_count)
    ]
    query_firsts = [tile_first + number * block_rows for number in range(block_count)]
    key_pair = jnp.stack([k_tile, v_tile])
    key_tiles = [key_pair]
    moving = key_pair
    for offset in range(1, REACH + 1):
        moving = shifted(moving, "ctx", 1)
        key_tiles.append(moving)

    def split_keys(tile_pair):
        key_list = [
            tile_pair[0, number * block_rows : (number + 1) * block_rows].reshape(
                block_rows, kv_local, HD
            )
            for number in range(block_count)
        ]
        value_list = [
            tile_pair[1, number * block_rows : (number + 1) * block_rows].reshape(
                block_rows, kv_local, HD
            )
            for number in range(block_count)
        ]
        return (key_list, value_list)

    states = [
        (
            jnp.full((block_rows, kv_local, group_size), NEG_FILL, jnp.float32),
            jnp.zeros((block_rows, kv_local, group_size), jnp.float32),
            jnp.zeros((block_rows, kv_local, group_size, HD), jnp.float32),
        )
        for number in range(block_count)
    ]
    for offset in range(REACH + 1):
        key_list, value_list = split_keys(key_tiles[offset])
        key_start = (ctx_index - offset) * tile_rows
        for query_number in range(block_count):
            query_block = query_blocks[query_number]
            query_first = query_firsts[query_number]
            start_rows = start_blocks[query_number]
            for key_number in range(block_count):
                key_block = key_list[key_number]
                value_block = value_list[key_number]
                key_first = key_start + key_number * block_rows

                def forward_block(
                    current,
                    query_block=query_block,
                    query_first=query_first,
                    start_rows=start_rows,
                    key_block=key_block,
                    value_block=value_block,
                    key_first=key_first,
                ):
                    max_old, sum_old, acc_old = current
                    mask = visible_pairs(query_first, key_first, start_rows, block_rows)
                    scores = (
                        jnp.einsum(
                            "qkgd,ckd->qkgc",
                            query_block,
                            key_block,
                            preferred_element_type=jnp.float32,
                        )
                        * scaling
                    )
                    scores = jnp.where(mask, scores, NEG_FILL)
                    max_new = jnp.maximum(max_old, jnp.max(scores, axis=-1))
                    prob_raw = jnp.where(mask, jnp.exp(scores - max_new[..., None]), 0.0)
                    rescale = jnp.exp(max_old - max_new)
                    sum_new = sum_old * rescale + jnp.sum(prob_raw, axis=-1)
                    acc_new = acc_old * rescale[..., None] + jnp.einsum(
                        "qkgc,ckd->qkgd",
                        prob_raw.astype(jnp.bfloat16),
                        value_block,
                        preferred_element_type=jnp.float32,
                    )
                    return (max_new, sum_new, acc_new)

                live = block_live(query_first, key_first, tile_starts, tile_first, block_rows)
                states[query_number] = lax.cond(
                    live, forward_block, lambda unchanged: unchanged, states[query_number]
                )
    out_blocks = [(state[2] / state[1][..., None]).astype(jnp.bfloat16) for state in states]
    lse_blocks = [state[0] + jnp.log(state[1]) for state in states]
    grad_tile = lax.all_to_all(d_out, "head", split_axis=1, concat_axis=0, tiled=True)
    grad_blocks = [
        grad_tile[number * block_rows : (number + 1) * block_rows].reshape(
            block_rows, kv_local, group_size, HD
        )
        for number in range(block_count)
    ]
    delta_blocks = [
        jnp.sum(
            grad_blocks[number].astype(jnp.float32) * out_blocks[number].astype(jnp.float32),
            axis=-1,
        )
        for number in range(block_count)
    ]
    query_totals = [
        jnp.zeros((block_rows, kv_local, group_size, HD), jnp.float32)
        for number in range(block_count)
    ]
    partial_grads = []
    for offset in range(REACH + 1):
        key_list, value_list = split_keys(key_tiles[offset])
        key_start = (ctx_index - offset) * tile_rows
        key_sums = [
            jnp.zeros((block_rows, kv_local, HD), jnp.float32) for number in range(block_count)
        ]
        value_sums = [
            jnp.zeros((block_rows, kv_local, HD), jnp.float32) for number in range(block_count)
        ]
        for query_number in range(block_count):
            query_block = query_blocks[query_number]
            grad_block = grad_blocks[query_number]
            query_first = query_firsts[query_number]
            start_rows = start_blocks[query_number]
            lse_rows = lse_blocks[query_number]
            delta_rows = delta_blocks[query_number]
            for key_number in range(block_count):
                key_block = key_list[key_number]
                value_block = value_list[key_number]
                key_first = key_start + key_number * block_rows

                def backward_block(
                    current,
                    query_block=query_block,
                    grad_block=grad_block,
                    query_first=query_first,
                    start_rows=start_rows,
                    lse_rows=lse_rows,
                    delta_rows=delta_rows,
                    key_block=key_block,
                    value_block=value_block,
                    key_first=key_first,
                ):
                    query_grad, key_grad, value_grad = current
                    mask = visible_pairs(query_first, key_first, start_rows, block_rows)
                    scores = (
                        jnp.einsum(
                            "qkgd,ckd->qkgc",
                            query_block,
                            key_block,
                            preferred_element_type=jnp.float32,
                        )
                        * scaling
                    )
                    prob_raw = jnp.where(mask, jnp.exp(scores - lse_rows[..., None]), 0.0)
                    weights = prob_raw.astype(jnp.bfloat16)
                    value_grad = value_grad + jnp.einsum(
                        "qkgc,qkgd->ckd", weights, grad_block, preferred_element_type=jnp.float32
                    )
                    prob_grad = jnp.einsum(
                        "qkgd,ckd->qkgc",
                        grad_block,
                        value_block,
                        preferred_element_type=jnp.float32,
                    )
                    score_grad = (prob_raw * (prob_grad - delta_rows[..., None]) * scaling).astype(
                        jnp.bfloat16
                    )
                    query_grad = query_grad + jnp.einsum(
                        "qkgc,ckd->qkgd", score_grad, key_block, preferred_element_type=jnp.float32
                    )
                    key_grad = key_grad + jnp.einsum(
                        "qkgc,qkgd->ckd",
                        score_grad,
                        query_block,
                        preferred_element_type=jnp.float32,
                    )
                    return (query_grad, key_grad, value_grad)

                live = block_live(query_first, key_first, tile_starts, tile_first, block_rows)
                current = (query_totals[query_number], key_sums[key_number], value_sums[key_number])
                query_totals[query_number], key_sums[key_number], value_sums[key_number] = lax.cond(
                    live, backward_block, lambda unchanged: unchanged, current
                )
        key_whole = jnp.concatenate(key_sums, axis=0).reshape(tile_rows, kv_local * HD)
        value_whole = jnp.concatenate(value_sums, axis=0).reshape(tile_rows, kv_local * HD)
        partial_grads.append(jnp.stack([key_whole, value_whole]))
    grad_total = partial_grads[REACH]
    for offset in range(REACH - 1, -1, -1):
        grad_total = (
            shifted(grad_total.astype(jnp.bfloat16), "ctx", -1).astype(grad_total.dtype)
            + partial_grads[offset]
        )
    out_tile = jnp.concatenate(out_blocks, axis=0).reshape(tile_rows, q_local * HD)
    query_tile = (
        jnp.concatenate(query_totals, axis=0).reshape(tile_rows, q_local * HD).astype(jnp.bfloat16)
    )
    attn_out, grad_queries = (
        lax.all_to_all(out_tile, "head", split_axis=0, concat_axis=1, tiled=True),
        lax.all_to_all(query_tile, "head", split_axis=0, concat_axis=1, tiled=True),
    )
    token_grads = lax.all_to_all(
        grad_total.astype(jnp.bfloat16), "head", split_axis=1, concat_axis=2, tiled=True
    ).astype(grad_total.dtype)
    if copies > 1:
        token_grads = jnp.sum(token_grads.reshape(2, tok_dev, KVH, copies, HD), axis=3).reshape(
            2, tok_dev, KVH * HD
        )
    token_grads = token_grads.astype(jnp.bfloat16)
    return (attn_out, grad_queries, token_grads[0], token_grads[1])


CHUNKS = ((0, 1, 2, 3),)
CONTRACT_LAST = (((1,), (1,)), ((), ()))
CONTRACT_FIRST = (((0,), (0,)), ((), ()))
VMEM = pl.BlockSpec(memory_space=pltpu.VMEM)
SMEM = pl.BlockSpec(memory_space=pltpu.SMEM)
SMALL = pltpu.CompilerParams(vmem_limit_bytes=8 * 1024 * 1024)


def flipped(value, ctx_bits, head_bits):
    ctx, heads = lax.axis_size("ctx"), lax.axis_size("head")
    pairs = [
        (c * heads + h, (c ^ ctx_bits) * heads + (h ^ head_bits))
        for c in range(ctx)
        for h in range(heads)
    ]
    return lax.ppermute(value, ("ctx", "head"), pairs)


def piece_columns(pieces, flip, wide, offset=0):
    index = lax.axis_index("ctx") // (lax.axis_size("ctx") // pieces)
    return pl.ds(pl.multiple_of(((index ^ flip) + offset) * wide, HD), wide)


def split_heads_kernel(pieces, wide, both_ref, *piece_refs):
    for flip, piece_ref in enumerate(piece_refs):
        for side in range(2):
            columns = piece_columns(pieces, flip, wide, side * pieces)
            piece_ref[:, side * wide : (side + 1) * wide] = both_ref[:, columns]


def join_heads_kernel(pieces, wide, *refs):
    piece_refs, (left_ref, right_ref) = refs[:pieces], refs[pieces:]
    for flip, piece_ref in enumerate(piece_refs):
        columns = piece_columns(pieces, flip, wide)
        left_ref[:, columns] = piece_ref[:, :wide]
        right_ref[:, columns] = piece_ref[:, wide:]


def split_heads(left, right, pieces):
    rows, wide = left.shape[0], left.shape[1] // pieces
    return pl.pallas_call(
        functools.partial(split_heads_kernel, pieces, wide),
        out_shape=[jax.ShapeDtypeStruct((rows, 2 * wide), left.dtype)] * pieces,
        in_specs=[VMEM],
        out_specs=[VMEM] * pieces,
        compiler_params=SMALL,
    )(jnp.concatenate([left, right], axis=1))


def join_heads(parts):
    pieces = len(parts)
    rows, wide = parts[0].shape[0], parts[0].shape[1] // 2
    return pl.pallas_call(
        functools.partial(join_heads_kernel, pieces, wide),
        out_shape=[jax.ShapeDtypeStruct((rows, wide * pieces), parts[0].dtype)] * 2,
        in_specs=[VMEM] * pieces,
        out_specs=[VMEM] * 2,
        compiler_params=SMALL,
    )(*parts)


def prepare_kernel(pieces, wide, lengths_ref, both_ref, *out_refs):
    piece_refs, marks_ref = out_refs[:pieces], out_refs[pieces]
    split_heads_kernel(pieces, wide, both_ref, *piece_refs)
    total, docs = marks_ref.shape[0], lengths_ref.shape[0]
    lane = lax.broadcasted_iota(jnp.int32, (1, MARKS), 1)
    ends = jnp.zeros((1, MARKS), jnp.int32)
    end = jnp.int32(0)
    for number in range(docs):
        end = end + lengths_ref[number]
        ends = jnp.where(lane == number, end, ends)

    def some_rows(step, _):
        rows = pl.ds(pl.multiple_of(step * 4 * KEY_ROWS, KEY_ROWS), 4 * KEY_ROWS)
        position = lax.broadcasted_iota(jnp.int32, (4 * KEY_ROWS, MARKS), 0)
        marks_ref[rows, :] = jnp.where(position < ends - step * 4 * KEY_ROWS, 1.0, 0.0).astype(jnp.bfloat16)
        return 0

    lax.fori_loop(0, total // (4 * KEY_ROWS), some_rows, 0)


def prepare(lengths, left, right, pieces, total):
    rows, wide = left.shape[0], left.shape[1] // pieces
    results = pl.pallas_call(
        functools.partial(prepare_kernel, pieces, wide),
        out_shape=[jax.ShapeDtypeStruct((rows, 2 * wide), left.dtype)] * pieces
        + [jax.ShapeDtypeStruct((total, MARKS), jnp.bfloat16)],
        in_specs=[SMEM, VMEM],
        out_specs=[VMEM] * (pieces + 1),
        compiler_params=SMALL,
    )(lengths, jnp.concatenate([left, right], axis=1))
    return results[:pieces], results[pieces]


KEY_ROWS = 256
BATCH = 6
MARKS = 128
HIDDEN = -(2.0**100)


def attention_kernel(cores, heads, tok, *refs):
    group = QH // KVH
    lanes = group * tok
    tile_rows = heads * tok
    kv_count = heads * cores * len(CHUNKS)
    lengths_ref, marks_ref, refs = refs[0], refs[1], refs[2:]
    docs = lengths_ref.shape[0]
    qd_refs, refs = refs[:KVH], refs[KVH:]
    kv_refs, refs = refs[:kv_count], refs[kv_count:]
    od_refs, refs = refs[:KVH], refs[KVH:]
    dkv_refs, refs = refs[: cores * len(CHUNKS)], refs[cores * len(CHUNKS) :]
    k_all, v_all, q_wide, g_all, dk_acc, dv_acc, score, prob, tops, acc, table = refs
    scaling = HD ** (-0.5)
    log_scale = scaling * math.log2(math.e)
    f32, bf16 = jnp.float32, jnp.bfloat16

    ctx_index, head_index = lax.axis_index("ctx"), lax.axis_index("head")
    part, core = ctx_index // cores, ctx_index % cores

    def rows_of(head_flip, core_flip, part_flip):
        tile = (part ^ part_flip) * cores + (core ^ core_flip)
        return pl.ds(pl.multiple_of((tile * heads + (head_index ^ head_flip)) * tok, tok), tok)

    for chunk_number, chunk in enumerate(CHUNKS):
        for number in range(heads * cores):
            kv_ref = kv_refs[chunk_number * heads * cores + number]
            for place, flip in enumerate(chunk):
                rows = rows_of(number // cores, number % cores, flip)
                k_all[rows, :] = kv_ref[place, :, :HD]
                v_all[rows, :] = kv_ref[place, :, HD:]
    feature = lax.broadcasted_iota(jnp.int32, (tok, MARKS), 1)
    for flip, qd_ref in enumerate(qd_refs):
        own_marks = marks_ref[rows_of(0, 0, flip), :].astype(f32)
        bias = jnp.where(feature < docs, (1.0 - own_marks) * HIDDEN, 0.0).astype(bf16)
        for member in range(group):
            rows = slice(member * tok, (member + 1) * tok)
            q_wide[flip, rows, :HD] = qd_ref[:, member * HD : (member + 1) * HD]
            q_wide[flip, rows, HD:] = bias
            g_all[flip, rows, :] = qd_ref[:, (group + member) * HD : (group + member + 1) * HD]
    dk_acc[...] = jnp.zeros_like(dk_acc)
    dv_acc[...] = jnp.zeros_like(dv_acc)
    tops[...] = jnp.full_like(tops, NEG_FILL)
    acc[...] = jnp.zeros_like(acc)

    def entry(number, flip, row, limit):
        table[0, number] = flip
        table[1, number] = row
        table[2, number] = limit

    total = jnp.int32(0)
    for flip in range(KVH):
        first = ((part ^ flip) * cores + core) * tile_rows + head_index * tok
        end, low = jnp.int32(0), jnp.int32(0)
        for number in range(docs):
            length = lengths_ref[number]
            end = end + length
            low = low + jnp.where(end <= first, length, 0)
        count = (first + tok - low // tok * tok + KEY_ROWS - 1) // KEY_ROWS
        begin = jnp.maximum(first + tok - count * KEY_ROWS, 0)

        def listed(step, _, flip=flip, first=first, begin=begin, total=total):
            row = begin + step * KEY_ROWS
            entry(total + step, flip, row, first - row)
            return 0

        lax.fori_loop(0, count, listed, 0)
        total = total + count
    for spare in range(BATCH - 1):
        entry(total + spare, 0, 0, -(1 << 20))
    rounds = (total + 1) // BATCH
    left_over = (total - rounds * BATCH + 1) // 2

    def sweep(body):
        def one_round(number, _):
            body([number * BATCH + place for place in range(BATCH)])
            return 0

        def one_pair(number, _):
            body([rounds * BATCH + number * 2 + place for place in range(2)])
            return 0

        lax.fori_loop(0, rounds, one_round, 0)
        lax.fori_loop(0, left_over, one_pair, 0)

    def key_rows(item):
        return pl.ds(pl.multiple_of(table[1, item], tok), KEY_ROWS)

    def score_rows(item):
        return pl.ds(pl.multiple_of(item * KEY_ROWS, KEY_ROWS), KEY_ROWS)

    def wide(ref, rows):
        return jnp.concatenate([ref[rows, :], marks_ref[rows, :]], axis=1)

    key_row = lax.broadcasted_iota(jnp.int32, (KEY_ROWS, lanes), 0)
    query_row = lax.broadcasted_iota(jnp.int32, (1, lanes), 1) % tok

    def scores_round(items):
        raws = [
            lax.dot_general(
                wide(k_all, key_rows(item)),
                q_wide[table[0, item]],
                CONTRACT_LAST,
                preferred_element_type=f32,
            )
            for item in items
        ]
        for item, raw in zip(items, raws):
            raw = jnp.where(key_row <= query_row + table[2, item], raw, NEG_FILL)
            score[score_rows(item), :] = raw
            flip = table[0, item]
            tops[flip] = jnp.maximum(
                tops[flip], jnp.max(raw.reshape(KEY_ROWS // 8, 8, lanes), axis=0)
            )

    sweep(scores_round)
    for flip in range(KVH):
        tops[flip] = jnp.broadcast_to(jnp.max(tops[flip], axis=0, keepdims=True), (8, lanes))

    ones = jnp.ones((acc.shape[1] - HD, KEY_ROWS), bf16)

    def out_round(items):
        weights = [
            jnp.exp2((score[score_rows(item), :] - tops[table[0, item], :1]) * log_scale).astype(bf16)
            for item in items
        ]
        for item, weight in zip(items, weights):
            prob[score_rows(item), :] = weight
        parts = [
            jnp.dot(
                jnp.concatenate([v_all[key_rows(item), :].T, ones], axis=0),
                weight,
                preferred_element_type=f32,
            )
            for item, weight in zip(items, weights)
        ]
        for item, value in zip(items, parts):
            acc[table[0, item]] += value

    sweep(out_round)
    for flip in range(KVH):
        inverse = 1.0 / acc[flip, HD : HD + 1, :]
        turned = (acc[flip, :HD, :] * inverse).astype(bf16)
        out = turned.T
        g_turned = g_all[flip].T.astype(f32)
        delta = jnp.sum(turned.astype(f32) * g_turned, axis=0, keepdims=True)
        acc[flip, HD : HD + 1, :] = inverse
        acc[flip, HD + 1 : HD + 2, :] = delta
        acc[flip, :HD, :] = jnp.zeros((HD, lanes), f32)
        for member in range(group):
            rows = slice(member * tok, (member + 1) * tok)
            od_refs[flip][:, member * HD : (member + 1) * HD] = out[rows, :]

    def grad_round(items):
        slopes = [
            lax.dot_general(
                v_all[key_rows(item), :],
                g_all[table[0, item]],
                CONTRACT_LAST,
                preferred_element_type=f32,
            )
            for item in items
        ]
        probs = [
            prob[score_rows(item), :].astype(f32) * acc[table[0, item], HD : HD + 1, :]
            for item in items
        ]
        weights = [value.astype(bf16) for value in probs]
        score_grads = [
            (value * (slope - acc[table[0, item], HD + 1 : HD + 2, :])).astype(bf16)
            for item, value, slope in zip(items, probs, slopes)
        ]
        for item, weight, score_grad in zip(items, weights, score_grads):
            flip, rows = table[0, item], key_rows(item)
            dv_acc[rows, :] += jnp.dot(weight, g_all[flip], preferred_element_type=f32)
            dk_acc[rows, :] += jnp.dot(score_grad, q_wide[flip, :, :HD], preferred_element_type=f32)
            acc[flip, :HD, :] += lax.dot_general(
                k_all[rows, :], score_grad, CONTRACT_FIRST, preferred_element_type=f32
            )

    sweep(grad_round)

    for flip, od_ref in enumerate(od_refs):
        turned = (acc[flip, :HD, :] * scaling).astype(bf16).T
        for member in range(group):
            rows = slice(member * tok, (member + 1) * tok)
            od_ref[:, (group + member) * HD : (group + member + 1) * HD] = turned[rows, :]
    for chunk_number, chunk in enumerate(CHUNKS):
        for core_flip in range(cores):
            dkv_ref = dkv_refs[chunk_number * cores + core_flip]
            for head_flip in range(heads):
                for place, flip in enumerate(chunk):
                    rows = rows_of(head_flip, core_flip, flip)
                    dkv_ref[head_flip, place, :, :HD] = (dk_acc[rows, :] * scaling).astype(bf16)
                    dkv_ref[head_flip, place, :, HD:] = dv_acc[rows, :].astype(bf16)


def attention(lengths, marks, qd, kv, cores, heads):
    tok, group = qd[0].shape[0], QH // KVH
    total = KVH * cores * heads * tok
    lanes = group * tok
    reach = REACH * heads * tok
    pair = sum(-(-(keys + tok) // KEY_ROWS) for keys in (reach, reach // 2))
    items = KVH // 2 * pair
    bf16, f32 = jnp.bfloat16, jnp.float32
    results = pl.pallas_call(
        functools.partial(attention_kernel, cores, heads, tok),
        out_shape=[jax.ShapeDtypeStruct(a.shape, a.dtype) for a in qd]
        + [
            jax.ShapeDtypeStruct((heads, len(chunk), tok, 2 * HD), bf16)
            for chunk in CHUNKS
            for _ in range(cores)
        ],
        in_specs=[SMEM] + [VMEM] * (1 + len(qd) + len(kv)),
        out_specs=[VMEM] * (len(qd) + cores * len(CHUNKS)),
        scratch_shapes=[
            pltpu.VMEM((total, HD), bf16),
            pltpu.VMEM((total, HD), bf16),
            pltpu.VMEM((KVH, lanes, HD + MARKS), bf16),
            pltpu.VMEM((KVH, lanes, HD), bf16),
            pltpu.VMEM((total, HD), f32),
            pltpu.VMEM((total, HD), f32),
            pltpu.VMEM((items * KEY_ROWS, lanes), f32),
            pltpu.VMEM((items * KEY_ROWS, lanes), bf16),
            pltpu.VMEM((KVH, 8, lanes), f32),
            pltpu.VMEM((KVH, HD + 16, lanes), f32),
            pltpu.SMEM((3, items + BATCH), jnp.int32),
        ],
        compiler_params=pltpu.CompilerParams(vmem_limit_bytes=42 * 1024 * 1024),
    )(lengths, marks, *qd, *kv)
    return results[: len(qd)], results[len(qd) :]


def part_shards(queries, keys, values, d_out, lengths):
    heads, ctx = lax.axis_size("head"), lax.axis_size("ctx")
    cores = ctx // KVH
    total = queries.shape[0] * heads * ctx
    together = lax.optimization_barrier

    def over_part(piece, flip):
        return flipped(piece, flip * cores, 0)

    def exchange(pieces):
        return [pieces[0]] + [over_part(piece, s + 1) for s, piece in enumerate(pieces[1:])]

    def summed(*terms):
        return sum(term.astype(jnp.float32) for term in terms).astype(jnp.bfloat16)

    kv_pieces = split_heads(keys, values, KVH)
    far_own = flipped(kv_pieces[0][None], 0, 2)
    kv_pieces = exchange(kv_pieces)
    kv_mine = jnp.stack(kv_pieces)
    far_rest = flipped(jnp.stack(kv_pieces[1:]), 0, 2)
    far = jnp.concatenate([far_own, far_rest])
    qd, marks = prepare(lengths, queries, d_out, KVH, total)
    qd = exchange(qd)
    near = flipped(kv_mine, 0, 1)
    kv = []
    for piece in (kv_mine, near, far, flipped(far, 0, 1)):
        kv += [piece, flipped(piece, 1, 0)]
    od, dkv = attention(lengths, marks, qd, kv, cores, heads)

    both = (dkv[0], flipped(dkv[1], 1, 0))
    third_rest = flipped(summed(*(term[3, 1:] for term in both)), 0, 1)
    first, last, _ = together(
        (
            summed(*(term[1] for term in both)),
            summed(*(term[3, 0] for term in both)),
            third_rest,
        )
    )
    first, third_own, rest, od_moved = together(
        (
            flipped(first, 0, 1),
            flipped(last, 0, 1),
            flipped(summed(*(term[2, 1:] for term in both), third_rest), 0, 2),
            exchange(od)[1:],
        )
    )
    own, grads = together(
        (
            summed(*(term[2, 0] for term in both), third_own),
            [summed(*(term[0, s] for term in both), first[s], rest[s - 1]) for s in (1, 2, 3)],
        )
    )
    own = flipped(own, 0, 2)
    grads = [over_part(grad, s + 1) for s, grad in enumerate(grads)]
    attn_out, grad_queries = join_heads([od[0], *od_moved])
    grads = [summed(*(term[0, 0] for term in both), first[0], own), *grads]
    grad_keys, grad_values = join_heads(grads)
    return attn_out, grad_queries, grad_keys, grad_values


def solution(mesh):
    ctx_dev, head_dev = mesh.shape["ctx"], mesh.shape["head"]
    local = part_shards if ctx_dev == 2 * KVH and head_dev == 4 else shards
    rows = P(("ctx", "head"), None)
    return jax.shard_map(
        local,
        mesh=mesh,
        in_specs=(rows, rows, rows, rows, P()),
        out_specs=(rows, rows, rows, rows),
        check_vma=False,
    )
```
